32 devices in a mesh: dp: 8 (over y, x, core), tensor: 4 (over z).
Axes of the slice: x: 2, y: 2, z: 4, core: 2. Of those that a mesh axis runs over, the one named last changes fastest.
Arguments:
- block_input: bfloat16 [24, 1376, 1024], P('dp', 'tensor'), may hold values from -6 to 6
- cotangent: bfloat16 [24, 1376, 1024], P('dp', 'tensor'), may hold values from -6 to 6
- lengths: int32 [24], P('dp'), may hold values from 685 to 1370, as said below
- w_qkv: bfloat16 [3, 1024, 1024], P(None, 'dp', 'tensor'), may hold values from -0.1875 to 0.1875
- b_qv: bfloat16 [2, 64, 16], P(None, 'dp', 'tensor'), may hold values from -2 to 2
- w_out: bfloat16 [1024, 1024], P('tensor', 'dp'), may hold values from -0.1875 to 0.1875
- w_fc1: bfloat16 [1024, 4096], P('dp', 'tensor'), may hold values from -0.1875 to 0.1875
- b_fc1: bfloat16 [64, 64], P('dp', 'tensor'), may hold values from -3 to 3
- w_fc2: bfloat16 [4096, 1024], P('tensor', 'dp'), may hold values from -0.09375 to 0.09375
- ln_gain: float32 [2, 1024], P(None, ('dp', 'tensor')), may hold values from 0.25 to 1.75
- ln_shift: float32 [2, 1024], P(None, ('dp', 'tensor')), may hold values from -2 to 2
- layer_scale: float32 [2, 1024], P(None, ('dp', 'tensor')), may hold values from 0.5 to 2
- out_bias: float32 [2, 1024], P(None, ('dp', 'tensor')), may hold values from -2 to 2
Outputs:
- block_out: bfloat16 [24, 1376, 1024], P('dp', 'tensor')
- grad_input: float32 [24, 1376, 1024], P('dp', 'tensor')
- grad_w_qkv: float32 [3, 1024, 1024], P(None, 'dp', 'tensor')
- grad_b_qv: float32 [2, 64, 16], P(None, 'dp', 'tensor')
- grad_w_out: float32 [1024, 1024], P('tensor', 'dp')
- grad_w_fc1: float32 [1024, 4096], P('dp', 'tensor')
- grad_b_fc1: float32 [64, 64], P('dp', 'tensor')
- grad_w_fc2: float32 [4096, 1024], P('tensor', 'dp')
- grad_ln_gain: float32 [2, 1024], P(None, ('dp', 'tensor'))
- grad_ln_shift: float32 [2, 1024], P(None, ('dp', 'tensor'))
- grad_layer_scale: float32 [2, 1024], P(None, ('dp', 'tensor'))
- grad_out_bias: float32 [2, 1024], P(None, ('dp', 'tensor'))
The draws below stay inside these ranges and needn't reach their ends.
Inputs may be any that keep to these rules, and one draw needn't show every extreme that they name: `lengths`: image 0 has exactly 1370 valid tokens.
All inputs are finite; a program needn't handle non-finite values.
Results may differ from the reference program's by a relative error of at most 0.011.
Values may be sent and summed in bfloat16 or wider, within the bound.
A program may use at most 320 MiB of HBM per device.

```python
import math
import jax
import jax.numpy as jnp
from jax import lax

D = 1024
HEADS = 16
HD = 64
FF = 4096
SEQ_REAL = 1370
SEQ = 1376
IMAGES = 24


def draw_lengths(key, part):
    key = jax.random.fold_in(key, 3)
    drawn = jax.random.randint(key, (IMAGES,), SEQ_REAL // 2, SEQ_REAL + 1)
    leading = jnp.arange(IMAGES) == 0
    return jnp.where(leading, SEQ_REAL, drawn).astype(jnp.int32)


def level_of(own_key, shape, shards, smallest, high):
    factor_of = 1.0
    for axis_at, blocks in shards:
        steps = jax.random.uniform(jax.random.fold_in(jax.random.fold_in(own_key, 6), axis_at), (blocks,), jnp.float32, smallest / len(shards), high / len(shards))
        factor_of = factor_of * jnp.repeat(jnp.exp(steps), shape[axis_at] // blocks).reshape((-1,) + (1,) * (len(shape) - 1 - axis_at))
    return factor_of


def noise(stream_key, dims, width, reach, pieces=(), kind=jnp.bfloat16):
    level = level_of(stream_key, dims, pieces, -0.22, 0.18) if pieces else 1.0
    values = jax.random.normal(stream_key, dims, jnp.float32) * width * level
    return jnp.minimum(jnp.maximum(values, -reach), reach).astype(kind)


def setup_inputs(seed: int = 0) -> dict:
    key_of = jax.random.split(jax.random.key(seed), 14)
    block_input = noise(key_of[0], (IMAGES, SEQ, D), 1.0, 6.0, ((0, 8), (1, 4)))
    cotangent = noise(key_of[1], (IMAGES, SEQ, D), 1.0, 6.0, ((0, 8), (1, 4)))
    lengths = draw_lengths(jax.random.fold_in(key_of[13], 71), 0)
    w_qkv = noise(key_of[3], (3, D, D), D ** -0.5, 0.1875, ((1, 8), (2, 4)))
    b_qv = noise(key_of[4], (2, HD, HEADS), 0.5, 2.0, ((1, 8), (2, 4)))
    w_out = noise(key_of[5], (D, D), D ** -0.5, 0.1875, ((0, 4), (1, 8)))
    w_fc1 = noise(key_of[6], (D, FF), D ** -0.5, 0.1875, ((0, 8), (1, 4)))
    b_fc1 = noise(key_of[7], (HD, FF // HD), 0.5, 3.0, ((0, 8), (1, 4)))
    w_fc2 = noise(key_of[8], (FF, D), FF ** -0.5, 0.09375, ((0, 4), (1, 8)))
    ln_gain = jnp.clip(1.0 + 0.15 * jax.random.normal(key_of[9], (2, D), jnp.float32), 0.25, 1.75)
    ln_shift = noise(key_of[10], (2, D), 0.3, 2.0, ((1, 32),), jnp.float32)
    layer_scale = jnp.clip(jnp.exp(math.log(2.0) - 1.3862944 * jax.random.uniform(key_of[11], (2, D), jnp.float32) ** level_of(key_of[11], (2, D), ((1, 32),), -0.2, 0.2)), 0.5, 2.0)
    out_bias = noise(key_of[12], (2, D), 0.3, 2.0, ((1, 32),), jnp.float32)
    return {"block_input": block_input, "cotangent": cotangent, "lengths": lengths, "w_qkv": w_qkv, "b_qv": b_qv, "w_out": w_out, "w_fc1": w_fc1, "b_fc1": b_fc1, "w_fc2": w_fc2, "ln_gain": ln_gain, "ln_shift": ln_shift, "layer_scale": layer_scale, "out_bias": out_bias}


def norm_rows(values, gain, shift):
    center = values - lax.optimization_barrier(jnp.mean(values, axis=-1, keepdims=True))
    inverse = lax.rsqrt(lax.optimization_barrier(jnp.mean(center * center, axis=-1, keepdims=True)) + 1e-06)
    normed = center * inverse
    return (normed * gain + shift, normed, inverse)

def norm_back(grad_norm, normed, inverse, gain):
    scaled = grad_norm * gain
    return inverse * (scaled - lax.optimization_barrier(jnp.mean(scaled, axis=-1, keepdims=True)) - normed * lax.optimization_barrier(jnp.mean(scaled * normed, axis=-1, keepdims=True)))

def gelu_back(pre_act, grad_act):
    return jax.vjp(lambda argument: jax.nn.gelu(argument, approximate=False), pre_act)[1](grad_act)[0]

def reference(block_input, cotangent, lengths, w_qkv, b_qv, w_out, w_fc1, b_fc1, w_fc2, ln_gain, ln_shift, layer_scale, out_bias):
    qv_bias = jnp.transpose(b_qv.astype(jnp.float32), (0, 2, 1)).reshape(2, D)
    fc1_bias = b_fc1.astype(jnp.float32).T.reshape(FF)
    factor = HD ** (-0.5)

    def one_image(carry, sample):
        source_rows, cot_rows, length = sample
        valid_rows = jnp.arange(SEQ, dtype=jnp.int32) < length
        row_mask = valid_rows.astype(jnp.float32)[:, None]
        source = source_rows.astype(jnp.float32)
        normed_one, hat_first, inv_first = norm_rows(source, ln_gain[0], ln_shift[0])
        normed1 = normed_one.astype(jnp.bfloat16)
        query = (jnp.dot(normed1, w_qkv[0], preferred_element_type=jnp.float32) + qv_bias[0]).astype(jnp.bfloat16)
        key_rows = jnp.dot(normed1, w_qkv[1], preferred_element_type=jnp.float32).astype(jnp.bfloat16)
        value = (jnp.dot(normed1, w_qkv[2], preferred_element_type=jnp.float32) + qv_bias[1]).astype(jnp.bfloat16)
        query_h = query.reshape(SEQ, HEADS, HD).astype(jnp.float32)
        key_h = key_rows.reshape(SEQ, HEADS, HD).astype(jnp.float32)
        value_h = value.reshape(SEQ, HEADS, HD).astype(jnp.float32)
        scores = jnp.einsum('qhe,khe->hqk', query_h, key_h) * factor
        scores = jnp.where(valid_rows[None, None, :], scores, -1e+30)
        row_max = lax.optimization_barrier(jnp.max(scores, axis=-1, keepdims=True))
        log_total = row_max + jnp.log(lax.optimization_barrier(jnp.sum(jnp.exp(scores - row_max), axis=-1, keepdims=True)))
        probs_f = jnp.exp(scores - log_total)
        probs = probs_f.astype(jnp.bfloat16)
        context = jnp.einsum('hqk,khe->qhe', probs.astype(jnp.float32), value_h).astype(jnp.bfloat16)
        context_flat = context.reshape(SEQ, D)
        attn = jnp.dot(context_flat, w_out, preferred_element_type=jnp.float32) + out_bias[0]
        hidden = source + layer_scale[0] * attn
        normed_two, hat_second, inv_second = norm_rows(hidden, ln_gain[1], ln_shift[1])
        normed2 = normed_two.astype(jnp.bfloat16)
        pre_act = jnp.dot(normed2, w_fc1, preferred_element_type=jnp.float32) + fc1_bias
        activation = jax.nn.gelu(pre_act, approximate=False).astype(jnp.bfloat16)
        mlp = jnp.dot(activation, w_fc2, preferred_element_type=jnp.float32) + out_bias[1]
        output = (row_mask * (hidden + layer_scale[1] * mlp)).astype(jnp.bfloat16)
        grad_out = row_mask * cot_rows.astype(jnp.float32)
        grad_scale2 = lax.optimization_barrier(jnp.sum(grad_out * mlp, axis=0))
        grad_mlp = grad_out * layer_scale[1]
        grad_bias2 = lax.optimization_barrier(jnp.sum(grad_mlp, axis=0))
        grad_mlp_b = grad_mlp.astype(jnp.bfloat16)
        grad_fc2 = jnp.dot(activation.T, grad_mlp_b, preferred_element_type=jnp.float32)
        grad_act = jnp.dot(grad_mlp_b, w_fc2.T, preferred_element_type=jnp.float32)
        grad_pre = gelu_back(pre_act, grad_act)
        grad_fc1_bias = lax.optimization_barrier(jnp.sum(grad_pre, axis=0))
        grad_pre_b = grad_pre.astype(jnp.bfloat16)
        grad_fc1 = jnp.dot(normed2.T, grad_pre_b, preferred_element_type=jnp.float32)
        grad_normed2 = jnp.dot(grad_pre_b, w_fc1.T, preferred_element_type=jnp.float32)
        grad_gain2 = lax.optimization_barrier(jnp.sum(grad_normed2 * hat_second, axis=0))
        grad_shift2 = lax.optimization_barrier(jnp.sum(grad_normed2, axis=0))
        grad_hidden = grad_out + norm_back(grad_normed2, hat_second, inv_second, ln_gain[1])
        grad_scale1 = lax.optimization_barrier(jnp.sum(grad_hidden * attn, axis=0))
        grad_attn = grad_hidden * layer_scale[0]
        grad_bias1 = lax.optimization_barrier(jnp.sum(grad_attn, axis=0))
        grad_attn_b = grad_attn.astype(jnp.bfloat16)
        grad_wout = jnp.dot(context_flat.T, grad_attn_b, preferred_element_type=jnp.float32)
        grad_context = jnp.dot(grad_attn_b, w_out.T, preferred_element_type=jnp.float32).astype(jnp.bfloat16)
        grad_context_h = grad_context.reshape(SEQ, HEADS, HD).astype(jnp.float32)
        grad_value = jnp.einsum('hqk,qhe->khe', probs.astype(jnp.float32), grad_context_h)
        grad_probs = jnp.einsum('qhe,khe->hqk', grad_context_h, value_h)
        correction = lax.optimization_barrier(jnp.sum(grad_context_h * context.astype(jnp.float32), axis=-1))
        grad_scores = (probs_f * (grad_probs - correction.T[:, :, None]) * factor).astype(jnp.bfloat16).astype(jnp.float32)
        grad_query = jnp.einsum('hqk,khe->qhe', grad_scores, key_h).reshape(SEQ, D)
        grad_key = jnp.einsum('hqk,qhe->khe', grad_scores, query_h).reshape(SEQ, D)
        grad_value = grad_value.reshape(SEQ, D)
        grad_qv = jnp.stack([lax.optimization_barrier(jnp.sum(grad_query, axis=0)), lax.optimization_barrier(jnp.sum(grad_value, axis=0))])
        grad_q_b = grad_query.astype(jnp.bfloat16)
        grad_k_b = grad_key.astype(jnp.bfloat16)
        grad_v_b = grad_value.astype(jnp.bfloat16)
        grad_wqkv = jnp.stack([jnp.dot(normed1.T, grad_q_b, preferred_element_type=jnp.float32), jnp.dot(normed1.T, grad_k_b, preferred_element_type=jnp.float32), jnp.dot(normed1.T, grad_v_b, preferred_element_type=jnp.float32)])
        grad_normed1 = jnp.dot(grad_q_b, w_qkv[0].T, preferred_element_type=jnp.float32) + jnp.dot(grad_k_b, w_qkv[1].T, preferred_element_type=jnp.float32) + jnp.dot(grad_v_b, w_qkv[2].T, preferred_element_type=jnp.float32)
        grad_gain1 = lax.optimization_barrier(jnp.sum(grad_normed1 * hat_first, axis=0))
        grad_shift1 = lax.optimization_barrier(jnp.sum(grad_normed1, axis=0))
        grad_source = grad_hidden + norm_back(grad_normed1, hat_first, inv_first, ln_gain[0])
        terms = (grad_wqkv, grad_qv, grad_wout, grad_fc1, grad_fc1_bias, grad_fc2, jnp.stack([grad_gain1, grad_gain2]), jnp.stack([grad_shift1, grad_shift2]), jnp.stack([grad_scale1, grad_scale2]), jnp.stack([grad_bias1, grad_bias2]))
        carry = tuple((total + term for total, term in zip(carry, terms)))
        return (carry, (output, grad_source))
    start = (jnp.zeros((3, D, D), jnp.float32), jnp.zeros((2, D), jnp.float32), jnp.zeros((D, D), jnp.float32), jnp.zeros((D, FF), jnp.float32), jnp.zeros((FF,), jnp.float32), jnp.zeros((FF, D), jnp.float32), jnp.zeros((2, D), jnp.float32), jnp.zeros((2, D), jnp.float32), jnp.zeros((2, D), jnp.float32), jnp.zeros((2, D), jnp.float32))
    totals, (outputs, grad_sources) = lax.scan(one_image, start, (block_input, cotangent, lengths))
    grad_wqkv, grad_qv, grad_wout, grad_fc1, grad_fc1_bias, grad_fc2, grad_gain, grad_shift, grad_scale, grad_bias = totals
    grad_bqv = jnp.transpose(grad_qv.reshape(2, HEADS, HD), (0, 2, 1))
    grad_bfc1 = grad_fc1_bias.reshape(FF // HD, HD).T
    return (outputs, grad_sources, grad_wqkv, grad_bqv, grad_wout, grad_fc1, grad_bfc1, grad_fc2, grad_gain, grad_shift, grad_scale, grad_bias)
```

```python
import functools
import math

import jax
import jax.numpy as jnp
from jax import lax
from jax.experimental import pallas as pl
from jax.experimental.pallas import tpu as pltpu
from jax.sharding import PartitionSpec as P

HD = 64
LANES = 128
LOG2E = math.log2(math.e)
NEG = -1e30
NT = (((1,), (1,)), ((), ()))
NN = (((1,), (0,)), ((), ()))
f32 = jnp.float32
bf16 = jnp.bfloat16


def round_up(n, m):
    return (n + m - 1) // m * m


def parts(x):
    hi = x.astype(bf16).astype(f32)
    rest = x - hi
    mid = rest.astype(bf16).astype(f32)
    return hi, mid, rest - mid


def keys_with_bias(keys, lane, row, length, own, spare):
    bias = jnp.where(row < length, 0.0, NEG)
    ones = jnp.where((lane >= spare) & (lane < spare + 3), 1.0, 0.0)
    return jnp.where(own, keys, jnp.where(lane == spare + 3, bias, ones)).astype(bf16)


def attend_forward_kernel(rows, padded, len_ref, q_ref, k_ref, v_ref, ctx_ref, qa_ref, ka, va):
    length = len_ref[0]
    lane = lax.broadcasted_iota(jnp.int32, (padded, LANES), 1)
    row = lax.broadcasted_iota(jnp.int32, (padded, LANES), 0)
    lb = lane[:rows]
    if padded > rows:
        va[rows:] = jnp.zeros((padded - rows, LANES), bf16)
    for half in range(2):
        own = (lb < HD) if half == 0 else (lb >= HD)
        spare = HD if half == 0 else 0
        ka[:rows] = keys_with_bias(k_ref[...].astype(f32), lb, row[:rows], length, own, spare)
        if padded > rows:
            ka[rows:] = jnp.where(lane[rows:] == spare + 3, NEG, 0.0).astype(bf16)
        va[:rows] = jnp.where(
            own, v_ref[...].astype(f32), jnp.where(lb == spare, 1.0, 0.0)
        ).astype(bf16)
        qa = jnp.where(own, q_ref[...].astype(f32), jnp.where(lb == spare + 3, 1.0, 0.0))
        s = lax.dot_general(qa.astype(bf16), ka[...], NT, preferred_element_type=f32)
        m = jnp.max(s, axis=1, keepdims=True)
        p = jnp.exp2(s - m).astype(bf16)
        o = lax.dot_general(p, va[...], NN, preferred_element_type=f32)
        total = o[:, spare : spare + 1]
        o = o / total
        hi, mid, lo = parts(-(m + jnp.log2(total)))
        if half == 0:
            ctx_ref[...] = o.astype(bf16)
        else:
            ctx_ref[...] = jnp.where(own, o, ctx_ref[...].astype(f32)).astype(bf16)
        stats = jnp.where(lb == spare + 2, lo, qa)
        stats = jnp.where(lb == spare + 1, mid, stats)
        qa_ref[half] = jnp.where(lb == spare, hi, stats).astype(bf16)


def attend_forward(length, q, k, v):
    rows, width = q.shape
    padded = round_up(rows, LANES)
    spec = pl.BlockSpec((rows, LANES), lambda j: (0, j))
    return pl.pallas_call(
        functools.partial(attend_forward_kernel, rows, padded),
        grid=(width // LANES,),
        in_specs=[pl.BlockSpec(memory_space=pltpu.SMEM), spec, spec, spec],
        out_specs=[spec, pl.BlockSpec((2, rows, LANES), lambda j: (j, 0, 0))],
        out_shape=[
            jax.ShapeDtypeStruct((rows, width), bf16),
            jax.ShapeDtypeStruct((width // HD, rows, LANES), bf16),
        ],
        scratch_shapes=[pltpu.VMEM((padded, LANES), bf16), pltpu.VMEM((padded, LANES), bf16)],
        compiler_params=pltpu.CompilerParams(vmem_limit_bytes=56 * 2**20),
        cost_estimate=pl.CostEstimate(
            flops=16 * rows * rows * width,
            bytes_accessed=12 * rows * width,
            transcendentals=rows * rows * width // HD,
        ),
        name="attend_forward",
    )(length, q, k, v)


def attend_backward_kernel(
    rows,
    padded,
    blocks,
    len_ref,
    qa_ref,
    k_ref,
    v_ref,
    gc_ref,
    ctx_ref,
    gq_ref,
    gk_ref,
    gv_ref,
    ka,
    va,
    qs,
    ga,
    acc,
):
    length = len_ref[0]
    lane = lax.broadcasted_iota(jnp.int32, (padded, LANES), 1)
    row = lax.broadcasted_iota(jnp.int32, (padded, LANES), 0)
    size = rows // blocks
    ls = lane[:rows]
    for half in range(2):
        own = (ls < HD) if half == 0 else (ls >= HD)
        spare = HD if half == 0 else 0
        ownb = own[:size]
        gc = gc_ref[...].astype(f32)
        corr = jnp.sum(
            jnp.where(own, gc * ctx_ref[...].astype(f32), 0.0), axis=1, keepdims=True
        )
        hi, mid, lo = parts(-corr)
        extra = jnp.where(ls == spare + 1, mid, jnp.where(ls == spare + 2, lo, 0.0))
        ga[:rows] = jnp.where(own, gc, jnp.where(ls == spare, hi, extra)).astype(bf16)
        qs[:rows] = qa_ref[half]
        if padded > rows:
            ga[rows:] = jnp.zeros((padded - rows, LANES), bf16)
            qs[rows:] = jnp.where(lane[rows:] == spare, NEG, 0.0).astype(bf16)
        ka[...] = keys_with_bias(k_ref[...].astype(f32), ls, row[:rows], length, own, spare)
        ones = jnp.where((ls >= spare) & (ls < spare + 3), 1.0, 0.0)
        va[...] = jnp.where(own, v_ref[...].astype(f32), ones).astype(bf16)
        acc[...] = jnp.zeros_like(acc)

        def block(b, carry):
            r = pl.ds(pl.multiple_of(b * size, 16), size)
            kb = ka[r, :]
            p = jnp.exp2(lax.dot_general(kb, qs[...], NT, preferred_element_type=f32))
            gp = lax.dot_general(va[r, :], ga[...], NT, preferred_element_type=f32)
            ds = (p * gp).astype(bf16)
            gv = lax.dot_general(p.astype(bf16), ga[...], NN, preferred_element_type=f32)
            gk = lax.dot_general(ds, qs[...], NN, preferred_element_type=f32) * (1.0 / LOG2E)
            acc[...] += lax.dot_general(kb.T, ds, NN, preferred_element_type=f32)
            if half == 0:
                gv_ref[r, :] = gv.astype(bf16)
                gk_ref[r, :] = gk.astype(bf16)
            else:
                gv_ref[r, :] = jnp.where(ownb, gv, gv_ref[r, :].astype(f32)).astype(bf16)
                gk_ref[r, :] = jnp.where(ownb, gk, gk_ref[r, :].astype(f32)).astype(bf16)
            return carry

        lax.fori_loop(0, blocks, block, 0)
        gq = acc[...].T[:rows] * HD ** (-0.5)
        if half == 0:
            gq_ref[...] = gq.astype(bf16)
        else:
            gq_ref[...] = jnp.where(own, gq, gq_ref[...].astype(f32)).astype(bf16)


def attend_backward(length, qa, k, v, gc, ctx):
    rows, width = k.shape
    padded = round_up(rows, LANES)
    blocks = 2 if rows % 32 == 0 else 1
    spec = pl.BlockSpec((rows, LANES), lambda j: (0, j))
    return pl.pallas_call(
        functools.partial(attend_backward_kernel, rows, padded, blocks),
        grid=(width // LANES,),
        in_specs=[
            pl.BlockSpec(memory_space=pltpu.SMEM),
            pl.BlockSpec((2, rows, LANES), lambda j: (j, 0, 0)),
            spec,
            spec,
            spec,
            spec,
        ],
        out_specs=[spec] * 3,
        out_shape=[jax.ShapeDtypeStruct((rows, width), bf16)] * 3,
        scratch_shapes=[
            pltpu.VMEM((rows, LANES), bf16),
            pltpu.VMEM((rows, LANES), bf16),
            pltpu.VMEM((padded, LANES), bf16),
            pltpu.VMEM((padded, LANES), bf16),
            pltpu.VMEM((LANES, padded), f32),
        ],
        compiler_params=pltpu.CompilerParams(vmem_limit_bytes=56 * 2**20),
        cost_estimate=pl.CostEstimate(
            flops=40 * rows * rows * width,
            bytes_accessed=16 * rows * width,
            transcendentals=rows * rows * width // HD,
        ),
        name="attend_backward",
    )(length, qa, k, v, gc, ctx)


def feed_forward_kernel(
    n2_ref, n2t_ref, gm_ref, gmt_ref, w1_ref, b1_ref, w2_ref, mlp_ref, gn_ref, gw1_ref, gw2_ref, gb_ref
):
    step = pl.program_id(0)
    pre = lax.dot_general(n2_ref[...], w1_ref[...], NN, preferred_element_type=f32) + b1_ref[...]
    gact = lax.dot_general(gm_ref[...], w2_ref[...], NT, preferred_element_type=f32)
    cdf = 0.5 * (1.0 + lax.erf(pre * (1 / math.sqrt(2))))
    act = (pre * cdf).astype(bf16)
    pdf = jnp.exp2(pre * pre * (-0.5 * LOG2E)) * (1 / math.sqrt(2 * math.pi))
    gpre = gact * (cdf + pre * pdf)
    gb_ref[...] = jnp.sum(gpre, axis=0, keepdims=True)
    gpre = gpre.astype(bf16)
    mlp = lax.dot_general(act, w2_ref[...], NN, preferred_element_type=f32)
    gn = lax.dot_general(gpre, w1_ref[...], NT, preferred_element_type=f32)

    @pl.when(step == 0)
    def _():
        mlp_ref[...] = mlp
        gn_ref[...] = gn

    @pl.when(step > 0)
    def _():
        mlp_ref[...] += mlp
        gn_ref[...] += gn

    gw1_ref[...] = lax.dot_general(
        n2t_ref[...], gpre, NN, preferred_element_type=f32
    ).astype(bf16)
    gw2_ref[...] = lax.dot_general(
        gmt_ref[...], act, NN, preferred_element_type=f32
    ).astype(bf16)


def feed_forward(n2, n2t, gm, gmt, w1, b1, w2):
    rows, width = n2.shape
    units = w1.shape[1]
    tile = 512

    def whole(a, b):
        return pl.BlockSpec((a, b), lambda j: (0, 0), pipeline_mode=pl.Buffered(1))

    return pl.pallas_call(
        feed_forward_kernel,
        grid=(units // tile,),
        in_specs=[
            whole(rows, width),
            whole(width, rows),
            whole(rows, width),
            whole(width, rows),
            pl.BlockSpec((width, tile), lambda j: (0, j)),
            pl.BlockSpec((1, tile), lambda j: (0, j)),
            pl.BlockSpec((tile, width), lambda j: (j, 0)),
        ],
        out_specs=[
            whole(rows, width),
            whole(rows, width),
            pl.BlockSpec((width, tile), lambda j: (0, j)),
            pl.BlockSpec((width, tile), lambda j: (0, j)),
            pl.BlockSpec((1, tile), lambda j: (0, j)),
        ],
        out_shape=[
            jax.ShapeDtypeStruct((rows, width), f32),
            jax.ShapeDtypeStruct((rows, width), f32),
            jax.ShapeDtypeStruct((width, units), bf16),
            jax.ShapeDtypeStruct((width, units), bf16),
            jax.ShapeDtypeStruct((1, units), f32),
        ],
        compiler_params=pltpu.CompilerParams(vmem_limit_bytes=60 * 2**20),
        cost_estimate=pl.CostEstimate(
            flops=16 * rows * width * units,
            bytes_accessed=8 * width * units,
            transcendentals=2 * rows * units,
        ),
        name="feed_forward",
    )(n2, n2t, gm, gmt, w1, b1, w2)


def norm_rows(values, gain, shift):
    center = values - jnp.mean(values, axis=-1, keepdims=True)
    inverse = lax.rsqrt(jnp.mean(center * center, axis=-1, keepdims=True) + 1e-06)
    normed = center * inverse
    return normed * gain + shift, normed, inverse


def norm_back(grad_norm, normed, inverse, gain):
    scaled = grad_norm * gain
    return inverse * (
        scaled
        - jnp.mean(scaled, axis=-1, keepdims=True)
        - normed * jnp.mean(scaled * normed, axis=-1, keepdims=True)
    )


def body(
    block_input,
    cotangent,
    lengths,
    w_qkv,
    b_qv,
    w_out,
    w_fc1,
    b_fc1,
    w_fc2,
    ln_gain,
    ln_shift,
    layer_scale,
    out_bias,
):
    images, part_rows, width = block_input.shape
    groups = lax.axis_size("dp")
    line = lax.axis_size("tensor")
    rows = part_rows * line
    group = lax.axis_index("dp")
    place = lax.axis_index("tensor")
    flip = group % 2
    mine = jnp.where(flip == 1, line - 1 - place, place)
    active = mine < images

    def image_of(g, z):
        return line - 1 - z if g % 2 else z

    def to_owner(x):
        own = jnp.where(active, x[jnp.minimum(mine, images - 1)], jnp.zeros_like(x[0]))
        out = jnp.zeros((rows, width), x.dtype)
        out = lax.dynamic_update_slice(out, own, (place * part_rows, 0))
        for shift in range(1, line):
            pairs = [
                (g * line + z, g * line + (z + shift) % line)
                for g in range(groups)
                for z in range(line)
                if image_of(g, (z + shift) % line) < images
            ]
            to = (place + shift) % line
            image = jnp.where(flip == 1, line - 1 - to, to)
            sent = lax.ppermute(x[jnp.minimum(image, images - 1)], ("dp", "tensor"), pairs)
            out = lax.dynamic_update_slice(
                out, sent, (((place - shift) % line) * part_rows, 0)
            )
        return out

    def from_owner(y):
        split = y.reshape(line, part_rows, width)
        arrived = [split[place]]
        for shift in range(1, line):
            pairs = [
                (g * line + z, g * line + (z + shift) % line)
                for g in range(groups)
                for z in range(line)
                if image_of(g, z) < images
            ]
            arrived.append(lax.ppermute(split[(place + shift) % line], ("dp", "tensor"), pairs))
        stacked = jnp.stack(arrived)
        out = []
        for i in range(images):
            source = jnp.where(flip == 1, line - 1 - i, i)
            out.append(stacked[(place - source) % line])
        return jnp.stack(out)

    small = jnp.concatenate(
        [
            ln_gain.reshape(-1),
            ln_shift.reshape(-1),
            layer_scale.reshape(-1),
            out_bias.reshape(-1),
            b_qv.astype(f32).reshape(-1),
            b_fc1.astype(f32).reshape(-1),
        ]
    )[None]
    small = lax.all_gather(small, "tensor", axis=0, tiled=False)
    small = lax.all_gather(small, "dp", axis=0, tiled=False).reshape(groups, line, -1)
    own_width = ln_gain.shape[1]
    at = 0

    def take(count):
        nonlocal at
        at += count
        return small[:, :, at - count : at]

    def vectors(x):
        return jnp.transpose(x.reshape(groups, line, 2, own_width), (2, 0, 1, 3)).reshape(2, width)

    gains = vectors(take(2 * own_width))
    shifts = vectors(take(2 * own_width))
    scales = vectors(take(2 * own_width))
    biases = vectors(take(2 * own_width))
    _, bq_rows, bq_cols = b_qv.shape
    qv_bias = jnp.transpose(
        take(2 * bq_rows * bq_cols).reshape(groups, line, 2, bq_rows, bq_cols), (2, 1, 4, 0, 3)
    ).reshape(2, width)
    f_rows, f_cols = b_fc1.shape
    fc1_bias = jnp.transpose(
        take(f_rows * f_cols).reshape(groups, line, f_rows, f_cols), (1, 3, 0, 2)
    ).reshape(1, -1)

    x_all = to_owner(block_input)
    wqkv = lax.all_gather(
        lax.all_gather(w_qkv, "tensor", axis=2, tiled=True), "dp", axis=1, tiled=True
    )
    wout = lax.all_gather(
        lax.all_gather(w_out, "tensor", axis=0, tiled=True), "dp", axis=1, tiled=True
    )
    wfc1 = lax.all_gather(
        lax.all_gather(w_fc1, "tensor", axis=1, tiled=True), "dp", axis=0, tiled=True
    )
    wfc2 = lax.all_gather(
        lax.all_gather(w_fc2, "tensor", axis=0, tiled=True), "dp", axis=1, tiled=True
    )
    cot = to_owner(cotangent)

    length = jnp.where(active, lengths[jnp.minimum(mine, images - 1)], 0).astype(jnp.int32)
    length_array = length.reshape(1)
    valid = (jnp.arange(rows, dtype=jnp.int32) < length).astype(f32)[:, None]

    source = x_all.astype(f32)
    normed_one, hat_first, inv_first = norm_rows(source, gains[0], shifts[0])
    normed1 = normed_one.astype(bf16)
    scale_q = HD ** (-0.5) * LOG2E

    def dot(a, b, dims=NN):
        return lax.dot_general(a, b, dims, preferred_element_type=f32)

    query = ((dot(normed1, wqkv[0]) + qv_bias[0]) * scale_q).astype(bf16)
    key = dot(normed1, wqkv[1]).astype(bf16)
    value = (dot(normed1, wqkv[2]) + qv_bias[1]).astype(bf16)
    context, query_stats = attend_forward(length_array, query, key, value)
    attn = dot(context, wout) + biases[0]
    hidden = source + scales[0] * attn
    normed_two, hat_second, inv_second = norm_rows(hidden, gains[1], shifts[1])
    normed2 = normed_two.astype(bf16)
    grad_out = valid * cot.astype(f32)
    grad_mlp = grad_out * scales[1]
    grad_mlp_b = grad_mlp.astype(bf16)
    mlp, grad_normed2, grad_fc1, grad_fc2, grad_bfc1 = feed_forward(
        normed2, normed2.T, grad_mlp_b, grad_mlp_b.T, wfc1, fc1_bias, wfc2
    )
    mlp = mlp + biases[1]
    block_out = from_owner((valid * (hidden + scales[1] * mlp)).astype(bf16))

    def reduced(grad):
        part = lax.psum_scatter(grad, "dp", scatter_dimension=0, tiled=True)
        return lax.psum_scatter(part, "tensor", scatter_dimension=1, tiled=True).astype(f32)

    shard_fc1 = reduced(grad_fc1)
    shard_fc2 = reduced(grad_fc2).T

    grad_scale2 = jnp.sum(grad_out * mlp, axis=0)
    grad_bias2 = jnp.sum(grad_mlp, axis=0)
    grad_gain2 = jnp.sum(grad_normed2 * hat_second, axis=0)
    grad_shift2 = jnp.sum(grad_normed2, axis=0)
    grad_hidden = grad_out + norm_back(grad_normed2, hat_second, inv_second, gains[1])
    grad_scale1 = jnp.sum(grad_hidden * attn, axis=0)
    grad_attn = grad_hidden * scales[0]
    grad_bias1 = jnp.sum(grad_attn, axis=0)
    grad_attn_b = grad_attn.astype(bf16)
    grad_context = dot(grad_attn_b, wout, NT).astype(bf16)
    grad_wout = dot(grad_attn_b.T, context).astype(bf16)
    shard_wout = reduced(grad_wout).T
    grad_query, grad_key, grad_value = attend_backward(
        length_array, query_stats, key, value, grad_context, context
    )
    grad_bq = jnp.sum(grad_query.astype(f32), axis=0)
    grad_bv = jnp.sum(grad_value.astype(f32), axis=0)
    normed1_t = normed1.T
    grad_wqkv = [dot(normed1_t, g).astype(bf16) for g in (grad_query, grad_key, grad_value)]
    shard_wqkv = jnp.stack([reduced(g) for g in grad_wqkv])
    grad_normed1 = (
        dot(grad_query, wqkv[0], NT) + dot(grad_key, wqkv[1], NT) + dot(grad_value, wqkv[2], NT)
    )
    grad_gain1 = jnp.sum(grad_normed1 * hat_first, axis=0)
    grad_shift1 = jnp.sum(grad_normed1, axis=0)
    grad_source = grad_hidden + norm_back(grad_normed1, hat_first, inv_first, gains[0])
    grad_input = from_owner(grad_source.astype(bf16)).astype(f32)

    small_grads = jnp.concatenate(
        [
            grad_gain1,
            grad_gain2,
            grad_shift1,
            grad_shift2,
            grad_scale1,
            grad_scale2,
            grad_bias1,
            grad_bias2,
            grad_bq,
            grad_bv,
            grad_bfc1.reshape(-1),
        ]
    ).reshape(-1, width)
    small_grads = lax.psum(lax.psum(small_grads, "tensor"), "dp")

    def own_columns(x):
        return lax.dynamic_slice_in_dim(x, (group * line + place) * own_width, own_width, 1)

    shard_gain, shard_shift, shard_scale, shard_bias = (
        own_columns(small_grads[2 * n : 2 * n + 2]) for n in range(4)
    )
    by_head = small_grads[8:10].reshape(2, line, bq_cols, groups, bq_rows)
    shard_bqv = jnp.transpose(by_head[:, place, :, group], (0, 2, 1))
    by_unit = small_grads[10:].reshape(line, f_cols, groups, f_rows)
    shard_bfc1 = by_unit[place, :, group].T
    return (
        block_out,
        grad_input,
        shard_wqkv,
        shard_bqv,
        shard_wout,
        shard_fc1,
        shard_bfc1,
        shard_fc2,
        shard_gain,
        shard_shift,
        shard_scale,
        shard_bias,
    )


def solution(mesh):
    rows = P("dp", "tensor", None)
    vector = P(None, ("dp", "tensor"))
    weights = (
        P(None, "dp", "tensor"),
        P(None, "dp", "tensor"),
        P("tensor", "dp"),
        P("dp", "tensor"),
        P("dp", "tensor"),
        P("tensor", "dp"),
    )
    return jax.shard_map(
        body,
        mesh=mesh,
        in_specs=(rows, rows, P("dp")) + weights + (vector,) * 4,
        out_specs=(rows, rows) + weights + (vector,) * 4,
        check_vma=False,
    )
```

```python
import functools
import math

import jax
import jax.numpy as jnp
from jax import lax
from jax.experimental import pallas as pl
from jax.experimental.pallas import tpu as pltpu
from jax.sharding import PartitionSpec as P

HD = 64
LANES = 128
LOG2E = math.log2(math.e)
NEG = -1e30
NT = (((1,), (1,)), ((), ()))
NN = (((1,), (0,)), ((), ()))
f32 = jnp.float32
bf16 = jnp.bfloat16


def round_up(n, m):
    return (n + m - 1) // m * m


def parts(x):
    hi = x.astype(bf16).astype(f32)
    rest = x - hi
    mid = rest.astype(bf16).astype(f32)
    return hi, mid, rest - mid


def keys_with_bias(keys, lane, row, length, own, spare):
    bias = jnp.where(row < length, 0.0, NEG)
    ones = jnp.where((lane >= spare) & (lane < spare + 3), 1.0, 0.0)
    return jnp.where(own, keys, jnp.where(lane == spare + 3, bias, ones)).astype(bf16)


MESH = pl.DeviceIdType.MESH
ANY = pl.BlockSpec(memory_space=pl.ANY)
DMA = pltpu.SemaphoreType.DMA


def flipped(g, mask):
    bit = 1
    while bit <= mask:
        if mask & bit:
            g = g + bit * (1 - 2 * ((g // bit) % 2))
        bit *= 2
    return g


class Place:
    def __init__(self, groups, line):
        self.groups, self.line = groups, line
        self.g, self.z = lax.axis_index("dp"), lax.axis_index("tensor")
        self.masks = list(range(0, groups, 2))
        self.square = groups == 8
        self.direct = [2, 4] if self.square else self.masks[1:]

    def image(self, z):
        odd = self.g % 2
        return z + odd * (self.line - 1 - 2 * z)

    def up(self, k):
        return lax.rem(self.z + k, self.line)

    def down(self, k):
        return lax.rem(self.z + self.line - k, self.line)

    def barrier(self):
        semaphore = pltpu.get_barrier_semaphore()
        peers = [(self.g, self.up(s)) for s in range(1, self.line)]
        peers += [(flipped(self.g, m), self.z) for m in self.direct + [1]]
        for peer in peers:
            pl.semaphore_signal(semaphore, inc=1, device_id=peer, device_id_type=MESH)
        pl.semaphore_wait(semaphore, len(peers))


def remote(src, dst, send, recv, device):
    return pltpu.make_async_remote_copy(
        src_ref=src, dst_ref=dst, send_sem=send, recv_sem=recv, device_id=device, device_id_type=MESH
    )


class Gather:
    @staticmethod
    def sems(groups, line):
        chips = groups // 2
        return [
            DMA((line,)),
            DMA((line,)),
            DMA((chips, line)),
            DMA((chips, line)),
            DMA((chips, line)),
            DMA((chips, line)),
        ]

    def __init__(self, at, shard, full, sems):
        self.at, self.shard, self.full = at, shard, full
        self.zs, self.zr, self.ds, self.dr, self.cs, self.cr = sems
        self.rows = shard.shape[0]

    def piece(self, mask, k):
        at = self.at
        rows = pl.ds(pl.multiple_of(flipped(at.g, mask) * self.rows, 8), self.rows)
        return self.full.at[at.down(k), rows, :]

    def own(self, k):
        return self.shard if k == 0 else self.piece(0, k)

    def local(self):
        return pltpu.make_async_copy(self.shard, self.piece(0, 0), self.zs.at[0])

    def along(self, k, arriving=False):
        dst = self.piece(0, k if arriving else 0)
        src = dst if arriving else self.shard
        return remote(src, dst, self.zs.at[k], self.zr.at[k], (self.at.g, self.at.up(k)))

    def across(self, mask, k, arriving=False):
        at = self.at
        if at.square and mask == 6:
            via, peer = (2, 4) if k < at.line // 2 else (4, 2)
            src = dst = self.piece(via, k)
        else:
            peer = mask
            src, dst = self.own(k), self.piece(0, k)
        if arriving:
            src = dst = self.piece(mask, k)
        return remote(
            src, dst, self.ds.at[mask // 2, k], self.dr.at[mask // 2, k], (flipped(at.g, peer), at.z)
        )

    def core(self, mask, k, arriving=False):
        at = self.at
        if arriving:
            dst = self.piece(mask ^ 1, k)
            src = dst
        else:
            dst = self.piece(mask, k)
            src = self.own(k) if mask == 0 else dst
        return remote(src, dst, self.cs.at[mask // 2, k], self.cr.at[mask // 2, k], (flipped(at.g, 1), at.z))

    def start(self):
        self.local().start()
        for k in range(1, self.at.line):
            self.along(k).start()
        self.spread(0)

    def spread(self, k):
        if k:
            self.along(k, True).wait_recv()
        for mask in self.at.direct:
            self.across(mask, k).start()
        self.core(0, k).start()

    def passing(self, k):
        at = self.at
        for mask in at.direct:
            self.across(mask, k, True).wait_recv()
            if at.square and mask == (2 if k < at.line // 2 else 4):
                self.across(6, k).start()
            self.core(mask, k).start()

    def last(self, k):
        if self.at.square:
            self.across(6, k, True).wait_recv()
            self.core(6, k).start()

    def finish(self):
        at = self.at
        for k in range(at.line):
            for mask in at.masks:
                self.core(mask, k, True).wait_recv()
                self.core(mask, k).wait_send()
                if mask:
                    self.across(mask, k).wait_send()
            if k:
                self.along(k).wait_send()
        self.local().wait()

    def steps(self):
        line = self.at.line
        out = [self.start]
        for k in range(1, line):
            out.append(functools.partial(self.spread, k))
        for k in range(line):
            out.append(functools.partial(self.passing, k))
        for k in range(line):
            out.append(functools.partial(self.last, k))
        out.append(self.finish)
        return out


class ToOwner:
    @staticmethod
    def sems(groups, line):
        return [DMA((line,)), DMA((line,))]

    def __init__(self, at, rows, image, sems):
        self.at, self.rows, self.image = at, rows, image
        self.send, self.recv = sems
        self.count = rows.shape[0]

    def local(self):
        at = self.at
        return pltpu.make_async_copy(
            self.rows.at[jnp.minimum(at.image(at.z), self.count - 1)], self.image.at[at.z], self.send.at[0]
        )

    def copy(self, k, arriving=False):
        at = self.at
        to = at.up(k)
        src = self.rows.at[jnp.minimum(at.image(to), self.count - 1)]
        dst = self.image.at[at.down(k) if arriving else at.z]
        return remote(src, dst, self.send.at[k], self.recv.at[k], (at.g, to))

    def start(self):
        at = self.at
        self.local().start()
        for k in range(1, at.line):
            pl.when(at.image(at.up(k)) < self.count)(self.copy(k).start)

    def finish(self):
        at = self.at
        for k in range(1, at.line):
            pl.when(at.image(at.up(k)) < self.count)(self.copy(k).wait_send)
            pl.when(at.image(at.z) < self.count)(self.copy(k, True).wait_recv)
        self.local().wait()


class FromOwner:
    sems = ToOwner.sems

    def __init__(self, at, image, rows, sems):
        self.at, self.rows, self.image = at, rows, image
        self.send, self.recv = sems
        self.count = rows.shape[0]

    def local(self):
        at = self.at
        return pltpu.make_async_copy(
            self.image.at[at.z], self.rows.at[jnp.minimum(at.image(at.z), self.count - 1)], self.send.at[0]
        )

    def copy(self, k, arriving=False):
        at = self.at
        owner = at.down(k) if arriving else at.z
        dst = self.rows.at[jnp.minimum(at.image(owner), self.count - 1)]
        return remote(self.image.at[at.up(k)], dst, self.send.at[k], self.recv.at[k], (at.g, at.up(k)))

    def start(self):
        at = self.at

        @pl.when(at.image(at.z) < self.count)
        def _():
            self.local().start()
            for k in range(1, at.line):
                self.copy(k).start()

    def finish(self):
        at = self.at

        @pl.when(at.image(at.z) < self.count)
        def _():
            for k in range(1, at.line):
                self.copy(k).wait_send()
            self.local().wait()

        for k in range(1, at.line):
            pl.when(at.image(at.down(k)) < self.count)(self.copy(k, True).wait_recv)


class Reduce:
    @staticmethod
    def scratch(groups, line, r, c, dtype):
        chips = groups // 2
        return [
            pltpu.VMEM((chips, line, r, c), dtype),
            pltpu.VMEM((chips, line, r, c), dtype),
            pltpu.VMEM((chips, line, r, c), dtype),
            pltpu.VMEM((line, r, c), dtype),
            DMA((chips, line)),
            DMA((chips, line)),
            DMA((chips, line)),
            DMA((chips, line)),
            DMA((chips, line)),
            DMA((line,)),
            DMA((line,)),
        ]

    def __init__(self, at, full, scratch, rows):
        self.at, self.full, self.rows = at, full, rows
        self.cbuf, self.sums, self.dbuf, self.zbuf = scratch[:4]
        self.ls, self.cs, self.cr, self.ds, self.dr, self.zs, self.zr = scratch[4:]
        self.order = [6, 2, 4, 0] if at.square else at.masks[1:] + [0]

    def piece(self, mask, k):
        at = self.at
        rows = pl.ds(pl.multiple_of(flipped(at.g, mask) * self.rows, 8), self.rows)
        return self.full.at[at.down(k), rows, :]

    def local(self, mask, k):
        return pltpu.make_async_copy(
            self.piece(mask, k), self.sums.at[mask // 2, k], self.ls.at[mask // 2, k]
        )

    def core(self, mask, k):
        at, m = self.at, mask // 2
        return remote(
            self.piece(mask ^ 1, k), self.cbuf.at[m, k], self.cs.at[m, k], self.cr.at[m, k],
            (flipped(at.g, 1), at.z),
        )

    def across(self, mask, k):
        at, m = self.at, mask // 2
        peer = mask
        if at.square and mask == 6:
            peer = 4 if k < at.line // 2 else 2
        return remote(
            self.sums.at[m, k], self.dbuf.at[m, k], self.ds.at[m, k], self.dr.at[m, k],
            (flipped(at.g, peer), at.z),
        )

    def along(self, k):
        at = self.at
        return remote(
            self.sums.at[0, k], self.zbuf.at[k], self.zs.at[k], self.zr.at[k], (at.g, at.down(k))
        )

    def start(self):
        for mask in self.order:
            for k in range(self.at.line):
                self.core(mask, k).start()
                self.local(mask, k).start()

    def add(self, m, k, other):
        total = self.sums[m, k].astype(f32) + other.astype(f32)
        self.sums[m, k] = total.astype(self.sums.dtype)

    def pair(self, mask, k):
        self.local(mask, k).wait()
        self.core(mask, k).wait_recv()
        self.add(mask // 2, k, self.cbuf[mask // 2, k])

    def pairs(self, mask):
        at = self.at
        for k in range(at.line):
            self.pair(mask, k)
            waits = at.square and mask == (2 if k < at.line // 2 else 4)
            if mask and not waits:
                self.across(mask, k).start()

    def joined(self, k):
        at = self.at
        if at.square:
            mask = 2 if k < at.line // 2 else 4
            self.across(6, k).wait_recv()
            self.add(mask // 2, k, self.dbuf[3, k])
            self.across(mask, k).start()

    def own(self, k):
        for mask in self.at.direct:
            self.across(mask, k).wait_recv()
            self.add(0, k, self.dbuf[mask // 2, k])
        if k:
            self.along(k).start()

    def finish(self):
        at = self.at
        for k in range(at.line):
            for mask in at.masks:
                self.core(mask, k).wait_send()
                if mask:
                    self.across(mask, k).wait_send()
            if k:
                self.along(k).wait_send()
                self.along(k).wait_recv()
        total = self.sums[0, 0].astype(f32)
        for k in range(1, at.line):
            total += self.zbuf[k].astype(f32)
        return total

    def steps(self):
        ks = range(self.at.line)
        out = [self.start]
        out += [functools.partial(self.pairs, mask) for mask in self.order]
        out += [functools.partial(self.joined, k) for k in ks]
        return out + [functools.partial(self.own, k) for k in ks]


def run_ticks(ticks, step, half):
    for at, work in ticks:
        if at % 2 == half:
            pl.when(step == at // 2)(work)


def arrive_kernel(groups, line, x_ref, shard_ref, small_ref, xo_ref, full_ref, smalls_ref, *sems):
    at = Place(groups, line)
    n = len(Gather.sems(groups, line))
    rows = ToOwner(at, x_ref, xo_ref, sems[2 * n :])
    weights = Gather(at, shard_ref, full_ref, sems[:n])
    small = Gather(at, small_ref, smalls_ref, sems[n : 2 * n])
    at.barrier()
    for one, two in zip(small.steps(), weights.steps()):
        one()
        two()
        if one == small.start:
            rows.start()
    rows.finish()


def arrive(groups, line, x, shard, small):
    images, part_rows, width = x.shape
    return pl.pallas_call(
        functools.partial(arrive_kernel, groups, line),
        in_specs=[ANY] * 3,
        out_specs=[ANY] * 3,
        out_shape=[
            jax.ShapeDtypeStruct((line, part_rows, width), x.dtype),
            jax.ShapeDtypeStruct((line, groups * shard.shape[0], shard.shape[1]), shard.dtype),
            jax.ShapeDtypeStruct((line, groups * small.shape[0], small.shape[1]), small.dtype),
        ],
        scratch_shapes=Gather.sems(groups, line) * 2 + ToOwner.sems(groups, line),
        compiler_params=pltpu.CompilerParams(collective_id=1, has_side_effects=True),
        name="arrive",
    )(x, shard, small)


def leave_kernel(groups, line, r, y_ref, full_ref, smalls_ref, yo_ref, shard_ref, small_ref, *scratch):
    at = Place(groups, line)
    n = len(ToOwner.sems(groups, line))
    m = (len(scratch) - n) // 2
    rows = FromOwner(at, y_ref, yo_ref, scratch[:n])
    weights = Reduce(at, full_ref, scratch[n : n + m], r)
    small = Reduce(at, smalls_ref, scratch[n + m :], small_ref.shape[0])
    at.barrier()
    for one, two in zip(weights.steps(), small.steps()):
        one()
        two()
        if two == small.start:
            rows.start()
    shard_ref[...] = weights.finish()
    small_ref[...] = small.finish()
    rows.finish()


def leave(groups, line, images, y, full, smalls):
    _, part_rows, width = y.shape
    _, r, c = full.shape
    r = r // groups
    sr, sc = smalls.shape[1] // groups, smalls.shape[2]
    vmem = pl.BlockSpec(memory_space=pltpu.VMEM)
    return pl.pallas_call(
        functools.partial(leave_kernel, groups, line, r),
        in_specs=[ANY] * 3,
        out_specs=[ANY, vmem, vmem],
        out_shape=[
            jax.ShapeDtypeStruct((images, part_rows, width), y.dtype),
            jax.ShapeDtypeStruct((r, c), f32),
            jax.ShapeDtypeStruct((sr, sc), f32),
        ],
        scratch_shapes=ToOwner.sems(groups, line)
        + Reduce.scratch(groups, line, r, c, full.dtype)
        + Reduce.scratch(groups, line, sr, sc, smalls.dtype),
        compiler_params=pltpu.CompilerParams(
            collective_id=2, has_side_effects=True, vmem_limit_bytes=40 * 2**20
        ),
        name="leave",
    )(y, full, smalls)


def project_kernel(n1_ref, w_ref, b_ref, out_ref):
    scale = jnp.where(pl.program_id(1) == 0, HD ** (-0.5) * LOG2E, 1.0)
    out = lax.dot_general(n1_ref[...], w_ref[0], NN, preferred_element_type=f32) + b_ref[0]
    out_ref[0] = (out * scale).astype(bf16)


def project(normed1, weights, bias):
    rows, width = normed1.shape
    line = weights.shape[0]
    cols = width // line
    return pl.pallas_call(
        project_kernel,
        grid=(line, 3),
        in_specs=[
            pl.BlockSpec((rows, width), lambda t, k: (0, 0), pipeline_mode=pl.Buffered(1)),
            pl.BlockSpec((1, width, cols), lambda t, k: (t, 0, k)),
            pl.BlockSpec((1, 1, cols), lambda t, k: (k, 0, t)),
        ],
        out_specs=pl.BlockSpec((1, rows, cols), lambda t, k: (k, 0, t)),
        out_shape=jax.ShapeDtypeStruct((3, rows, width), bf16),
        compiler_params=pltpu.CompilerParams(vmem_limit_bytes=40 * 2**20),
        cost_estimate=pl.CostEstimate(
            flops=6 * rows * width * width, bytes_accessed=16 * rows * width, transcendentals=0
        ),
        name="project",
    )(normed1, weights, bias)


def attend_forward_kernel(
    groups, line, rows, padded, len_ref, q_ref, k_ref, v_ref, shard_ref, cot_ref,
    ctx_ref, qa_ref, full_ref, coto_ref, ka, va, *sems
):
    at = Place(groups, line)
    n = len(Gather.sems(groups, line))
    weights = Gather(at, shard_ref, full_ref, sems[:n])
    cot = ToOwner(at, cot_ref, coto_ref, sems[n:])
    steps = weights.steps()
    halves = 2 * pl.num_programs(0)
    first, spreads, passes, rest = steps[0], steps[1:line], steps[line : 2 * line], steps[2 * line :]

    def begin():
        at.barrier()
        first()

    ticks = [(0, begin), (6, cot.start)]
    for k in range(1, line):
        ticks.append((min(4 * k, 15), spreads[k - 1]))
    for k in range(line):
        ticks.append((min(4 * k + 4, 15), passes[k]))
    step = pl.program_id(0)
    length = len_ref[0]
    lane = lax.broadcasted_iota(jnp.int32, (padded, LANES), 1)
    row = lax.broadcasted_iota(jnp.int32, (padded, LANES), 0)
    lb = lane[:rows]
    if padded > rows:
        va[rows:] = jnp.zeros((padded - rows, LANES), bf16)
    for half in range(2):
        run_ticks(ticks, step, half)
        own = (lb < HD) if half == 0 else (lb >= HD)
        spare = HD if half == 0 else 0
        ka[:rows] = keys_with_bias(k_ref[...].astype(f32), lb, row[:rows], length, own, spare)
        if padded > rows:
            ka[rows:] = jnp.where(lane[rows:] == spare + 3, NEG, 0.0).astype(bf16)
        va[:rows] = jnp.where(
            own, v_ref[...].astype(f32), jnp.where(lb == spare, 1.0, 0.0)
        ).astype(bf16)
        qa = jnp.where(own, q_ref[...].astype(f32), jnp.where(lb == spare + 3, 1.0, 0.0))
        s = lax.dot_general(qa.astype(bf16), ka[...], NT, preferred_element_type=f32)
        m = jnp.max(s, axis=1, keepdims=True)
        p = jnp.exp2(s - m).astype(bf16)
        o = lax.dot_general(p, va[...], NN, preferred_element_type=f32)
        total = o[:, spare : spare + 1]
        o = o / total
        hi, mid, lo = parts(-(m + jnp.log2(total)))
        if half == 0:
            ctx_ref[...] = o.astype(bf16)
        else:
            ctx_ref[...] = jnp.where(own, o, ctx_ref[...].astype(f32)).astype(bf16)
        stats = jnp.where(lb == spare + 2, lo, qa)
        stats = jnp.where(lb == spare + 1, mid, stats)
        qa_ref[half] = jnp.where(lb == spare, hi, stats).astype(bf16)

    @pl.when(step == pl.num_programs(0) - 1)
    def _():
        for work in rest:
            work()
        cot.finish()


def attend_forward(groups, line, length, qkv, shard, cot):
    _, rows, width = qkv.shape
    padded = round_up(rows, LANES)
    spec = pl.BlockSpec((rows, LANES), lambda j: (0, j))

    def third(n):
        return pl.BlockSpec((None, rows, LANES), lambda j: (n, 0, j))

    return pl.pallas_call(
        functools.partial(attend_forward_kernel, groups, line, rows, padded),
        grid=(width // LANES,),
        in_specs=[pl.BlockSpec(memory_space=pltpu.SMEM), third(0), third(1), third(2), ANY, ANY],
        out_specs=[spec, pl.BlockSpec((2, rows, LANES), lambda j: (j, 0, 0)), ANY, ANY],
        out_shape=[
            jax.ShapeDtypeStruct((rows, width), bf16),
            jax.ShapeDtypeStruct((width // HD, rows, LANES), bf16),
            jax.ShapeDtypeStruct((line, groups * shard.shape[0], shard.shape[1]), shard.dtype),
            jax.ShapeDtypeStruct((line,) + cot.shape[1:], cot.dtype),
        ],
        scratch_shapes=[pltpu.VMEM((padded, LANES), bf16), pltpu.VMEM((padded, LANES), bf16)]
        + Gather.sems(groups, line)
        + ToOwner.sems(groups, line),
        compiler_params=pltpu.CompilerParams(
            collective_id=3, has_side_effects=True, vmem_limit_bytes=56 * 2**20
        ),
        cost_estimate=pl.CostEstimate(
            flops=16 * rows * rows * width,
            bytes_accessed=12 * rows * width,
            transcendentals=rows * rows * width // HD,
        ),
        name="attend_forward",
    )(length, qkv, qkv, qkv, shard, cot)


def attend_backward_kernel(
    groups, line, rows, padded, blocks, len_ref, qa_ref, k_ref, v_ref, gc_ref, ctx_ref, y_ref, full_ref,
    gq_ref, gk_ref, gv_ref, yo_ref, shard_ref, ka, va, qs, ga, acc, *scratch
):
    at = Place(groups, line)
    n = len(ToOwner.sems(groups, line))
    back = FromOwner(at, y_ref, yo_ref, scratch[:n])
    weights = Reduce(at, full_ref, scratch[n:], shard_ref.shape[0])
    steps = weights.steps()
    chips = groups // 2

    def begin():
        at.barrier()
        steps[0]()
        back.start()

    ticks = [(0, begin)]
    for i in range(chips):
        ticks.append((min(i + 1, 4), steps[1 + i]))
    for k in range(line):
        ticks.append((min(6 + k // 2, 15), steps[1 + chips + k]))
    for k in range(line):
        ticks.append((12, steps[1 + chips + line + k]))
    step = pl.program_id(0)
    length = len_ref[0]
    lane = lax.broadcasted_iota(jnp.int32, (padded, LANES), 1)
    row = lax.broadcasted_iota(jnp.int32, (padded, LANES), 0)
    size = rows // blocks
    ls = lane[:rows]
    for half in range(2):
        run_ticks(ticks, step, half)
        own = (ls < HD) if half == 0 else (ls >= HD)
        spare = HD if half == 0 else 0
        ownb = own[:size]
        gc = gc_ref[...].astype(f32)
        corr = jnp.sum(
            jnp.where(own, gc * ctx_ref[...].astype(f32), 0.0), axis=1, keepdims=True
        )
        hi, mid, lo = parts(-corr)
        extra = jnp.where(ls == spare + 1, mid, jnp.where(ls == spare + 2, lo, 0.0))
        ga[:rows] = jnp.where(own, gc, jnp.where(ls == spare, hi, extra)).astype(bf16)
        qs[:rows] = qa_ref[half]
        if padded > rows:
            ga[rows:] = jnp.zeros((padded - rows, LANES), bf16)
            qs[rows:] = jnp.where(lane[rows:] == spare, NEG, 0.0).astype(bf16)
        ka[...] = keys_with_bias(k_ref[...].astype(f32), ls, row[:rows], length, own, spare)
        ones = jnp.where((ls >= spare) & (ls < spare + 3), 1.0, 0.0)
        va[...] = jnp.where(own, v_ref[...].astype(f32), ones).astype(bf16)
        acc[...] = jnp.zeros_like(acc)

        def block(b, carry):
            r = pl.ds(pl.multiple_of(b * size, 16), size)
            kb = ka[r, :]
            p = jnp.exp2(lax.dot_general(kb, qs[...], NT, preferred_element_type=f32))
            gp = lax.dot_general(va[r, :], ga[...], NT, preferred_element_type=f32)
            ds = (p * gp).astype(bf16)
            gv = lax.dot_general(p.astype(bf16), ga[...], NN, preferred_element_type=f32)
            gk = lax.dot_general(ds, qs[...], NN, preferred_element_type=f32) * (1.0 / LOG2E)
            acc[...] += lax.dot_general(kb.T, ds, NN, preferred_element_type=f32)
            if half == 0:
                gv_ref[r, :] = gv.astype(bf16)
                gk_ref[r, :] = gk.astype(bf16)
            else:
                gv_ref[r, :] = jnp.where(ownb, gv, gv_ref[r, :].astype(f32)).astype(bf16)
                gk_ref[r, :] = jnp.where(ownb, gk, gk_ref[r, :].astype(f32)).astype(bf16)
            return carry

        lax.fori_loop(0, blocks, block, 0)
        gq = acc[...].T[:rows] * HD ** (-0.5)
        if half == 0:
            gq_ref[...] = gq.astype(bf16)
        else:
            gq_ref[...] = jnp.where(own, gq, gq_ref[...].astype(f32)).astype(bf16)

    @pl.when(step == pl.num_programs(0) - 1)
    def _():
        shard_ref[...] = weights.finish()
        back.finish()


def attend_backward(groups, line, images, length, qa, qkv, gc, ctx, y, full):
    _, rows, width = qkv.shape
    padded = round_up(rows, LANES)
    blocks = 2 if rows % 32 == 0 else 1
    spec = pl.BlockSpec((rows, LANES), lambda j: (0, j))
    r, c = full.shape[1] // groups, full.shape[2]

    def third(n):
        return pl.BlockSpec((None, rows, LANES), lambda j: (n, 0, j))

    return pl.pallas_call(
        functools.partial(attend_backward_kernel, groups, line, rows, padded, blocks),
        grid=(width // LANES,),
        in_specs=[
            pl.BlockSpec(memory_space=pltpu.SMEM),
            pl.BlockSpec((2, rows, LANES), lambda j: (j, 0, 0)),
            third(1),
            third(2),
            spec,
            spec,
            ANY,
            ANY,
        ],
        out_specs=[spec] * 3 + [ANY, pl.BlockSpec((r, c), lambda j: (0, 0))],
        out_shape=[jax.ShapeDtypeStruct((rows, width), bf16)] * 3
        + [jax.ShapeDtypeStruct((images,) + y.shape[1:], y.dtype), jax.ShapeDtypeStruct((r, c), f32)],
        scratch_shapes=[
            pltpu.VMEM((rows, LANES), bf16),
            pltpu.VMEM((rows, LANES), bf16),
            pltpu.VMEM((padded, LANES), bf16),
            pltpu.VMEM((padded, LANES), bf16),
            pltpu.VMEM((LANES, padded), f32),
        ]
        + ToOwner.sems(groups, line)
        + Reduce.scratch(groups, line, r, c, full.dtype),
        compiler_params=pltpu.CompilerParams(
            collective_id=4, has_side_effects=True, vmem_limit_bytes=62 * 2**20
        ),
        cost_estimate=pl.CostEstimate(
            flops=40 * rows * rows * width,
            bytes_accessed=16 * rows * width,
            transcendentals=rows * rows * width // HD,
        ),
        name="attend_backward",
    )(length, qa, qkv, qkv, gc, ctx, y, full)


def feed_forward_kernel(
    tile, n2_ref, n2t_ref, gm_ref, gmt_ref, w_ref, b1_ref, mlp_ref, gn_ref, gw_ref, gb_ref
):
    step = pl.program_id(0)
    w1 = w_ref[0, :, :tile]
    w2t = w_ref[0, :, tile:]
    pre = lax.dot_general(n2_ref[...], w1, NN, preferred_element_type=f32) + b1_ref[...]
    gact = lax.dot_general(gm_ref[...], w2t, NN, preferred_element_type=f32)
    cdf = 0.5 * (1.0 + lax.erf(pre * (1 / math.sqrt(2))))
    act = (pre * cdf).astype(bf16)
    pdf = jnp.exp2(pre * pre * (-0.5 * LOG2E)) * (1 / math.sqrt(2 * math.pi))
    gpre = gact * (cdf + pre * pdf)
    gb_ref[...] = jnp.sum(gpre, axis=0, keepdims=True)
    gpre = gpre.astype(bf16)
    mlp = lax.dot_general(act, w2t, NT, preferred_element_type=f32)
    gn = lax.dot_general(gpre, w1, NT, preferred_element_type=f32)

    @pl.when(step == 0)
    def _():
        mlp_ref[...] = mlp
        gn_ref[...] = gn

    @pl.when(step > 0)
    def _():
        mlp_ref[...] += mlp
        gn_ref[...] += gn

    gw_ref[0, :, :tile] = lax.dot_general(
        n2t_ref[...], gpre, NN, preferred_element_type=f32
    ).astype(bf16)
    gw_ref[0, :, tile:] = lax.dot_general(
        gmt_ref[...], act, NN, preferred_element_type=f32
    ).astype(bf16)


def feed_forward(n2, n2t, gm, gmt, weights, b1, tile):
    rows, width = n2.shape
    units = b1.shape[1]
    per = weights.shape[2] // (2 * tile)

    def whole(a, b):
        return pl.BlockSpec((a, b), lambda j: (0, 0), pipeline_mode=pl.Buffered(1))

    both = pl.BlockSpec((1, width, 2 * tile), lambda j: (j // per, 0, j % per))
    return pl.pallas_call(
        functools.partial(feed_forward_kernel, tile),
        grid=(units // tile,),
        in_specs=[
            whole(rows, width),
            whole(width, rows),
            whole(rows, width),
            whole(width, rows),
            both,
            pl.BlockSpec((1, tile), lambda j: (0, j)),
        ],
        out_specs=[
            whole(rows, width),
            whole(rows, width),
            both,
            pl.BlockSpec((1, tile), lambda j: (0, j)),
        ],
        out_shape=[
            jax.ShapeDtypeStruct((rows, width), f32),
            jax.ShapeDtypeStruct((rows, width), f32),
            jax.ShapeDtypeStruct(weights.shape, bf16),
            jax.ShapeDtypeStruct((1, units), f32),
        ],
        compiler_params=pltpu.CompilerParams(vmem_limit_bytes=60 * 2**20),
        cost_estimate=pl.CostEstimate(
            flops=16 * rows * width * units,
            bytes_accessed=8 * width * units,
            transcendentals=2 * rows * units,
        ),
        name="feed_forward",
    )(n2, n2t, gm, gmt, weights, b1)


def norm_rows(values, gain, shift):
    center = values - jnp.mean(values, axis=-1, keepdims=True)
    inverse = lax.rsqrt(jnp.mean(center * center, axis=-1, keepdims=True) + 1e-06)
    normed = center * inverse
    return normed * gain + shift, normed, inverse


def norm_back(grad_norm, normed, inverse, gain):
    scaled = grad_norm * gain
    return inverse * (
        scaled
        - jnp.mean(scaled, axis=-1, keepdims=True)
        - normed * jnp.mean(scaled * normed, axis=-1, keepdims=True)
    )


def body(
    block_input,
    cotangent,
    lengths,
    w_qkv,
    b_qv,
    w_out,
    w_fc1,
    b_fc1,
    w_fc2,
    ln_gain,
    ln_shift,
    layer_scale,
    out_bias,
):
    images, part_rows, width = block_input.shape
    groups = lax.axis_size("dp")
    line = lax.axis_size("tensor")
    rows = part_rows * line
    group = lax.axis_index("dp")
    place = lax.axis_index("tensor")
    flip = group % 2
    mine = jnp.where(flip == 1, line - 1 - place, place)
    active = mine < images

    tile = min(512, w_fc1.shape[1])
    qkv_out = jnp.concatenate([w_qkv[0], w_qkv[1], w_qkv[2], w_out.T], axis=1)
    tiles = (w_fc1.shape[0], -1, 1, tile)
    fc_both = jnp.concatenate([w_fc1.reshape(tiles), w_fc2.T.reshape(tiles)], axis=2).reshape(
        w_fc1.shape[0], -1
    )
    small = jnp.concatenate(
        [
            ln_gain.reshape(-1),
            ln_shift.reshape(-1),
            layer_scale.reshape(-1),
            out_bias.reshape(-1),
            b_qv.astype(f32).reshape(-1),
            b_fc1.astype(f32).reshape(-1),
        ]
    )
    small = jnp.pad(small, (0, round_up(small.size, 8 * LANES) - small.size)).reshape(-1, LANES)
    x_all, weights, small = arrive(groups, line, block_input, qkv_out, small)
    x_all = jnp.where(active, x_all.reshape(rows, width), 0)
    small = jnp.transpose(small.reshape(line, groups, -1), (1, 0, 2))
    own_width = ln_gain.shape[1]
    at = 0

    def take(count):
        nonlocal at
        at += count
        return small[:, :, at - count : at]

    def vectors(x):
        return jnp.transpose(x.reshape(groups, line, 2, own_width), (2, 0, 1, 3)).reshape(2, width)

    gains = vectors(take(2 * own_width))
    shifts = vectors(take(2 * own_width))
    scales = vectors(take(2 * own_width))
    biases = vectors(take(2 * own_width))
    _, bq_rows, bq_cols = b_qv.shape
    qv_bias = jnp.transpose(
        take(2 * bq_rows * bq_cols).reshape(groups, line, 2, bq_rows, bq_cols), (2, 1, 4, 0, 3)
    ).reshape(2, width)
    f_rows, f_cols = b_fc1.shape
    fc1_bias = jnp.transpose(
        take(f_rows * f_cols).reshape(groups, line, f_rows, f_cols), (1, 3, 0, 2)
    ).reshape(1, -1)

    length = jnp.where(active, lengths[jnp.minimum(mine, images - 1)], 0).astype(jnp.int32)
    length_array = length.reshape(1)
    valid = (jnp.arange(rows, dtype=jnp.int32) < length).astype(f32)[:, None]

    source = x_all.astype(f32)
    normed_one, hat_first, inv_first = norm_rows(source, gains[0], shifts[0])
    normed1 = normed_one.astype(bf16)

    def dot(a, b, dims=NN):
        return lax.dot_general(a, b, dims, preferred_element_type=f32)

    cols = width // line
    zero = jnp.zeros_like(qv_bias[:1])
    qkv = project(normed1, weights, jnp.stack([qv_bias[:1], zero, qv_bias[1:]]))
    context, query_stats, fc_weights, cot = attend_forward(
        groups, line, length_array, qkv, fc_both, cotangent
    )
    cot = jnp.where(active, cot.reshape(rows, width), 0)
    wout_t = weights[:, :, 3 * cols :]
    attn = (
        jnp.einsum(
            "stc,tdc->sd", context.reshape(rows, line, cols), wout_t, preferred_element_type=f32
        )
        + biases[0]
    )
    hidden = source + scales[0] * attn
    normed_two, hat_second, inv_second = norm_rows(hidden, gains[1], shifts[1])
    normed2 = normed_two.astype(bf16)
    grad_out = valid * cot.astype(f32)
    grad_mlp = grad_out * scales[1]
    grad_mlp_b = grad_mlp.astype(bf16)
    mlp, grad_normed2, grad_fc, grad_bfc1 = feed_forward(
        normed2, normed2.T, grad_mlp_b, grad_mlp_b.T, fc_weights, fc1_bias, tile
    )
    mlp = mlp + biases[1]
    block_out = (valid * (hidden + scales[1] * mlp)).astype(bf16).reshape(line, part_rows, width)
    grad_scale2 = jnp.sum(grad_out * mlp, axis=0)
    grad_bias2 = jnp.sum(grad_mlp, axis=0)
    grad_gain2 = jnp.sum(grad_normed2 * hat_second, axis=0)
    grad_shift2 = jnp.sum(grad_normed2, axis=0)
    grad_hidden = grad_out + norm_back(grad_normed2, hat_second, inv_second, gains[1])
    grad_scale1 = jnp.sum(grad_hidden * attn, axis=0)
    grad_attn = grad_hidden * scales[0]
    grad_bias1 = jnp.sum(grad_attn, axis=0)
    grad_attn_b = grad_attn.astype(bf16)
    grad_context = (
        jnp.einsum("sd,tdc->stc", grad_attn_b, wout_t, preferred_element_type=f32)
        .astype(bf16)
        .reshape(rows, width)
    )
    grad_query, grad_key, grad_value, block_out, shard_fc = attend_backward(
        groups,
        line,
        images,
        length_array,
        query_stats,
        qkv,
        grad_context,
        context,
        block_out,
        grad_fc,
    )
    grad_bq = jnp.sum(grad_query.astype(f32), axis=0)
    grad_bv = jnp.sum(grad_value.astype(f32), axis=0)
    split = (rows, line, cols)
    grad_parts = [
        jnp.einsum("sd,stc->tdc", a, b.reshape(split), preferred_element_type=f32).astype(bf16)
        for a, b in (
            (normed1, grad_query),
            (normed1, grad_key),
            (normed1, grad_value),
            (grad_attn_b, context),
        )
    ]
    grad_weights = jnp.concatenate(grad_parts, axis=2)
    grad_normed1 = sum(
        jnp.einsum(
            "stc,tdc->sd",
            g.reshape(split),
            weights[:, :, n * cols : (n + 1) * cols],
            preferred_element_type=f32,
        )
        for n, g in enumerate((grad_query, grad_key, grad_value))
    )
    grad_gain1 = jnp.sum(grad_normed1 * hat_first, axis=0)
    grad_shift1 = jnp.sum(grad_normed1, axis=0)
    grad_source = grad_hidden + norm_back(grad_normed1, hat_first, inv_first, gains[0])
    grad_source = grad_source.astype(bf16).reshape(line, part_rows, width)

    by_device = [
        jnp.transpose(
            jnp.stack(pair).reshape(2, groups, line, own_width), (2, 1, 0, 3)
        ).reshape(line, groups, -1)
        for pair in (
            (grad_gain1, grad_gain2),
            (grad_shift1, grad_shift2),
            (grad_scale1, grad_scale2),
            (grad_bias1, grad_bias2),
        )
    ]
    by_device.append(
        jnp.transpose(
            jnp.stack([grad_bq, grad_bv]).reshape(2, line, bq_cols, groups, bq_rows), (1, 3, 0, 4, 2)
        ).reshape(line, groups, -1)
    )
    by_device.append(
        jnp.transpose(grad_bfc1.reshape(line, f_cols, groups, f_rows), (0, 2, 3, 1)).reshape(
            line, groups, -1
        )
    )
    by_device = jnp.concatenate(by_device, axis=2)
    short = small.shape[2] - by_device.shape[2]
    by_device = jnp.pad(by_device, ((0, 0), (0, 0), (0, short))).reshape(line, -1, LANES)
    grad_input, shard_weights, shard_small = leave(
        groups, line, images, grad_source, grad_weights, by_device
    )
    grad_input = grad_input.astype(f32)
    own = cols
    shard_wqkv = jnp.stack([shard_weights[:, n * own : (n + 1) * own] for n in range(3)])
    shard_wout = shard_weights[:, 3 * own :].T
    shard_fc = shard_fc.reshape(shard_fc.shape[0], -1, 2, tile)
    shard_fc1 = shard_fc[:, :, 0].reshape(w_fc1.shape)
    shard_fc2 = shard_fc[:, :, 1].reshape(w_fc1.shape).T
    shard_small = shard_small.reshape(-1)
    at = 0

    def give(shape):
        nonlocal at
        at += math.prod(shape)
        return shard_small[at - math.prod(shape) : at].reshape(shape)

    shard_gain, shard_shift, shard_scale, shard_bias = (give(ln_gain.shape) for _ in range(4))
    shard_bqv = give(b_qv.shape)
    shard_bfc1 = give(b_fc1.shape)
    return (
        block_out,
        grad_input,
        shard_wqkv,
        shard_bqv,
        shard_wout,
        shard_fc1,
        shard_bfc1,
        shard_fc2,
        shard_gain,
        shard_shift,
        shard_scale,
        shard_bias,
    )


def solution(mesh):
    rows = P("dp", "tensor", None)
    vector = P(None, ("dp", "tensor"))
    weights = (
        P(None, "dp", "tensor"),
        P(None, "dp", "tensor"),
        P("tensor", "dp"),
        P("dp", "tensor"),
        P("dp", "tensor"),
        P("tensor", "dp"),
    )
    return jax.shard_map(
        body,
        mesh=mesh,
        in_specs=(rows, rows, P("dp")) + weights + (vector,) * 4,
        out_specs=(rows, rows) + weights + (vector,) * 4,
        check_vma=False,
    )
```

```python
import functools
import math

import jax
import jax.numpy as jnp
from jax import lax
from jax.experimental import pallas as pl
from jax.experimental.pallas import tpu as pltpu
from jax.sharding import PartitionSpec as P

HD = 64
LANES = 128
LOG2E = math.log2(math.e)
NEG = -1e30
NT = (((1,), (1,)), ((), ()))
NN = (((1,), (0,)), ((), ()))
TN = (((0,), (0,)), ((), ()))
f32 = jnp.float32
bf16 = jnp.bfloat16


def round_up(n, m):
    return (n + m - 1) // m * m


def parts(x):
    hi = x.astype(bf16).astype(f32)
    rest = x - hi
    mid = rest.astype(bf16).astype(f32)
    return hi, mid, rest - mid


def keys_with_bias(keys, lane, row, length, own, spare):
    bias = jnp.where(row < length, 0.0, NEG)
    ones = jnp.where((lane >= spare) & (lane < spare + 3), 1.0, 0.0)
    return jnp.where(own, keys, jnp.where(lane == spare + 3, bias, ones)).astype(bf16)


MESH = pl.DeviceIdType.MESH
ANY = pl.BlockSpec(memory_space=pl.ANY)
DMA = pltpu.SemaphoreType.DMA


def flipped(g, mask):
    bit = 1
    while bit <= mask:
        if mask & bit:
            g = g + bit * (1 - 2 * ((g // bit) % 2))
        bit *= 2
    return g


class Place:
    def __init__(self, groups, line):
        self.groups, self.line = groups, line
        self.g, self.z = lax.axis_index("dp"), lax.axis_index("tensor")
        self.masks = list(range(0, groups, 2))
        self.square = groups == 8
        self.direct = [2, 4] if self.square else self.masks[1:]

    def image(self, z):
        odd = self.g % 2
        return z + odd * (self.line - 1 - 2 * z)

    def up(self, k):
        return lax.rem(self.z + k, self.line)

    def down(self, k):
        return lax.rem(self.z + self.line - k, self.line)

    def barrier(self):
        semaphore = pltpu.get_barrier_semaphore()
        peers = [(self.g, self.up(s)) for s in range(1, self.line)]
        peers += [(flipped(self.g, m), self.z) for m in self.direct + [1]]
        for peer in peers:
            pl.semaphore_signal(semaphore, inc=1, device_id=peer, device_id_type=MESH)
        pl.semaphore_wait(semaphore, len(peers))


def remote(src, dst, send, recv, device):
    return pltpu.make_async_remote_copy(
        src_ref=src, dst_ref=dst, send_sem=send, recv_sem=recv, device_id=device, device_id_type=MESH
    )


class Gather:
    @staticmethod
    def sems(groups, line):
        chips = groups // 2
        return [
            DMA((line,)),
            DMA((line,)),
            DMA((chips, line)),
            DMA((chips, line)),
            DMA((chips, line)),
            DMA((chips, line)),
        ]

    def __init__(self, at, shard, full, sems):
        self.at, self.shard, self.full = at, shard, full
        self.zs, self.zr, self.ds, self.dr, self.cs, self.cr = sems
        self.rows = shard.shape[0]

    def piece(self, mask, k):
        at = self.at
        rows = pl.ds(pl.multiple_of(flipped(at.g, mask) * self.rows, 8), self.rows)
        return self.full.at[at.down(k), rows, :]

    def own(self, k):
        return self.shard if k == 0 else self.piece(0, k)

    def local(self):
        return pltpu.make_async_copy(self.shard, self.piece(0, 0), self.zs.at[0])

    def along(self, k, arriving=False):
        dst = self.piece(0, k if arriving else 0)
        src = dst if arriving else self.shard
        return remote(src, dst, self.zs.at[k], self.zr.at[k], (self.at.g, self.at.up(k)))

    def across(self, mask, k, arriving=False):
        at = self.at
        if at.square and mask == 6:
            via, peer = (2, 4) if k < at.line // 2 else (4, 2)
            src = dst = self.piece(via, k)
        else:
            peer = mask
            src, dst = self.own(k), self.piece(0, k)
        if arriving:
            src = dst = self.piece(mask, k)
        return remote(
            src, dst, self.ds.at[mask // 2, k], self.dr.at[mask // 2, k], (flipped(at.g, peer), at.z)
        )

    def core(self, mask, k, arriving=False):
        at = self.at
        if arriving:
            dst = self.piece(mask ^ 1, k)
            src = dst
        else:
            dst = self.piece(mask, k)
            src = self.own(k) if mask == 0 else dst
        return remote(src, dst, self.cs.at[mask // 2, k], self.cr.at[mask // 2, k], (flipped(at.g, 1), at.z))

    def start(self):
        self.local().start()
        for k in range(1, self.at.line):
            self.along(k).start()
        self.spread(0)

    def spread(self, k):
        if k:
            self.along(k, True).wait_recv()
        for mask in self.at.direct:
            self.across(mask, k).start()
        self.core(0, k).start()

    def passing(self, k):
        at = self.at
        for mask in at.direct:
            self.across(mask, k, True).wait_recv()
            if at.square and mask == (2 if k < at.line // 2 else 4):
                self.across(6, k).start()
            self.core(mask, k).start()

    def last(self, k):
        if self.at.square:
            self.across(6, k, True).wait_recv()
            self.core(6, k).start()

    def finish(self):
        at = self.at
        for k in range(at.line):
            for mask in at.masks:
                self.core(mask, k, True).wait_recv()
                self.core(mask, k).wait_send()
                if mask:
                    self.across(mask, k).wait_send()
            if k:
                self.along(k).wait_send()
        self.local().wait()

    def steps(self):
        line = self.at.line
        out = [self.start]
        for k in range(1, line):
            out.append(functools.partial(self.spread, k))
        for k in range(line):
            out.append(functools.partial(self.passing, k))
        for k in range(line):
            out.append(functools.partial(self.last, k))
        out.append(self.finish)
        return out


class ToOwner:
    @staticmethod
    def sems(groups, line):
        return [DMA((line,)), DMA((line,))]

    def __init__(self, at, rows, image, sems):
        self.at, self.rows, self.image = at, rows, image
        self.send, self.recv = sems
        self.count = rows.shape[0]

    def local(self):
        at = self.at
        return pltpu.make_async_copy(
            self.rows.at[jnp.minimum(at.image(at.z), self.count - 1)], self.image.at[at.z], self.send.at[0]
        )

    def copy(self, k, arriving=False):
        at = self.at
        to = at.up(k)
        src = self.rows.at[jnp.minimum(at.image(to), self.count - 1)]
        dst = self.image.at[at.down(k) if arriving else at.z]
        return remote(src, dst, self.send.at[k], self.recv.at[k], (at.g, to))

    def start(self):
        at = self.at
        self.local().start()
        for k in range(1, at.line):
            pl.when(at.image(at.up(k)) < self.count)(self.copy(k).start)

    def finish(self):
        at = self.at
        for k in range(1, at.line):
            pl.when(at.image(at.up(k)) < self.count)(self.copy(k).wait_send)
            pl.when(at.image(at.z) < self.count)(self.copy(k, True).wait_recv)
        self.local().wait()


class FromOwner:
    sems = ToOwner.sems

    def __init__(self, at, image, rows, sems):
        self.at, self.rows, self.image = at, rows, image
        self.send, self.recv = sems
        self.count = rows.shape[0]

    def local(self):
        at = self.at
        return pltpu.make_async_copy(
            self.image.at[at.z], self.rows.at[jnp.minimum(at.image(at.z), self.count - 1)], self.send.at[0]
        )

    def copy(self, k, arriving=False):
        at = self.at
        owner = at.down(k) if arriving else at.z
        dst = self.rows.at[jnp.minimum(at.image(owner), self.count - 1)]
        return remote(self.image.at[at.up(k)], dst, self.send.at[k], self.recv.at[k], (at.g, at.up(k)))

    def start(self):
        at = self.at

        @pl.when(at.image(at.z) < self.count)
        def _():
            self.local().start()
            for k in range(1, at.line):
                self.copy(k).start()

    def finish(self):
        at = self.at

        @pl.when(at.image(at.z) < self.count)
        def _():
            for k in range(1, at.line):
                self.copy(k).wait_send()
            self.local().wait()

        for k in range(1, at.line):
            pl.when(at.image(at.down(k)) < self.count)(self.copy(k, True).wait_recv)


class Reduce:
    @staticmethod
    def scratch(groups, line, r, c, dtype):
        chips = groups // 2
        return [
            pltpu.VMEM((chips, line, r, c), dtype),
            pltpu.VMEM((chips, line, r, c), dtype),
            pltpu.VMEM((chips - 1, line, r, c), dtype),
            pltpu.VMEM((line, r, c), dtype),
            DMA((chips, line)),
            DMA((chips, line)),
            DMA((chips, line)),
            DMA((chips, line)),
            DMA((chips, line)),
            DMA((line,)),
            DMA((line,)),
        ]

    def __init__(self, at, full, scratch, rows):
        self.at, self.full, self.rows = at, full, rows
        self.cbuf, self.sums, self.dbuf, self.zbuf = scratch[:4]
        self.ls, self.cs, self.cr, self.ds, self.dr, self.zs, self.zr = scratch[4:]
        self.order = [6, 2, 4, 0] if at.square else at.masks[1:] + [0]

    def piece(self, mask, k):
        at = self.at
        rows = pl.ds(pl.multiple_of(flipped(at.g, mask) * self.rows, 8), self.rows)
        return self.full.at[at.down(k), rows, :]

    def local(self, mask, k):
        return pltpu.make_async_copy(
            self.piece(mask, k), self.sums.at[mask // 2, k], self.ls.at[mask // 2, k]
        )

    def core(self, mask, k):
        at, m = self.at, mask // 2
        return remote(
            self.piece(mask ^ 1, k), self.cbuf.at[m, k], self.cs.at[m, k], self.cr.at[m, k],
            (flipped(at.g, 1), at.z),
        )

    def across(self, mask, k):
        at, m = self.at, mask // 2
        peer = mask
        if at.square and mask == 6:
            peer = 4 if k < at.line // 2 else 2
        return remote(
            self.sums.at[m, k], self.dbuf.at[m - 1, k], self.ds.at[m, k], self.dr.at[m, k],
            (flipped(at.g, peer), at.z),
        )

    def along(self, k):
        at = self.at
        return remote(
            self.sums.at[0, k], self.zbuf.at[k], self.zs.at[k], self.zr.at[k], (at.g, at.down(k))
        )

    def start(self):
        for mask in self.order:
            for k in range(self.at.line):
                self.core(mask, k).start()
                self.local(mask, k).start()

    def add(self, m, k, other):
        total = self.sums[m, k].astype(f32) + other.astype(f32)
        self.sums[m, k] = total.astype(self.sums.dtype)

    def pair(self, mask, k):
        self.local(mask, k).wait()
        self.core(mask, k).wait_recv()
        self.add(mask // 2, k, self.cbuf[mask // 2, k])

    def pairs(self, mask):
        at = self.at
        for k in range(at.line):
            self.pair(mask, k)
            waits = at.square and mask == (2 if k < at.line // 2 else 4)
            if mask and not waits:
                self.across(mask, k).start()

    def joined(self, k):
        at = self.at
        if at.square:
            mask = 2 if k < at.line // 2 else 4
            self.across(6, k).wait_recv()
            self.add(mask // 2, k, self.dbuf[2, k])
            self.across(mask, k).start()

    def own(self, k):
        for mask in self.at.direct:
            self.across(mask, k).wait_recv()
            self.add(0, k, self.dbuf[mask // 2 - 1, k])
        if k:
            self.along(k).start()

    def finish(self):
        at = self.at
        for k in range(at.line):
            for mask in at.masks:
                self.core(mask, k).wait_send()
                if mask:
                    self.across(mask, k).wait_send()
            if k:
                self.along(k).wait_send()
                self.along(k).wait_recv()
        total = self.sums[0, 0].astype(f32)
        for k in range(1, at.line):
            total += self.zbuf[k].astype(f32)
        return total

    def steps(self):
        ks = range(self.at.line)
        out = [self.start]
        out += [functools.partial(self.pairs, mask) for mask in self.order]
        out += [functools.partial(self.joined, k) for k in ks]
        return out + [functools.partial(self.own, k) for k in ks]


def run_ticks(ticks, step, half):
    for at, work in ticks:
        if at % 2 == half:
            pl.when(step == at // 2)(work)


def arrive_kernel(groups, line, x_ref, shard_ref, small_ref, xo_ref, full_ref, smalls_ref, *sems):
    at = Place(groups, line)
    n = len(Gather.sems(groups, line))
    rows = ToOwner(at, x_ref, xo_ref, sems[2 * n :])
    weights = Gather(at, shard_ref, full_ref, sems[:n])
    small = Gather(at, small_ref, smalls_ref, sems[n : 2 * n])
    at.barrier()
    for one, two in zip(small.steps(), weights.steps()):
        one()
        two()
        if one == small.start:
            rows.start()
    rows.finish()


def arrive(groups, line, x, shard, small):
    images, part_rows, width = x.shape
    return pl.pallas_call(
        functools.partial(arrive_kernel, groups, line),
        in_specs=[ANY] * 3,
        out_specs=[ANY] * 3,
        out_shape=[
            jax.ShapeDtypeStruct((line, part_rows, width), x.dtype),
            jax.ShapeDtypeStruct((line, groups * shard.shape[0], shard.shape[1]), shard.dtype),
            jax.ShapeDtypeStruct((line, groups * small.shape[0], small.shape[1]), small.dtype),
        ],
        scratch_shapes=Gather.sems(groups, line) * 2 + ToOwner.sems(groups, line),
        compiler_params=pltpu.CompilerParams(collective_id=1, has_side_effects=True),
        name="arrive",
    )(x, shard, small)


def leave_kernel(
    groups, line, gq_ref, gk_ref, gv_ref, w_ref, n1t_ref, x_ref, gh_ref, v_ref, smalls_ref,
    yo_ref, shard_ref, small_ref, gn, y, full, smalls, *scratch
):
    at = Place(groups, line)
    n = len(ToOwner.sems(groups, line))
    m = (len(scratch) - n) // 2
    rows = FromOwner(at, y, yo_ref, scratch[:n])
    weights = Reduce(at, full, scratch[n : n + m], shard_ref.shape[0])
    small = Reduce(at, smalls, scratch[n + m :], small_ref.shape[0])
    step = pl.program_id(0)
    cols = gq_ref.shape[1]
    grads = (gq_ref, gk_ref, gv_ref)

    @pl.when(step == 0)
    def _():
        at.barrier()
        smalls[...] = smalls_ref[...]
        gn[...] = jnp.zeros_like(gn)

    @pl.when(step < line)
    def _():
        for i, ref in enumerate(grads):
            gn[...] += lax.dot_general(
                ref[...], w_ref[0, :, i * cols : (i + 1) * cols], NT, preferred_element_type=f32
            )

    @pl.when(step == line - 1)
    def _():
        part = x_ref.shape[1]

        def piece(p, carry):
            gain, shift = carry
            hat, inverse = norm_stats(x_ref[p].astype(f32))
            g = gn[p * part : (p + 1) * part]
            y[p] = (gh_ref[p] + norm_back(g, hat, inverse, v_ref[0:1])).astype(bf16)
            gain += jnp.sum(g * hat, axis=0, keepdims=True)
            return gain, shift + jnp.sum(g, axis=0, keepdims=True)

        zero = jnp.zeros((1, gn.shape[1]), f32)
        carry = (zero, zero)
        for p in range(line):
            carry = piece(p, carry)
        rows.start()
        wide = gn.shape[1] // groups
        for j, total in enumerate(carry):
            for g in range(groups):
                row = total[:, g * wide : (g + 1) * wide]
                if wide < LANES:
                    row = jnp.concatenate([row, jnp.zeros((1, LANES - wide), f32)], axis=1)
                at_row = g * small_ref.shape[0] + 2 * j
                for t in range(line):
                    smalls[t, at_row : at_row + 1, :] = row
        small.start()

    for t in range(line):

        @pl.when(step == line + t)
        def _(t=t):
            for i, ref in enumerate(grads):
                full[t, :, i * cols : (i + 1) * cols] = lax.dot_general(
                    n1t_ref[...], ref[...], NN, preferred_element_type=f32
                ).astype(bf16)

    @pl.when(step == 2 * line - 1)
    def _():
        for one, two in zip(weights.steps(), small.steps()):
            one()
            if two != small.start:
                two()
        shard_ref[...] = weights.finish()
        small_ref[...] = small.finish()
        rows.finish()


def leave(groups, line, images, gq, gk, gv, weights, n1t, x, ghid, vectors, smalls):
    _, part, width = x.shape
    rows = line * part
    cols = width // line
    r, c = width // groups, 3 * cols
    sr, sc = smalls.shape[1] // groups, smalls.shape[2]
    grad = pl.BlockSpec((rows, cols), lambda j: (0, j % line))
    return pl.pallas_call(
        functools.partial(leave_kernel, groups, line),
        grid=(2 * line,),
        in_specs=[
            grad,
            grad,
            grad,
            pl.BlockSpec((1, width, c), lambda j: (jnp.minimum(j, line - 1), 0, 0)),
            whole(width, rows),
            whole(line, part, width),
            whole(line, part, width),
            whole(*vectors.shape),
            whole(*smalls.shape),
        ],
        out_specs=[ANY, whole(r, c), whole(sr, sc)],
        out_shape=[
            jax.ShapeDtypeStruct((images, part, width), bf16),
            jax.ShapeDtypeStruct((r, c), f32),
            jax.ShapeDtypeStruct((sr, sc), f32),
        ],
        scratch_shapes=[
            pltpu.VMEM((rows, width), f32),
            pltpu.VMEM((line, part, width), bf16),
            pltpu.VMEM((line, width, c), bf16),
            pltpu.VMEM(smalls.shape, f32),
        ]
        + ToOwner.sems(groups, line)
        + Reduce.scratch(groups, line, r, c, bf16)
        + Reduce.scratch(groups, line, sr, sc, f32),
        compiler_params=pltpu.CompilerParams(
            collective_id=2, has_side_effects=True, vmem_limit_bytes=62 * 2**20
        ),
        name="leave",
    )(gq, gk, gv, weights, n1t, x, ghid, vectors, smalls)


def norm_stats(values):
    center = values - jnp.mean(values, axis=-1, keepdims=True)
    inverse = lax.rsqrt(jnp.mean(center * center, axis=-1, keepdims=True) + 1e-06)
    return center * inverse, inverse


def norm_back(grad_norm, normed, inverse, gain):
    scaled = grad_norm * gain
    return inverse * (
        scaled
        - jnp.mean(scaled, axis=-1, keepdims=True)
        - normed * jnp.mean(scaled * normed, axis=-1, keepdims=True)
    )


def project_kernel(flag_ref, x_ref, v_ref, w_ref, b_ref, out_ref, xc_ref, n1t_ref, n1):
    @pl.when((pl.program_id(0) == 0) & (pl.program_id(1) == 0))
    def _():
        rows = x_ref.shape[0]
        size = 32 if rows % 32 == 0 else 16

        def chunk(i, carry):
            r = pl.ds(pl.multiple_of(i * size, 16), size)
            x = jnp.where(flag_ref[1] > 0, x_ref[r, :].astype(f32), 0.0)
            xc_ref[r, :] = x.astype(bf16)
            hat, _ = norm_stats(x)
            n1[r, :] = (hat * v_ref[0:1] + v_ref[2:3]).astype(bf16)
            return carry

        lax.fori_loop(0, rows // size, chunk, 0)
        n1t_ref[...] = n1[...].T

    scale = jnp.where(pl.program_id(1) == 0, HD ** (-0.5) * LOG2E, 1.0)
    out = lax.dot_general(n1[...], w_ref[0], NN, preferred_element_type=f32) + b_ref[0]
    out_ref[0] = (out * scale).astype(bf16)


def whole(*shape):
    return pl.BlockSpec(shape, lambda *_: (0,) * len(shape), pipeline_mode=pl.Buffered(1))


SMEM = pl.BlockSpec(memory_space=pltpu.SMEM)


def project(flags, x, vectors, weights, bias):
    rows, width = x.shape
    line = weights.shape[0]
    cols = width // line
    return pl.pallas_call(
        project_kernel,
        grid=(line, 3),
        in_specs=[
            SMEM,
            whole(rows, width),
            whole(*vectors.shape),
            pl.BlockSpec((1, width, cols), lambda t, k: (t, 0, k)),
            pl.BlockSpec((1, 1, cols), lambda t, k: (k, 0, t)),
        ],
        out_specs=[
            pl.BlockSpec((1, rows, cols), lambda t, k: (k, 0, t)),
            whole(rows, width),
            whole(width, rows),
        ],
        out_shape=[
            jax.ShapeDtypeStruct((3, rows, width), bf16),
            jax.ShapeDtypeStruct((rows, width), bf16),
            jax.ShapeDtypeStruct((width, rows), bf16),
        ],
        scratch_shapes=[pltpu.VMEM((rows, width), bf16)],
        compiler_params=pltpu.CompilerParams(vmem_limit_bytes=40 * 2**20),
        cost_estimate=pl.CostEstimate(
            flops=6 * rows * width * width, bytes_accessed=16 * rows * width, transcendentals=0
        ),
        name="project",
    )(flags, x, vectors, weights, bias)


def valid_rows(flag_ref, shape):
    row = pl.program_id(0) * shape[0] + lax.broadcasted_iota(jnp.int32, shape, 0)
    return row < flag_ref[0]


def middle_kernel(flag_ref, ctx_ref, x_ref, cot_ref, v_ref, w_ref, hid_ref, n2_ref, gm_ref):
    line, _, cols = w_ref.shape
    attn = v_ref[6:7]
    for t in range(line):
        part = ctx_ref[0, :, t * cols : (t + 1) * cols]
        attn = attn + lax.dot_general(part, w_ref[t], NT, preferred_element_type=f32)
    hidden = x_ref[0].astype(f32) + v_ref[4:5] * attn
    hid_ref[0] = hidden
    hat, _ = norm_stats(hidden)
    n2_ref[0] = (hat * v_ref[1:2] + v_ref[3:4]).astype(bf16)
    gout = jnp.where(valid_rows(flag_ref, hidden.shape), cot_ref[0].astype(f32), 0.0)
    gm_ref[0] = (gout * v_ref[5:6]).astype(bf16)


def middle(flags, context, x, cot, vectors, weights):
    line, part, width = x.shape
    cols = width // line
    piece = pl.BlockSpec((1, part, width), lambda p: (p, 0, 0))
    return pl.pallas_call(
        middle_kernel,
        grid=(line,),
        in_specs=[
            SMEM,
            piece,
            piece,
            piece,
            whole(*vectors.shape),
            pl.BlockSpec(
                (line, width, cols), lambda p: (0, 0, 3), pipeline_mode=pl.Buffered(1)
            ),
        ],
        out_specs=[piece] * 3,
        out_shape=[
            jax.ShapeDtypeStruct(x.shape, f32),
            jax.ShapeDtypeStruct(x.shape, bf16),
            jax.ShapeDtypeStruct(x.shape, bf16),
        ],
        compiler_params=pltpu.CompilerParams(vmem_limit_bytes=40 * 2**20),
        name="middle",
    )(flags, context, x, cot, vectors, weights)


def turn_kernel(
    flag_ref, mlp_ref, gn_ref, hid_ref, x_ref, cot_ref, ctx_ref, v_ref, w_ref,
    out_ref, gh_ref, gc_ref, gw_ref, sum_ref, acc
):
    step = pl.program_id(0)
    line, _, cols = w_ref.shape
    hidden = hid_ref[0]
    mlp = mlp_ref[0] + v_ref[7:8]
    gn = gn_ref[0]
    valid = valid_rows(flag_ref, hidden.shape)
    out_ref[0] = jnp.where(valid, hidden + v_ref[5:6] * mlp, 0.0).astype(bf16)
    gout = jnp.where(valid, cot_ref[0].astype(f32), 0.0)
    hat, inverse = norm_stats(hidden)
    ghid = gout + norm_back(gn, hat, inverse, v_ref[1:2])
    gh_ref[0] = ghid
    gattn = ghid * v_ref[4:5]
    attn = (hidden - x_ref[0].astype(f32)) / v_ref[4:5]

    def total(x):
        return jnp.sum(x, axis=0, keepdims=True)

    sums = [gn * hat, gn, ghid * attn, gout * mlp, gattn, gout * v_ref[5:6]]
    sums = jnp.concatenate([total(x) for x in sums] + [jnp.zeros((2, gn.shape[1]), f32)], axis=0)

    @pl.when(step == 0)
    def _():
        sum_ref[...] = sums
        acc[...] = jnp.zeros_like(acc)

    @pl.when(step > 0)
    def _():
        sum_ref[...] += sums

    gattn = gattn.astype(bf16)
    for t in range(line):
        part = ctx_ref[0, :, t * cols : (t + 1) * cols]
        gc_ref[0, :, t * cols : (t + 1) * cols] = lax.dot_general(
            gattn, w_ref[t], NN, preferred_element_type=f32
        ).astype(bf16)
        acc[t] += lax.dot_general(gattn, part, TN, preferred_element_type=f32)

    @pl.when(step == line - 1)
    def _():
        gw_ref[...] = acc[...].astype(bf16)


def turn(flags, mlp, gn, hidden, x, cot, context, vectors, weights):
    line, part, width = x.shape
    cols = width // line
    piece = pl.BlockSpec((1, part, width), lambda p: (p, 0, 0))
    return pl.pallas_call(
        turn_kernel,
        grid=(line,),
        in_specs=[SMEM]
        + [piece] * 6
        + [
            whole(*vectors.shape),
            pl.BlockSpec(
                (line, width, cols), lambda p: (0, 0, 3), pipeline_mode=pl.Buffered(1)
            ),
        ],
        out_specs=[piece] * 3 + [whole(line, width, cols), whole(8, width)],
        out_shape=[
            jax.ShapeDtypeStruct(x.shape, bf16),
            jax.ShapeDtypeStruct(x.shape, f32),
            jax.ShapeDtypeStruct(x.shape, bf16),
            jax.ShapeDtypeStruct((line, width, cols), bf16),
            jax.ShapeDtypeStruct((8, width), f32),
        ],
        scratch_shapes=[pltpu.VMEM((line, width, cols), f32)],
        compiler_params=pltpu.CompilerParams(vmem_limit_bytes=56 * 2**20),
        name="turn",
    )(flags, mlp, gn, hidden, x, cot, context, vectors, weights)


def attend_forward_kernel(
    groups, line, rows, padded, len_ref, q_ref, k_ref, v_ref, shard_ref, cot_ref,
    ctx_ref, qa_ref, full_ref, coto_ref, ka, va, *sems
):
    at = Place(groups, line)
    n = len(Gather.sems(groups, line))
    weights = Gather(at, shard_ref, full_ref, sems[:n])
    cot = ToOwner(at, cot_ref, coto_ref, sems[n:])
    steps = weights.steps()
    halves = 2 * pl.num_programs(0)
    first, spreads, passes, rest = steps[0], steps[1:line], steps[line : 2 * line], steps[2 * line :]

    def begin():
        at.barrier()
        first()

    ticks = [(0, begin), (6, cot.start)]
    for k in range(1, line):
        ticks.append((min(4 * k, 15), spreads[k - 1]))
    for k in range(line):
        ticks.append((min(4 * k + 4, 15), passes[k]))
    step = pl.program_id(0)
    length = len_ref[0]
    lane = lax.broadcasted_iota(jnp.int32, (padded, LANES), 1)
    row = lax.broadcasted_iota(jnp.int32, (padded, LANES), 0)
    lb = lane[:rows]
    if padded > rows:
        va[rows:] = jnp.zeros((padded - rows, LANES), bf16)
    for half in range(2):
        run_ticks(ticks, step, half)
        own = (lb < HD) if half == 0 else (lb >= HD)
        spare = HD if half == 0 else 0
        ka[:rows] = keys_with_bias(k_ref[...].astype(f32), lb, row[:rows], length, own, spare)
        if padded > rows:
            ka[rows:] = jnp.where(lane[rows:] == spare + 3, NEG, 0.0).astype(bf16)
        va[:rows] = jnp.where(
            own, v_ref[...].astype(f32), jnp.where(lb == spare, 1.0, 0.0)
        ).astype(bf16)
        qa = jnp.where(own, q_ref[...].astype(f32), jnp.where(lb == spare + 3, 1.0, 0.0))
        s = lax.dot_general(qa.astype(bf16), ka[...], NT, preferred_element_type=f32)
        m = jnp.max(s, axis=1, keepdims=True)
        p = jnp.exp2(s - m).astype(bf16)
        o = lax.dot_general(p, va[...], NN, preferred_element_type=f32)
        total = o[:, spare : spare + 1]
        o = o / total
        hi, mid, lo = parts(-(m + jnp.log2(total)))
        if half == 0:
            ctx_ref[...] = o.astype(bf16)
        else:
            ctx_ref[...] = jnp.where(own, o, ctx_ref[...].astype(f32)).astype(bf16)
        stats = jnp.where(lb == spare + 2, lo, qa)
        stats = jnp.where(lb == spare + 1, mid, stats)
        qa_ref[half] = jnp.where(lb == spare, hi, stats).astype(bf16)

    @pl.when(step == pl.num_programs(0) - 1)
    def _():
        for work in rest:
            work()
        cot.finish()


def attend_forward(groups, line, length, qkv, shard, cot):
    _, rows, width = qkv.shape
    padded = round_up(rows, LANES)
    spec = pl.BlockSpec((rows, LANES), lambda j: (0, j))

    def third(n):
        return pl.BlockSpec((None, rows, LANES), lambda j: (n, 0, j))

    return pl.pallas_call(
        functools.partial(attend_forward_kernel, groups, line, rows, padded),
        grid=(width // LANES,),
        in_specs=[pl.BlockSpec(memory_space=pltpu.SMEM), third(0), third(1), third(2), ANY, ANY],
        out_specs=[spec, pl.BlockSpec((2, rows, LANES), lambda j: (j, 0, 0)), ANY, ANY],
        out_shape=[
            jax.ShapeDtypeStruct((rows, width), bf16),
            jax.ShapeDtypeStruct((width // HD, rows, LANES), bf16),
            jax.ShapeDtypeStruct((line, groups * shard.shape[0], shard.shape[1]), shard.dtype),
            jax.ShapeDtypeStruct((line,) + cot.shape[1:], cot.dtype),
        ],
        scratch_shapes=[pltpu.VMEM((padded, LANES), bf16), pltpu.VMEM((padded, LANES), bf16)]
        + Gather.sems(groups, line)
        + ToOwner.sems(groups, line),
        compiler_params=pltpu.CompilerParams(
            collective_id=3, has_side_effects=True, vmem_limit_bytes=56 * 2**20
        ),
        cost_estimate=pl.CostEstimate(
            flops=16 * rows * rows * width,
            bytes_accessed=12 * rows * width,
            transcendentals=rows * rows * width // HD,
        ),
        name="attend_forward",
    )(length, qkv, qkv, qkv, shard, cot)


def attend_backward_kernel(
    groups, line, rows, padded, blocks, len_ref, qa_ref, k_ref, v_ref, gc_ref, ctx_ref, y_ref, full_ref,
    out_ref, gq_ref, gk_ref, gv_ref, gb_ref, yo_ref, shard_ref, oshard_ref, ka, va, qs, ga, acc, *scratch
):
    at = Place(groups, line)
    n = len(ToOwner.sems(groups, line))
    back = FromOwner(at, y_ref, yo_ref, scratch[:n])
    m = (len(scratch) - n) // 2
    weights = Reduce(at, full_ref, scratch[n : n + m], shard_ref.shape[0])
    out_weights = Reduce(at, out_ref, scratch[n + m :], oshard_ref.shape[0])
    pairs = list(zip(weights.steps(), out_weights.steps()))
    chips = groups // 2

    def both(i):
        def run():
            for work in pairs[i]:
                work()

        return run

    steps = [both(i) for i in range(len(pairs))]

    def begin():
        at.barrier()
        steps[0]()
        back.start()

    ticks = [(0, begin)]
    for i in range(chips):
        ticks.append((min(i + 1, 4), steps[1 + i]))
    for k in range(line):
        ticks.append((min(6 + k // 2, 15), steps[1 + chips + k]))
    for k in range(line):
        ticks.append((12, steps[1 + chips + line + k]))
    step = pl.program_id(0)
    length = len_ref[0]
    lane = lax.broadcasted_iota(jnp.int32, (padded, LANES), 1)
    row = lax.broadcasted_iota(jnp.int32, (padded, LANES), 0)
    size = rows // blocks
    ls = lane[:rows]
    for half in range(2):
        run_ticks(ticks, step, half)
        own = (ls < HD) if half == 0 else (ls >= HD)
        spare = HD if half == 0 else 0
        ownb = own[:size]
        gc = gc_ref[...].astype(f32)
        corr = jnp.sum(
            jnp.where(own, gc * ctx_ref[...].astype(f32), 0.0), axis=1, keepdims=True
        )
        hi, mid, lo = parts(-corr)
        extra = jnp.where(ls == spare + 1, mid, jnp.where(ls == spare + 2, lo, 0.0))
        ga[:rows] = jnp.where(own, gc, jnp.where(ls == spare, hi, extra)).astype(bf16)
        qs[:rows] = qa_ref[half]
        if padded > rows:
            ga[rows:] = jnp.zeros((padded - rows, LANES), bf16)
            qs[rows:] = jnp.where(lane[rows:] == spare, NEG, 0.0).astype(bf16)
        ka[...] = keys_with_bias(k_ref[...].astype(f32), ls, row[:rows], length, own, spare)
        ones = jnp.where((ls >= spare) & (ls < spare + 3), 1.0, 0.0)
        va[...] = jnp.where(own, v_ref[...].astype(f32), ones).astype(bf16)
        acc[...] = jnp.zeros_like(acc)

        def block(b, carry):
            r = pl.ds(pl.multiple_of(b * size, 16), size)
            kb = ka[r, :]
            p = jnp.exp2(lax.dot_general(kb, qs[...], NT, preferred_element_type=f32))
            gp = lax.dot_general(va[r, :], ga[...], NT, preferred_element_type=f32)
            ds = (p * gp).astype(bf16)
            gv = lax.dot_general(p.astype(bf16), ga[...], NN, preferred_element_type=f32)
            gk = lax.dot_general(ds, qs[...], NN, preferred_element_type=f32) * (1.0 / LOG2E)
            acc[...] += lax.dot_general(kb.T, ds, NN, preferred_element_type=f32)
            bv = carry + jnp.sum(gv, axis=0, keepdims=True)
            if half == 0:
                gv_ref[r, :] = gv.astype(bf16)
                gk_ref[r, :] = gk.astype(bf16)
            else:
                gv_ref[r, :] = jnp.where(ownb, gv, gv_ref[r, :].astype(f32)).astype(bf16)
                gk_ref[r, :] = jnp.where(ownb, gk, gk_ref[r, :].astype(f32)).astype(bf16)
            return bv

        bv = lax.fori_loop(0, blocks, block, jnp.zeros((1, LANES), f32))
        gq = acc[...].T[:rows] * HD ** (-0.5)
        sums = jnp.concatenate(
            [jnp.sum(gq, axis=0, keepdims=True), bv, jnp.zeros((6, LANES), f32)], axis=0
        )
        if half == 0:
            gb_ref[0] = sums
        else:
            gb_ref[0] = jnp.where(own[:8], sums, gb_ref[0])
        if half == 0:
            gq_ref[...] = gq.astype(bf16)
        else:
            gq_ref[...] = jnp.where(own, gq, gq_ref[...].astype(f32)).astype(bf16)

    @pl.when(step == pl.num_programs(0) - 1)
    def _():
        shard_ref[...] = weights.finish()
        oshard_ref[...] = out_weights.finish()
        back.finish()


def attend_backward(groups, line, images, length, qa, qkv, gc, ctx, y, full, out_full):
    _, rows, width = qkv.shape
    padded = round_up(rows, LANES)
    blocks = 2 if rows % 32 == 0 else 1
    spec = pl.BlockSpec((rows, LANES), lambda j: (0, j))
    r, c, oc = full.shape[1] // groups, full.shape[2], out_full.shape[2]

    def third(n):
        return pl.BlockSpec((None, rows, LANES), lambda j: (n, 0, j))

    return pl.pallas_call(
        functools.partial(attend_backward_kernel, groups, line, rows, padded, blocks),
        grid=(width // LANES,),
        in_specs=[
            pl.BlockSpec(memory_space=pltpu.SMEM),
            pl.BlockSpec((2, rows, LANES), lambda j: (j, 0, 0)),
            third(1),
            third(2),
            spec,
            spec,
            ANY,
            ANY,
            ANY,
        ],
        out_specs=[spec] * 3
        + [pl.BlockSpec((1, 8, LANES), lambda j: (j, 0, 0)), ANY, whole(r, c), whole(r, oc)],
        out_shape=[jax.ShapeDtypeStruct((rows, width), bf16)] * 3
        + [
            jax.ShapeDtypeStruct((width // LANES, 8, LANES), f32),
            jax.ShapeDtypeStruct((images,) + y.shape[1:], y.dtype),
            jax.ShapeDtypeStruct((r, c), f32),
            jax.ShapeDtypeStruct((r, oc), f32),
        ],
        scratch_shapes=[
            pltpu.VMEM((rows, LANES), bf16),
            pltpu.VMEM((rows, LANES), bf16),
            pltpu.VMEM((padded, LANES), bf16),
            pltpu.VMEM((padded, LANES), bf16),
            pltpu.VMEM((LANES, padded), f32),
        ]
        + ToOwner.sems(groups, line)
        + Reduce.scratch(groups, line, r, c, full.dtype)
        + Reduce.scratch(groups, line, r, oc, full.dtype),
        compiler_params=pltpu.CompilerParams(
            collective_id=4, has_side_effects=True, vmem_limit_bytes=62 * 2**20
        ),
        cost_estimate=pl.CostEstimate(
            flops=40 * rows * rows * width,
            bytes_accessed=16 * rows * width,
            transcendentals=rows * rows * width // HD,
        ),
        name="attend_backward",
    )(length, qa, qkv, qkv, gc, ctx, y, full, out_full)


def feed_forward_kernel(
    tile, n2_ref, gm_ref, w_ref, b1_ref, mlp_ref, gn_ref, gw_ref, gb_ref, n2t, gmt
):
    step = pl.program_id(0)

    @pl.when(step == 0)
    def _():
        n2t[...] = n2_ref[...].T
        gmt[...] = gm_ref[...].T

    w1 = w_ref[0, :, :tile]
    w2t = w_ref[0, :, tile:]
    pre = lax.dot_general(n2_ref[...], w1, NN, preferred_element_type=f32) + b1_ref[...]
    gact = lax.dot_general(gm_ref[...], w2t, NN, preferred_element_type=f32)
    cdf = 0.5 * (1.0 + lax.erf(pre * (1 / math.sqrt(2))))
    act = (pre * cdf).astype(bf16)
    pdf = jnp.exp2(pre * pre * (-0.5 * LOG2E)) * (1 / math.sqrt(2 * math.pi))
    gpre = gact * (cdf + pre * pdf)
    gb_ref[...] = jnp.sum(gpre, axis=0, keepdims=True)
    gpre = gpre.astype(bf16)
    mlp = lax.dot_general(act, w2t, NT, preferred_element_type=f32)
    gn = lax.dot_general(gpre, w1, NT, preferred_element_type=f32)

    @pl.when(step == 0)
    def _():
        mlp_ref[...] = mlp
        gn_ref[...] = gn

    @pl.when(step > 0)
    def _():
        mlp_ref[...] += mlp
        gn_ref[...] += gn

    gw_ref[0, :, :tile] = lax.dot_general(
        n2t[...], gpre, NN, preferred_element_type=f32
    ).astype(bf16)
    gw_ref[0, :, tile:] = lax.dot_general(
        gmt[...], act, NN, preferred_element_type=f32
    ).astype(bf16)


def feed_forward(n2, gm, weights, b1, tile):
    rows, width = n2.shape
    units = b1.shape[1]
    per = weights.shape[2] // (2 * tile)

    both = pl.BlockSpec((1, width, 2 * tile), lambda j: (j // per, 0, j % per))
    return pl.pallas_call(
        functools.partial(feed_forward_kernel, tile),
        grid=(units // tile,),
        in_specs=[
            whole(rows, width),
            whole(rows, width),
            both,
            pl.BlockSpec((1, tile), lambda j: (0, j)),
        ],
        out_specs=[
            whole(rows, width),
            whole(rows, width),
            both,
            pl.BlockSpec((1, tile), lambda j: (0, j)),
        ],
        out_shape=[
            jax.ShapeDtypeStruct((rows, width), f32),
            jax.ShapeDtypeStruct((rows, width), f32),
            jax.ShapeDtypeStruct(weights.shape, bf16),
            jax.ShapeDtypeStruct((1, units), f32),
        ],
        scratch_shapes=[pltpu.VMEM((width, rows), bf16), pltpu.VMEM((width, rows), bf16)],
        compiler_params=pltpu.CompilerParams(vmem_limit_bytes=60 * 2**20),
        cost_estimate=pl.CostEstimate(
            flops=16 * rows * width * units,
            bytes_accessed=8 * width * units,
            transcendentals=2 * rows * units,
        ),
        name="feed_forward",
    )(n2, gm, weights, b1)


def body(
    block_input,
    cotangent,
    lengths,
    w_qkv,
    b_qv,
    w_out,
    w_fc1,
    b_fc1,
    w_fc2,
    ln_gain,
    ln_shift,
    layer_scale,
    out_bias,
):
    images, part_rows, width = block_input.shape
    groups = lax.axis_size("dp")
    line = lax.axis_size("tensor")
    rows = part_rows * line
    group = lax.axis_index("dp")
    place = lax.axis_index("tensor")
    mine = place + (group % 2) * (line - 1 - 2 * place)
    active = mine < images

    tile = min(512, w_fc1.shape[1])
    qkv_out = jnp.concatenate([w_qkv[0], w_qkv[1], w_qkv[2], w_out.T], axis=1)
    tiles = (w_fc1.shape[0], -1, 1, tile)
    fc_both = jnp.concatenate([w_fc1.reshape(tiles), w_fc2.T.reshape(tiles)], axis=2).reshape(
        w_fc1.shape[0], -1
    )

    def lanes(x):
        return jnp.pad(x, ((0, 0), (0, LANES - x.shape[1])))

    own_width = ln_gain.shape[1]
    _, bq_rows, bq_cols = b_qv.shape
    f_rows, f_cols = b_fc1.shape
    small = [ln_gain, ln_shift, layer_scale, out_bias, b_qv.astype(f32).reshape(-1, bq_cols)]
    small = jnp.concatenate([lanes(x) for x in small + [b_fc1.astype(f32)]], axis=0)
    small_rows = round_up(small.shape[0], 8)
    small = jnp.pad(small, ((0, small_rows - small.shape[0]), (0, 0)))
    b_at = 8 + 2 * bq_rows

    x_all, weights, small = arrive(groups, line, block_input, qkv_out, small)
    small = small.reshape(line, groups, small_rows, LANES)
    vectors = jnp.transpose(small[:, :, :8, :own_width], (2, 1, 0, 3)).reshape(8, width)
    qv_bias = jnp.transpose(
        small[:, :, 8:b_at, :bq_cols].reshape(line, groups, 2, bq_rows, bq_cols), (2, 0, 4, 1, 3)
    ).reshape(2, 1, width)
    fc1_bias = jnp.transpose(
        small[:, :, b_at : b_at + f_rows, :f_cols], (0, 3, 1, 2)
    ).reshape(1, -1)

    length = jnp.where(active, lengths[jnp.minimum(mine, images - 1)], 0).astype(jnp.int32)
    flags = jnp.stack([length, active.astype(jnp.int32)])
    pieces = (line, part_rows, width)

    zero = jnp.zeros((1, 1, width), f32)
    qkv, x_all, normed1_t = project(
        flags,
        x_all.reshape(rows, width),
        vectors,
        weights,
        jnp.concatenate([qv_bias[:1], zero, qv_bias[1:]]),
    )
    x_all = x_all.reshape(pieces)
    context, query_stats, fc_weights, cot = attend_forward(
        groups, line, flags, qkv, fc_both, cotangent
    )
    context3 = context.reshape(pieces)
    hidden, normed2, grad_mlp = middle(flags, context3, x_all, cot, vectors, weights)
    mlp, grad_normed2, grad_fc, grad_bfc1 = feed_forward(
        normed2.reshape(rows, width), grad_mlp.reshape(rows, width), fc_weights, fc1_bias, tile
    )
    block_out, grad_hidden, grad_context, grad_wout, sums = turn(
        flags,
        mlp.reshape(pieces),
        grad_normed2.reshape(pieces),
        hidden,
        x_all,
        cot,
        context3,
        vectors,
        weights,
    )
    grad_query, grad_key, grad_value, grad_bqv, block_out, shard_fc, shard_wout = attend_backward(
        groups,
        line,
        images,
        flags,
        query_stats,
        qkv,
        grad_context.reshape(rows, width),
        context,
        block_out,
        grad_fc,
        grad_wout,
    )

    wide = width // groups
    none = jnp.zeros((1, width), f32)
    by_vector = jnp.concatenate(
        [none, sums[0:1], none, sums[1:2], sums[2:6]], axis=0
    ).reshape(8, groups, wide)
    by_vector = jnp.pad(jnp.transpose(by_vector, (1, 0, 2)), ((0, 0), (0, 0), (0, LANES - wide)))
    by_vector = jnp.broadcast_to(by_vector[None], (line, groups, 8, LANES))
    by_head = jnp.transpose(grad_bqv[:, :2], (1, 0, 2)).reshape(2, line, bq_cols, groups, bq_rows)
    by_head = jnp.transpose(by_head, (1, 3, 0, 4, 2)).reshape(line, groups, 2 * bq_rows, bq_cols)
    by_unit = jnp.transpose(grad_bfc1.reshape(line, f_cols, groups, f_rows), (0, 2, 3, 1))

    def wider(x):
        return jnp.pad(x, ((0, 0), (0, 0), (0, 0), (0, LANES - x.shape[3])))

    smalls = jnp.concatenate([by_vector, wider(by_head), wider(by_unit)], axis=2)
    smalls = jnp.pad(smalls, ((0, 0), (0, 0), (0, small_rows - smalls.shape[2]), (0, 0)))
    grad_input, shard_weights, shard_small = leave(
        groups,
        line,
        images,
        grad_query,
        grad_key,
        grad_value,
        weights,
        normed1_t,
        x_all,
        grad_hidden,
        vectors,
        smalls.reshape(line, groups * small_rows, LANES),
    )
    grad_input = grad_input.astype(f32)
    cols = width // line
    shard_wqkv = jnp.stack([shard_weights[:, n * cols : (n + 1) * cols] for n in range(3)])
    shard_wout = shard_wout.T
    shard_fc = shard_fc.reshape(shard_fc.shape[0], -1, 2, tile)
    shard_fc1 = shard_fc[:, :, 0].reshape(w_fc1.shape)
    shard_fc2 = shard_fc[:, :, 1].reshape(w_fc1.shape).T
    own = lax.dynamic_slice_in_dim(shard_small[:8], place * own_width, own_width, 1)
    shard_gain, shard_shift, shard_scale, shard_bias = (own[2 * n : 2 * n + 2] for n in range(4))
    shard_bqv = shard_small[8:b_at, :bq_cols].reshape(b_qv.shape)
    shard_bfc1 = shard_small[b_at : b_at + f_rows, :f_cols]
    return (
        block_out,
        grad_input,
        shard_wqkv,
        shard_bqv,
        shard_wout,
        shard_fc1,
        shard_bfc1,
        shard_fc2,
        shard_gain,
        shard_shift,
        shard_scale,
        shard_bias,
    )


def solution(mesh):
    rows = P("dp", "tensor", None)
    vector = P(None, ("dp", "tensor"))
    weights = (
        P(None, "dp", "tensor"),
        P(None, "dp", "tensor"),
        P("tensor", "dp"),
        P("dp", "tensor"),
        P("dp", "tensor"),
        P("tensor", "dp"),
    )
    return jax.shard_map(
        body,
        mesh=mesh,
        in_specs=(rows, rows, P("dp")) + weights + (vector,) * 4,
        out_specs=(rows, rows) + weights + (vector,) * 4,
        check_vma=False,
    )
```

```python
import functools
import math

import jax
import jax.numpy as jnp
from jax import lax
from jax.experimental import pallas as pl
from jax.experimental.pallas import tpu as pltpu
from jax.sharding import PartitionSpec as P

HD = 64
LANES = 128
LOG2E = math.log2(math.e)
NEG = -1e30
NT = (((1,), (1,)), ((), ()))
NN = (((1,), (0,)), ((), ()))
TN = (((0,), (0,)), ((), ()))
f32 = jnp.float32
bf16 = jnp.bfloat16


def round_up(n, m):
    return (n + m - 1) // m * m


def parts(x):
    hi = x.astype(bf16).astype(f32)
    rest = x - hi
    mid = rest.astype(bf16).astype(f32)
    return hi, mid, rest - mid


def keys_with_bias(keys, lane, row, length, own, spare):
    bias = jnp.where(row < length, 0.0, NEG)
    ones = jnp.where((lane >= spare) & (lane < spare + 3), 1.0, 0.0)
    return jnp.where(own, keys, jnp.where(lane == spare + 3, bias, ones)).astype(bf16)


MESH = pl.DeviceIdType.MESH
ANY = pl.BlockSpec(memory_space=pl.ANY)
DMA = pltpu.SemaphoreType.DMA


def flipped(g, mask):
    bit = 1
    while bit <= mask:
        if mask & bit:
            g = g + bit * (1 - 2 * ((g // bit) % 2))
        bit *= 2
    return g


class Place:
    def __init__(self, groups, line):
        self.groups, self.line = groups, line
        self.g, self.z = lax.axis_index("dp"), lax.axis_index("tensor")
        self.masks = list(range(0, groups, 2))
        self.square = groups == 8
        self.direct = [2, 4] if self.square else self.masks[1:]

    def image(self, z):
        odd = self.g % 2
        return z + odd * (self.line - 1 - 2 * z)

    def near(self, k):
        place = 0
        if not isinstance(k, int):
            for i in range(self.line):
                place = jnp.where(k == i, self.near(i), place)
            return place
        for z in range(self.line):
            order = sorted(range(self.line), key=lambda t: (abs(t - z), t))
            place = jnp.where(self.z == z, order[k], place)
        return place

    def up(self, k):
        return lax.rem(self.z + k, self.line)

    def down(self, k):
        return lax.rem(self.z + self.line - k, self.line)

    def barrier(self):
        semaphore = pltpu.get_barrier_semaphore()
        peers = [(self.g, self.up(s)) for s in range(1, self.line)]
        peers += [(flipped(self.g, m), self.z) for m in self.direct + [1]]
        for peer in peers:
            pl.semaphore_signal(semaphore, inc=1, device_id=peer, device_id_type=MESH)
        pl.semaphore_wait(semaphore, len(peers))


def remote(src, dst, send, recv, device):
    return pltpu.make_async_remote_copy(
        src_ref=src, dst_ref=dst, send_sem=send, recv_sem=recv, device_id=device, device_id_type=MESH
    )


class Gather:
    @staticmethod
    def sems(groups, line):
        chips = groups // 2
        return [DMA((line,))] * 2 + [DMA((chips, line))] * 4

    def __init__(self, at, shard, full, sems):
        self.at, self.shard, self.full = at, shard, full
        self.zs, self.zr, self.ds, self.dr, self.cs, self.cr = sems
        self.rows = shard.shape[0]

    def piece(self, mask, t):
        rows = pl.ds(pl.multiple_of(flipped(self.at.g, mask) * self.rows, 8), self.rows)
        return self.full.at[t, rows, :]

    def source(self, mask, k):
        own = mask == 0 and k == 0
        return self.shard if own else self.piece(mask, self.at.near(k))

    def local(self):
        return pltpu.make_async_copy(self.shard, self.piece(0, self.at.z), self.zr.at[self.at.z])

    def along(self, k):
        at = self.at
        t = at.near(k)
        return remote(
            self.shard, self.piece(0, at.z), self.zs.at[t], self.zr.at[at.z], (at.g, t)
        )

    def across(self, mask, k):
        at = self.at
        via, peer = 0, mask
        if at.square and mask == 6:
            via, peer = (2, 4) if k % 2 == 0 else (4, 2)
        t = at.near(k)
        m = mask // 2
        return remote(
            self.source(via, k), self.piece(via, t), self.ds.at[m, t], self.dr.at[m, t],
            (flipped(at.g, peer), at.z),
        )

    def core(self, mask, k):
        at = self.at
        t = at.near(k)
        m = mask // 2
        return remote(
            self.source(mask, k), self.piece(mask, t), self.cs.at[m, t], self.cr.at[m, t],
            (flipped(at.g, 1), at.z),
        )

    def arrived(self, mask, t, sem):
        piece = self.piece(mask, t)
        remote(piece, piece, sem, sem, (flipped(self.at.g, 1), self.at.z)).wait_recv()

    def start(self):
        self.local().start()
        for k in range(1, self.at.line):
            self.along(k).start()
        self.spread(0)

    def spread(self, k):
        at = self.at
        if k:
            t = at.near(k)
            self.arrived(0, t, self.zr.at[t])
        for mask in at.direct:
            self.across(mask, k).start()
        self.core(0, k).start()

    def passing(self, k):
        at = self.at
        t = at.near(k)
        for mask in at.direct:
            self.arrived(mask, t, self.dr.at[mask // 2, t])
            if at.square and mask == (2 if k % 2 == 0 else 4):
                self.across(6, k).start()
            self.core(mask, k).start()

    def last(self, k):
        at = self.at
        if at.square:
            t = at.near(k)
            self.arrived(6, t, self.dr.at[3, t])
            self.core(6, k).start()

    def finish(self):
        at = self.at
        for k in range(at.line):
            t = at.near(k)
            if k:
                self.along(k).wait_send()
            for mask in at.masks:
                self.arrived(mask ^ 1, t, self.cr.at[mask // 2, t])
                self.core(mask, k).wait_send()
                if mask:
                    self.across(mask, k).wait_send()
        self.local().wait()

    def steps(self):
        line = self.at.line
        out = []
        for i in range(line + 2):
            for work, k in ((self.spread, i), (self.passing, i - 1), (self.last, i - 2)):
                if 0 <= k < line:
                    out.append(functools.partial(work, k) if i else self.start)
        return out + [self.finish]


class ToOwner:
    @staticmethod
    def sems(groups, line):
        return [DMA((line,)), DMA((line,))]

    def __init__(self, at, rows, image, sems):
        self.at, self.rows, self.image = at, rows, image
        self.send, self.recv = sems
        self.count = rows.shape[0]

    def local(self):
        at = self.at
        return pltpu.make_async_copy(
            self.rows.at[jnp.minimum(at.image(at.z), self.count - 1)], self.image.at[at.z], self.send.at[0]
        )

    def copy(self, k, arriving=False):
        at = self.at
        to = at.near(k)
        src = self.rows.at[jnp.minimum(at.image(to), self.count - 1)]
        slot = to if arriving else at.z
        return remote(src, self.image.at[slot], self.send.at[k], self.recv.at[slot], (at.g, to))

    def start_one(self, k):
        at = self.at
        if k == 0:
            self.local().start()
        else:
            pl.when(at.image(at.near(k)) < self.count)(self.copy(k).start)

    def start(self):
        for k in range(self.at.line):
            self.start_one(k)

    def finish(self):
        at = self.at
        for k in range(1, at.line):
            pl.when(at.image(at.near(k)) < self.count)(self.copy(k).wait_send)
            pl.when(at.image(at.z) < self.count)(self.copy(k, True).wait_recv)
        self.local().wait()


class FromOwner:
    sems = ToOwner.sems

    def __init__(self, at, image, rows, sems):
        self.at, self.rows, self.image = at, rows, image
        self.send, self.recv = sems
        self.count = rows.shape[0]

    def local(self):
        at = self.at
        return pltpu.make_async_copy(
            self.image.at[at.z], self.rows.at[jnp.minimum(at.image(at.z), self.count - 1)], self.send.at[0]
        )

    def copy(self, k, arriving=False):
        at = self.at
        owner = at.down(k) if arriving else at.z
        dst = self.rows.at[jnp.minimum(at.image(owner), self.count - 1)]
        return remote(self.image.at[at.up(k)], dst, self.send.at[k], self.recv.at[k], (at.g, at.up(k)))

    def start_piece(self, p):
        at = self.at
        own = at.image(at.z) < self.count
        k = lax.rem(p - at.z + at.line, at.line)
        pl.when(own & (k == 0))(lambda: self.local().start())
        pl.when(own & (k > 0))(lambda: self.copy(k).start())

    def start(self):
        for p in range(self.at.line):
            self.start_piece(p)

    def finish(self):
        at = self.at

        @pl.when(at.image(at.z) < self.count)
        def _():
            for k in range(1, at.line):
                self.copy(k).wait_send()
            self.local().wait()

        for k in range(1, at.line):
            pl.when(at.image(at.down(k)) < self.count)(self.copy(k, True).wait_recv)


class Reduce:
    @staticmethod
    def scratch(groups, line, r, c, dtype):
        chips = groups // 2
        return [
            pltpu.VMEM((chips, line, r, c), dtype),
            pltpu.VMEM((chips, line, r, c), dtype),
            pltpu.VMEM((chips - 1, line, r, c), dtype),
            pltpu.VMEM((line, r, c), dtype),
        ] + [DMA((chips, line))] * 5 + [DMA((line,))] * 2

    def __init__(self, at, full, scratch, rows):
        self.at, self.full, self.rows, self.apart = at, full, rows, False
        self.cbuf, self.sums, self.dbuf, self.zbuf = scratch[:4]
        self.ls, self.cs, self.cr, self.ds, self.dr, self.zs, self.zr = scratch[4:]
        self.order = [6, 2, 4, 0] if at.square else at.masks[1:] + [0]

    def far(self, k):
        return self.at.near(self.at.line - 1 - k)

    def piece(self, mask, t):
        rows = pl.ds(pl.multiple_of(flipped(self.at.g, mask) * self.rows, 8), self.rows)
        return self.full.at[t, rows, :]

    def local(self, mask, t):
        m = mask // 2
        return pltpu.make_async_copy(self.piece(mask, t), self.sums.at[m, t], self.ls.at[m, t])

    def core(self, mask, t):
        at, m = self.at, mask // 2
        return remote(
            self.piece(mask ^ 1, t), self.cbuf.at[m, t], self.cs.at[m, t], self.cr.at[m, t],
            (flipped(at.g, 1), at.z),
        )

    def across(self, mask, k):
        at, m = self.at, mask // 2
        peer, t = mask, self.far(k)
        if at.square and mask == 6:
            peer = 4 if k % 2 == 0 else 2
        return remote(
            self.sums.at[m, t], self.dbuf.at[m - 1, t], self.ds.at[m, t], self.dr.at[m, t],
            (flipped(at.g, peer), at.z),
        )

    def along(self, t):
        at = self.at
        return remote(
            self.sums.at[0, t], self.zbuf.at[at.z], self.zs.at[t], self.zr.at[at.z], (at.g, t)
        )

    def add(self, m, t, other):
        total = self.sums[m, t].astype(f32) + other.astype(f32)
        self.sums[m, t] = total.astype(self.sums.dtype)

    def begin(self, k):
        t = self.far(k)
        for mask in self.order:
            self.core(mask, t).start()
            self.local(mask, t).start()

    def pair(self, k):
        at = self.at
        t = self.far(k)
        for mask in self.order:
            m = mask // 2
            self.local(mask, t).wait()
            self.core(mask, t).wait_recv()
            self.add(m, t, self.cbuf[m, t])
            waits = at.square and mask == (2 if k % 2 == 0 else 4)
            if mask and not waits:
                self.across(mask, k).start()
        if k + 2 < at.line and not self.apart:
            self.begin(k + 2)

    def joined(self, k):
        at = self.at
        if at.square:
            mask = 2 if k % 2 == 0 else 4
            t = self.far(k)
            self.across(6, k).wait_recv()
            self.add(mask // 2, t, self.dbuf[2, t])
            self.across(mask, k).start()

    def own(self, k):
        at = self.at
        t = self.far(k)
        for mask in at.direct:
            self.across(mask, k).wait_recv()
            self.add(0, t, self.dbuf[mask // 2 - 1, t])
        if k < at.line - 1:
            self.along(t).start()

    def finish(self, out_ref):
        at = self.at
        total = self.sums[0, at.z].astype(f32)
        for k in range(1, at.line):
            t = at.near(k)
            buf, sem = self.zbuf.at[t], self.zr.at[t]
            remote(buf, buf, sem, sem, (flipped(at.g, 1), at.z)).wait_recv()
            total += self.zbuf[t].astype(f32)
        out_ref[...] = total
        for k in range(at.line):
            t = self.far(k)
            for mask in at.masks:
                self.core(mask, t).wait_send()
                if mask:
                    self.across(mask, k).wait_send()
            if k < at.line - 1:
                self.along(t).wait_send()

    def early(self):
        self.apart = True
        line = self.at.line
        out = []
        for i in range(line):
            todo = [functools.partial(self.begin, i)]
            for work, late in ((self.pair, 1), (self.joined, 3)):
                if i >= late:
                    todo.append(functools.partial(work, i - late))
            out.append(todo)
        return out

    def late(self):
        line = self.at.line
        out = [functools.partial(self.pair, line - 1)]
        done = max(line - 3, 0)
        for i in range(line):
            if done + i < line:
                out.append(functools.partial(self.joined, done + i))
            out.append(functools.partial(self.own, i))
        return out

    def start(self):
        self.begin(0)
        self.begin(1)

    def steps(self):
        line = self.at.line
        out = [self.start]
        for i in range(line + 4):
            for work, late in ((self.pair, 0), (self.joined, 2), (self.own, 4)):
                if 0 <= i - late < line:
                    out.append(functools.partial(work, i - late))
        return out


FWD = (3, 4, 7, 8, 8, 11, 12, 12, 15, 16)
COT = 4
ARRIVE = (0, 0, 1, 3)
FFC = 2
BACK = 6
BWD = (2, 2, 7, 7, 7, 7, 16, 16, 16, 16, 27, 27)


def run_ticks(ticks, step, part, parts):
    for at, work in ticks:
        if at % parts == part:
            pl.when(step == at // parts)(work)


def arrive_kernel(groups, line, x_ref, shard_ref, small_ref, xo_ref, full_ref, smalls_ref, *sems):
    at = Place(groups, line)
    n = len(Gather.sems(groups, line))
    rows = ToOwner(at, x_ref, xo_ref, sems[2 * n :])
    weights = Gather(at, shard_ref, full_ref, sems[:n])
    small = Gather(at, small_ref, smalls_ref, sems[n : 2 * n])
    at.barrier()
    for i, (one, two) in enumerate(zip(small.steps(), weights.steps())):
        one()
        two()
        for k in range(line):
            if ARRIVE[min(k, 3)] == i:
                rows.start_one(k)
    rows.finish()


def arrive(groups, line, x, shard, small):
    images, part_rows, width = x.shape
    return pl.pallas_call(
        functools.partial(arrive_kernel, groups, line),
        in_specs=[ANY] * 3,
        out_specs=[ANY] * 3,
        out_shape=[
            jax.ShapeDtypeStruct((line, part_rows, width), x.dtype),
            jax.ShapeDtypeStruct((line, groups * shard.shape[0], shard.shape[1]), shard.dtype),
            jax.ShapeDtypeStruct((line, groups * small.shape[0], small.shape[1]), small.dtype),
        ],
        scratch_shapes=Gather.sems(groups, line) * 2 + ToOwner.sems(groups, line),
        compiler_params=pltpu.CompilerParams(collective_id=1, has_side_effects=True),
        name="arrive",
    )(x, shard, small)


def leave_kernel(
    groups, line, gq_ref, gk_ref, gv_ref, w_ref, n1t_ref, x_ref, gh_ref, v_ref, smalls_ref,
    yo_ref, shard_ref, small_ref, gn, y, full, smalls, sums, *scratch
):
    at = Place(groups, line)
    n = len(ToOwner.sems(groups, line))
    m = (len(scratch) - n) // 2
    rows = FromOwner(at, y, yo_ref, scratch[:n])
    weights = Reduce(at, full, scratch[n : n + m], shard_ref.shape[0])
    small = Reduce(at, smalls, scratch[n + m :], small_ref.shape[0])
    step = pl.program_id(0)
    cols = gq_ref.shape[1]
    grads = (gq_ref, gk_ref, gv_ref)

    @pl.when(step == 0)
    def _():
        at.barrier()
        smalls[...] = smalls_ref[...]
        gn[...] = jnp.zeros_like(gn)

    @pl.when(step < line)
    def _():
        for i, ref in enumerate(grads):
            gn[...] += lax.dot_general(
                ref[...], w_ref[0, :, i * cols : (i + 1) * cols], NT, preferred_element_type=f32
            )

    @pl.when(step == line - 1)
    def _():
        part = x_ref.shape[1]
        sums[...] = jnp.zeros_like(sums)
        for p in range(line):

            def work(r, first, count, p=p):
                at_rows = slice(p * part + first, p * part + first + count)
                hat, inverse = norm_stats(x_ref[p, r].astype(f32))
                g = gn[at_rows, :]
                y[p, r] = (gh_ref[p, r] + norm_back(g, hat, inverse, v_ref[0:1])).astype(bf16)
                add_rows(sums, 0, g * hat)
                add_rows(sums, 8, g)

            work(slice(0, part), 0, part)
            rows.start_piece(p)
        carry = [jnp.sum(sums[8 * j : 8 * j + 8], axis=0, keepdims=True) for j in range(2)]
        wide = gn.shape[1] // groups
        for j, total in enumerate(carry):
            for g in range(groups):
                row = total[:, g * wide : (g + 1) * wide]
                if wide < LANES:
                    row = jnp.concatenate([row, jnp.zeros((1, LANES - wide), f32)], axis=1)
                at_row = g * small_ref.shape[0] + 2 * j
                for t in range(line):
                    smalls[t, at_row : at_row + 1, :] = row
        small.start()

    @pl.when(step >= line)
    def _():
        t = weights.far(step - line)
        for i, ref in enumerate(grads):
            full[t, :, i * cols : (i + 1) * cols] = lax.dot_general(
                n1t_ref[...], ref[...], NN, preferred_element_type=f32
            ).astype(bf16)

    for i, todo in enumerate(weights.early()):

        @pl.when(step == line + i)
        def _(todo=todo):
            for work in todo:
                work()

    @pl.when(step == 2 * line - 1)
    def _():
        for work in small.steps()[1:]:
            work()
        for work in weights.late():
            work()
        weights.finish(shard_ref)
        small.finish(small_ref)
        rows.finish()


def leave(groups, line, images, gq, gk, gv, weights, n1t, x, ghid, vectors, smalls):
    _, part, width = x.shape
    rows = line * part
    cols = width // line
    r, c = width // groups, 3 * cols
    sr, sc = smalls.shape[1] // groups, smalls.shape[2]

    def column(j):
        far = Place(groups, line).near(jnp.clip(2 * line - 1 - j, 0, line - 1))
        return 0, jnp.where(j < line, j, far)

    grad = pl.BlockSpec((rows, cols), column)
    return pl.pallas_call(
        functools.partial(leave_kernel, groups, line),
        grid=(2 * line,),
        in_specs=[
            grad,
            grad,
            grad,
            pl.BlockSpec((1, width, c), lambda j: (jnp.minimum(j, line - 1), 0, 0)),
            whole(width, rows),
            whole(line, part, width),
            whole(line, part, width),
            whole(*vectors.shape),
            whole(*smalls.shape),
        ],
        out_specs=[ANY, whole(r, c), whole(sr, sc)],
        out_shape=[
            jax.ShapeDtypeStruct((images, part, width), bf16),
            jax.ShapeDtypeStruct((r, c), f32),
            jax.ShapeDtypeStruct((sr, sc), f32),
        ],
        scratch_shapes=[
            pltpu.VMEM((rows, width), f32),
            pltpu.VMEM((line, part, width), bf16),
            pltpu.VMEM((line, width, c), bf16),
            pltpu.VMEM(smalls.shape, f32),
            pltpu.VMEM((16, width), f32),
        ]
        + ToOwner.sems(groups, line)
        + Reduce.scratch(groups, line, r, c, bf16)
        + Reduce.scratch(groups, line, sr, sc, f32),
        compiler_params=pltpu.CompilerParams(
            collective_id=2, has_side_effects=True, vmem_limit_bytes=62 * 2**20
        ),
        name="leave",
    )(gq, gk, gv, weights, n1t, x, ghid, vectors, smalls)


def norm_stats(values):
    center = values - jnp.mean(values, axis=-1, keepdims=True)
    inverse = lax.rsqrt(jnp.mean(center * center, axis=-1, keepdims=True) + 1e-06)
    return center * inverse, inverse


def norm_back(grad_norm, normed, inverse, gain):
    scaled = grad_norm * gain
    return inverse * (
        scaled
        - jnp.mean(scaled, axis=-1, keepdims=True)
        - normed * jnp.mean(scaled * normed, axis=-1, keepdims=True)
    )


def project_kernel(flag_ref, x_ref, v_ref, w_ref, b_ref, out_ref, xc_ref, n1t_ref, n1):
    @pl.when(pl.program_id(0) == 0)
    def _():
        rows = x_ref.shape[0]
        size = 32 if rows % 32 == 0 else 16

        def chunk(i, carry):
            r = pl.ds(pl.multiple_of(i * size, 16), size)
            x = jnp.where(flag_ref[1] > 0, x_ref[r, :].astype(f32), 0.0)
            xc_ref[r, :] = x.astype(bf16)
            hat, _ = norm_stats(x)
            n1[r, :] = (hat * v_ref[0:1] + v_ref[2:3]).astype(bf16)
            return carry

        lax.fori_loop(0, rows // size, chunk, 0)
    cols = out_ref.shape[2]
    part = pl.ds(pl.multiple_of(pl.program_id(0) * cols, LANES), cols)
    n1t_ref[part, :] = n1[:, part].T
    for i in range(3):
        w = w_ref[0, :, i * cols : (i + 1) * cols]
        out = lax.dot_general(n1[...], w, NN, preferred_element_type=f32) + b_ref[i]
        if i == 0:
            out = out * (HD ** (-0.5) * LOG2E)
        out_ref[i] = out.astype(bf16)


def whole(*shape):
    return pl.BlockSpec(shape, lambda *_: (0,) * len(shape), pipeline_mode=pl.Buffered(1))


def add_rows(ref, first, x):
    ref[first : first + 1] += jnp.sum(x, axis=0, keepdims=True)


SMEM = pl.BlockSpec(memory_space=pltpu.SMEM)


def project(flags, x, vectors, weights, bias):
    rows, width = x.shape
    line = weights.shape[0]
    cols = width // line
    return pl.pallas_call(
        project_kernel,
        grid=(line,),
        in_specs=[
            SMEM,
            whole(rows, width),
            whole(*vectors.shape),
            pl.BlockSpec((1, width, 3 * cols), lambda t: (t, 0, 0)),
            pl.BlockSpec((3, 1, cols), lambda t: (0, 0, t)),
        ],
        out_specs=[
            pl.BlockSpec((3, rows, cols), lambda t: (0, 0, t)),
            whole(rows, width),
            whole(width, rows),
        ],
        out_shape=[
            jax.ShapeDtypeStruct((3, rows, width), bf16),
            jax.ShapeDtypeStruct((rows, width), bf16),
            jax.ShapeDtypeStruct((width, rows), bf16),
        ],
        scratch_shapes=[pltpu.VMEM((rows, width), bf16)],
        compiler_params=pltpu.CompilerParams(vmem_limit_bytes=40 * 2**20),
        cost_estimate=pl.CostEstimate(
            flops=6 * rows * width * width, bytes_accessed=16 * rows * width, transcendentals=0
        ),
        name="project",
    )(flags, x, vectors, weights, bias)


def valid_rows(flag_ref, shape):
    row = pl.program_id(0) * shape[0] + lax.broadcasted_iota(jnp.int32, shape, 0)
    return row < flag_ref[0]


def middle_kernel(flag_ref, ctx_ref, x_ref, cot_ref, v_ref, w_ref, hid_ref, n2_ref, gm_ref):
    line, _, cols = w_ref.shape
    attn = v_ref[6:7]
    for t in range(line):
        part = ctx_ref[0, :, t * cols : (t + 1) * cols]
        attn = attn + lax.dot_general(part, w_ref[t], NT, preferred_element_type=f32)
    hidden = x_ref[0].astype(f32) + v_ref[4:5] * attn
    hid_ref[0] = hidden
    hat, _ = norm_stats(hidden)
    n2_ref[0] = (hat * v_ref[1:2] + v_ref[3:4]).astype(bf16)
    gout = jnp.where(valid_rows(flag_ref, hidden.shape), cot_ref[0].astype(f32), 0.0)
    gm_ref[0] = (gout * v_ref[5:6]).astype(bf16)


def middle(flags, context, x, cot, vectors, weights):
    line, part, width = x.shape
    cols = width // line
    piece = pl.BlockSpec((1, part, width), lambda p: (p, 0, 0))
    return pl.pallas_call(
        middle_kernel,
        grid=(line,),
        in_specs=[
            SMEM,
            piece,
            piece,
            piece,
            whole(*vectors.shape),
            pl.BlockSpec(
                (line, width, cols), lambda p: (0, 0, 3), pipeline_mode=pl.Buffered(1)
            ),
        ],
        out_specs=[piece] * 3,
        out_shape=[
            jax.ShapeDtypeStruct(x.shape, f32),
            jax.ShapeDtypeStruct(x.shape, bf16),
            jax.ShapeDtypeStruct(x.shape, bf16),
        ],
        compiler_params=pltpu.CompilerParams(vmem_limit_bytes=40 * 2**20),
        name="middle",
    )(flags, context, x, cot, vectors, weights)


def turn_kernel(
    flag_ref, mlp_ref, gn_ref, hid_ref, x_ref, cot_ref, ctx_ref, v_ref, w_ref,
    out_ref, gh_ref, gc_ref, gw_ref, sum_ref, acc, gattn, sums
):
    step = pl.program_id(0)
    line, _, cols = w_ref.shape
    part = hid_ref.shape[1]

    @pl.when(step == 0)
    def _():
        sums[...] = jnp.zeros_like(sums)
        acc[...] = jnp.zeros_like(acc)

    def work(r, first, count):
        hidden = hid_ref[0, r]
        mlp = mlp_ref[0, r] + v_ref[7:8]
        gn = gn_ref[0, r]
        row = step * part + first + lax.broadcasted_iota(jnp.int32, hidden.shape, 0)
        valid = row < flag_ref[0]
        out_ref[0, r] = jnp.where(valid, hidden + v_ref[5:6] * mlp, 0.0).astype(bf16)
        gout = jnp.where(valid, cot_ref[0, r].astype(f32), 0.0)
        hat, inverse = norm_stats(hidden)
        ghid = gout + norm_back(gn, hat, inverse, v_ref[1:2])
        gh_ref[0, r] = ghid
        attn = (hidden - x_ref[0, r].astype(f32)) / v_ref[4:5]
        grad = ghid * v_ref[4:5]
        gattn[r] = grad.astype(bf16)
        terms = (gn * hat, gn, ghid * attn, gout * mlp, grad, gout * v_ref[5:6])
        for j, term in enumerate(terms):
            add_rows(sums, 8 * j, term)

    work(slice(0, part), 0, part)

    @pl.when(step == line - 1)
    def _():
        rows = [jnp.sum(sums[8 * j : 8 * j + 8], axis=0, keepdims=True) for j in range(6)]
        sum_ref[...] = jnp.concatenate(rows + [jnp.zeros((2, sums.shape[1]), f32)], axis=0)

    for t in range(line):
        ctx = ctx_ref[0, :, t * cols : (t + 1) * cols]
        gc_ref[0, :, t * cols : (t + 1) * cols] = lax.dot_general(
            gattn[...], w_ref[t], NN, preferred_element_type=f32
        ).astype(bf16)
        acc[t] += lax.dot_general(gattn[...], ctx, TN, preferred_element_type=f32)

    @pl.when(step == line - 1)
    def _():
        gw_ref[...] = acc[...].astype(bf16)


def turn(flags, mlp, gn, hidden, x, cot, context, vectors, weights):
    line, part, width = x.shape
    cols = width // line
    piece = pl.BlockSpec((1, part, width), lambda p: (p, 0, 0))
    return pl.pallas_call(
        turn_kernel,
        grid=(line,),
        in_specs=[SMEM]
        + [piece] * 6
        + [
            whole(*vectors.shape),
            pl.BlockSpec(
                (line, width, cols), lambda p: (0, 0, 3), pipeline_mode=pl.Buffered(1)
            ),
        ],
        out_specs=[piece] * 3 + [whole(line, width, cols), whole(8, width)],
        out_shape=[
            jax.ShapeDtypeStruct(x.shape, bf16),
            jax.ShapeDtypeStruct(x.shape, f32),
            jax.ShapeDtypeStruct(x.shape, bf16),
            jax.ShapeDtypeStruct((line, width, cols), bf16),
            jax.ShapeDtypeStruct((8, width), f32),
        ],
        scratch_shapes=[
            pltpu.VMEM((line, width, cols), f32),
            pltpu.VMEM((part, width), bf16),
            pltpu.VMEM((48, width), f32),
        ],
        compiler_params=pltpu.CompilerParams(vmem_limit_bytes=56 * 2**20),
        name="turn",
    )(flags, mlp, gn, hidden, x, cot, context, vectors, weights)


def attend_forward_kernel(
    groups, line, rows, padded, len_ref, q_ref, k_ref, v_ref, shard_ref, cot_ref,
    ctx_ref, qa_ref, full_ref, coto_ref, ka, va, *sems
):
    at = Place(groups, line)
    n = len(Gather.sems(groups, line))
    weights = Gather(at, shard_ref, full_ref, sems[:n])
    cot = ToOwner(at, cot_ref, coto_ref, sems[n:])
    steps = weights.steps()

    def begin():
        at.barrier()
        steps[0]()

    ticks = [(0, begin), (COT, cot.start)]
    for i, work in enumerate(steps[1:]):
        ticks.append((FWD[min(i, len(FWD) - 1)], work))
    step = pl.program_id(0)
    length = len_ref[0]
    lane = lax.broadcasted_iota(jnp.int32, (padded, LANES), 1)
    row = lax.broadcasted_iota(jnp.int32, (padded, LANES), 0)
    lb = lane[:rows]
    if padded > rows:
        va[rows:] = jnp.zeros((padded - rows, LANES), bf16)
    for half in range(2):
        run_ticks(ticks, step, half, 2)
        own = (lb < HD) if half == 0 else (lb >= HD)
        spare = HD if half == 0 else 0
        ka[:rows] = keys_with_bias(k_ref[...].astype(f32), lb, row[:rows], length, own, spare)
        if padded > rows:
            ka[rows:] = jnp.where(lane[rows:] == spare + 3, NEG, 0.0).astype(bf16)
        va[:rows] = jnp.where(
            own, v_ref[...].astype(f32), jnp.where(lb == spare, 1.0, 0.0)
        ).astype(bf16)
        qa = jnp.where(own, q_ref[...].astype(f32), jnp.where(lb == spare + 3, 1.0, 0.0))
        s = lax.dot_general(qa.astype(bf16), ka[...], NT, preferred_element_type=f32)
        m = jnp.max(s, axis=1, keepdims=True)
        p = jnp.exp2(s - m).astype(bf16)
        o = lax.dot_general(p, va[...], NN, preferred_element_type=f32)
        total = o[:, spare : spare + 1]
        o = o / total
        hi, mid, lo = parts(-(m + jnp.log2(total)))
        if half == 0:
            ctx_ref[...] = o.astype(bf16)
        else:
            ctx_ref[...] = jnp.where(own, o, ctx_ref[...].astype(f32)).astype(bf16)
        stats = jnp.where(lb == spare + 2, lo, qa)
        stats = jnp.where(lb == spare + 1, mid, stats)
        qa_ref[half] = jnp.where(lb == spare, hi, stats).astype(bf16)

    @pl.when(step == pl.num_programs(0) - 1)
    def _():
        for at_tick, work in ticks:
            if at_tick > 15:
                work()
        cot.finish()


def attend_forward(groups, line, length, qkv, shard, cot):
    _, rows, width = qkv.shape
    padded = round_up(rows, LANES)
    spec = pl.BlockSpec((rows, LANES), lambda j: (0, j))

    def third(n):
        return pl.BlockSpec((None, rows, LANES), lambda j: (n, 0, j))

    return pl.pallas_call(
        functools.partial(attend_forward_kernel, groups, line, rows, padded),
        grid=(width // LANES,),
        in_specs=[pl.BlockSpec(memory_space=pltpu.SMEM), third(0), third(1), third(2), ANY, ANY],
        out_specs=[spec, pl.BlockSpec((2, rows, LANES), lambda j: (j, 0, 0)), ANY, ANY],
        out_shape=[
            jax.ShapeDtypeStruct((rows, width), bf16),
            jax.ShapeDtypeStruct((width // HD, rows, LANES), bf16),
            jax.ShapeDtypeStruct((line, groups * shard.shape[0], shard.shape[1]), shard.dtype),
            jax.ShapeDtypeStruct((line,) + cot.shape[1:], cot.dtype),
        ],
        scratch_shapes=[pltpu.VMEM((padded, LANES), bf16), pltpu.VMEM((padded, LANES), bf16)]
        + Gather.sems(groups, line)
        + ToOwner.sems(groups, line),
        compiler_params=pltpu.CompilerParams(
            collective_id=3, has_side_effects=True, vmem_limit_bytes=56 * 2**20
        ),
        cost_estimate=pl.CostEstimate(
            flops=16 * rows * rows * width,
            bytes_accessed=12 * rows * width,
            transcendentals=rows * rows * width // HD,
        ),
        name="attend_forward",
    )(length, qkv, qkv, qkv, shard, cot)


def attend_backward_kernel(
    groups, line, rows, padded, blocks, len_ref, qa_ref, k_ref, v_ref, gc_ref, ctx_ref, y_ref, full_ref,
    out_ref, gq_ref, gk_ref, gv_ref, gb_ref, yo_ref, shard_ref, oshard_ref, ka, va, qs, ga, acc, *scratch
):
    at = Place(groups, line)
    n = len(ToOwner.sems(groups, line))
    back = FromOwner(at, y_ref, yo_ref, scratch[:n])
    m = (len(scratch) - n) // 2
    weights = Reduce(at, full_ref, scratch[n : n + m], shard_ref.shape[0])
    out_weights = Reduce(at, out_ref, scratch[n + m :], oshard_ref.shape[0])
    pairs = list(zip(weights.steps(), out_weights.steps()))

    def both(i):
        def run():
            for work in pairs[i]:
                work()

        return run

    steps = [both(i) for i in range(len(pairs))]

    def begin():
        at.barrier()
        steps[0]()

    ticks = [(0, begin), (BACK * blocks // 2, back.start)]
    for i, work in enumerate(steps[1:]):
        ticks.append((BWD[min(i, len(BWD) - 1)] * blocks // 2, work))
    step = pl.program_id(0)
    length = len_ref[0]
    lane = lax.broadcasted_iota(jnp.int32, (padded, LANES), 1)
    row = lax.broadcasted_iota(jnp.int32, (padded, LANES), 0)
    size = rows // blocks
    ls = lane[:rows]
    for half in range(2):
        own = (ls < HD) if half == 0 else (ls >= HD)
        spare = HD if half == 0 else 0
        ownb = own[:size]
        gc = gc_ref[...].astype(f32)
        corr = jnp.sum(
            jnp.where(own, gc * ctx_ref[...].astype(f32), 0.0), axis=1, keepdims=True
        )
        hi, mid, lo = parts(-corr)
        extra = jnp.where(ls == spare + 1, mid, jnp.where(ls == spare + 2, lo, 0.0))
        ga[:rows] = jnp.where(own, gc, jnp.where(ls == spare, hi, extra)).astype(bf16)
        qs[:rows] = qa_ref[half]
        if padded > rows:
            ga[rows:] = jnp.zeros((padded - rows, LANES), bf16)
            qs[rows:] = jnp.where(lane[rows:] == spare, NEG, 0.0).astype(bf16)
        ka[...] = keys_with_bias(k_ref[...].astype(f32), ls, row[:rows], length, own, spare)
        ones = jnp.where((ls >= spare) & (ls < spare + 3), 1.0, 0.0)
        va[...] = jnp.where(own, v_ref[...].astype(f32), ones).astype(bf16)
        bv = jnp.zeros((1, LANES), f32)
        for b in range(blocks):
            run_ticks(ticks, step, half * blocks + b, 2 * blocks)
            r = slice(b * size, (b + 1) * size)
            kb = ka[r]
            p = jnp.exp2(lax.dot_general(kb, qs[...], NT, preferred_element_type=f32))
            gp = lax.dot_general(va[r], ga[...], NT, preferred_element_type=f32)
            ds = (p * gp).astype(bf16)
            gv = lax.dot_general(p.astype(bf16), ga[...], NN, preferred_element_type=f32)
            gk = lax.dot_general(ds, qs[...], NN, preferred_element_type=f32) * (1.0 / LOG2E)
            gqt = lax.dot_general(kb.T, ds, NN, preferred_element_type=f32)
            acc[...] = gqt if b == 0 else acc[...] + gqt
            bv += jnp.sum(gv, axis=0, keepdims=True)
            if half == 0:
                gv_ref[r] = gv.astype(bf16)
                gk_ref[r] = gk.astype(bf16)
            else:
                gv_ref[r] = jnp.where(ownb, gv, gv_ref[r].astype(f32)).astype(bf16)
                gk_ref[r] = jnp.where(ownb, gk, gk_ref[r].astype(f32)).astype(bf16)
        gq = acc[...].T[:rows] * HD ** (-0.5)
        sums = jnp.concatenate(
            [jnp.sum(gq, axis=0, keepdims=True), bv, jnp.zeros((6, LANES), f32)], axis=0
        )
        if half == 0:
            gb_ref[0] = sums
        else:
            gb_ref[0] = jnp.where(own[:8], sums, gb_ref[0])
        if half == 0:
            gq_ref[...] = gq.astype(bf16)
        else:
            gq_ref[...] = jnp.where(own, gq, gq_ref[...].astype(f32)).astype(bf16)

    @pl.when(step == pl.num_programs(0) - 1)
    def _():
        for at_tick, work in ticks:
            if at_tick >= 2 * blocks * 8:
                work()
        weights.finish(shard_ref)
        out_weights.finish(oshard_ref)
        back.finish()


def attend_backward(groups, line, images, length, qa, qkv, gc, ctx, y, full, out_full):
    _, rows, width = qkv.shape
    padded = round_up(rows, LANES)
    blocks = 2 if rows % 32 == 0 else 1
    spec = pl.BlockSpec((rows, LANES), lambda j: (0, j))
    r, c, oc = full.shape[1] // groups, full.shape[2], out_full.shape[2]

    def third(n):
        return pl.BlockSpec((None, rows, LANES), lambda j: (n, 0, j))

    return pl.pallas_call(
        functools.partial(attend_backward_kernel, groups, line, rows, padded, blocks),
        grid=(width // LANES,),
        in_specs=[
            pl.BlockSpec(memory_space=pltpu.SMEM),
            pl.BlockSpec((2, rows, LANES), lambda j: (j, 0, 0)),
            third(1),
            third(2),
            spec,
            spec,
            ANY,
            ANY,
            ANY,
        ],
        out_specs=[spec] * 3
        + [pl.BlockSpec((1, 8, LANES), lambda j: (j, 0, 0)), ANY, whole(r, c), whole(r, oc)],
        out_shape=[jax.ShapeDtypeStruct((rows, width), bf16)] * 3
        + [
            jax.ShapeDtypeStruct((width // LANES, 8, LANES), f32),
            jax.ShapeDtypeStruct((images,) + y.shape[1:], y.dtype),
            jax.ShapeDtypeStruct((r, c), f32),
            jax.ShapeDtypeStruct((r, oc), f32),
        ],
        scratch_shapes=[
            pltpu.VMEM((rows, LANES), bf16),
            pltpu.VMEM((rows, LANES), bf16),
            pltpu.VMEM((padded, LANES), bf16),
            pltpu.VMEM((padded, LANES), bf16),
            pltpu.VMEM((LANES, padded), f32),
        ]
        + ToOwner.sems(groups, line)
        + Reduce.scratch(groups, line, r, c, full.dtype)
        + Reduce.scratch(groups, line, r, oc, full.dtype),
        compiler_params=pltpu.CompilerParams(
            collective_id=4, has_side_effects=True, vmem_limit_bytes=62 * 2**20
        ),
        cost_estimate=pl.CostEstimate(
            flops=40 * rows * rows * width,
            bytes_accessed=16 * rows * width,
            transcendentals=rows * rows * width // HD,
        ),
        name="attend_backward",
    )(length, qa, qkv, qkv, gc, ctx, y, full, out_full)


def feed_forward_kernel(
    tile, chunks, n2_ref, gm_ref, w_ref, b1_ref, mlp_ref, gn_ref, gw_ref, gb_ref, n2t, gmt, act_s, gpre_s
):
    @pl.when(pl.program_id(0) == 0)
    def _():
        n2t[...] = n2_ref[...].T
        gmt[...] = gm_ref[...].T
        mlp_ref[...] = jnp.zeros_like(mlp_ref)
        gn_ref[...] = jnp.zeros_like(gn_ref)

    w1 = w_ref[0, :, :tile]
    w2t = w_ref[0, :, tile:]
    size = n2_ref.shape[0] // chunks
    for c in range(chunks):
        r = slice(c * size, (c + 1) * size)
        pre = lax.dot_general(n2_ref[r], w1, NN, preferred_element_type=f32) + b1_ref[...]
        gact = lax.dot_general(gm_ref[r], w2t, NN, preferred_element_type=f32)
        cdf = 0.5 * (1.0 + lax.erf(pre * (1 / math.sqrt(2))))
        act_s[r] = (pre * cdf).astype(bf16)
        pdf = jnp.exp2(pre * pre * (-0.5 * LOG2E)) * (1 / math.sqrt(2 * math.pi))
        gpre = gact * (cdf + pre * pdf)
        total = jnp.sum(gpre, axis=0, keepdims=True)
        gb_ref[...] = total if c == 0 else gb_ref[...] + total
        gpre_s[r] = gpre.astype(bf16)
        mlp_ref[r] += lax.dot_general(act_s[r], w2t, NT, preferred_element_type=f32)
        gn_ref[r] += lax.dot_general(gpre_s[r], w1, NT, preferred_element_type=f32)
    gw_ref[0, :, :tile] = lax.dot_general(
        n2t[...], gpre_s[...], NN, preferred_element_type=f32
    ).astype(bf16)
    gw_ref[0, :, tile:] = lax.dot_general(
        gmt[...], act_s[...], NN, preferred_element_type=f32
    ).astype(bf16)


def feed_forward(n2, gm, weights, b1, tile):
    rows, width = n2.shape
    units = b1.shape[1]
    per = weights.shape[2] // (2 * tile)

    both = pl.BlockSpec((1, width, 2 * tile), lambda j: (j // per, 0, j % per))
    return pl.pallas_call(
        functools.partial(feed_forward_kernel, tile, FFC if rows % (16 * FFC) == 0 else 1),
        grid=(units // tile,),
        in_specs=[
            whole(rows, width),
            whole(rows, width),
            both,
            pl.BlockSpec((1, tile), lambda j: (0, j)),
        ],
        out_specs=[
            whole(rows, width),
            whole(rows, width),
            both,
            pl.BlockSpec((1, tile), lambda j: (0, j)),
        ],
        out_shape=[
            jax.ShapeDtypeStruct((rows, width), f32),
            jax.ShapeDtypeStruct((rows, width), f32),
            jax.ShapeDtypeStruct(weights.shape, bf16),
            jax.ShapeDtypeStruct((1, units), f32),
        ],
        scratch_shapes=[pltpu.VMEM((width, rows), bf16)] * 2 + [pltpu.VMEM((rows, tile), bf16)] * 2,
        compiler_params=pltpu.CompilerParams(vmem_limit_bytes=62 * 2**20),
        cost_estimate=pl.CostEstimate(
            flops=16 * rows * width * units,
            bytes_accessed=8 * width * units,
            transcendentals=2 * rows * units,
        ),
        name="feed_forward",
    )(n2, gm, weights, b1)


def body(
    block_input,
    cotangent,
    lengths,
    w_qkv,
    b_qv,
    w_out,
    w_fc1,
    b_fc1,
    w_fc2,
    ln_gain,
    ln_shift,
    layer_scale,
    out_bias,
):
    images, part_rows, width = block_input.shape
    groups = lax.axis_size("dp")
    line = lax.axis_size("tensor")
    rows = part_rows * line
    group = lax.axis_index("dp")
    place = lax.axis_index("tensor")
    mine = place + (group % 2) * (line - 1 - 2 * place)
    active = mine < images

    tile = min(512, w_fc1.shape[1])
    qkv_out = jnp.concatenate([w_qkv[0], w_qkv[1], w_qkv[2], w_out.T], axis=1)
    tiles = (w_fc1.shape[0], -1, 1, tile)
    fc_both = jnp.concatenate([w_fc1.reshape(tiles), w_fc2.T.reshape(tiles)], axis=2).reshape(
        w_fc1.shape[0], -1
    )

    def lanes(x):
        return jnp.pad(x, ((0, 0), (0, LANES - x.shape[1])))

    own_width = ln_gain.shape[1]
    _, bq_rows, bq_cols = b_qv.shape
    f_rows, f_cols = b_fc1.shape
    small = [ln_gain, ln_shift, layer_scale, out_bias, b_qv.astype(f32).reshape(-1, bq_cols)]
    small = jnp.concatenate([lanes(x) for x in small + [b_fc1.astype(f32)]], axis=0)
    small_rows = round_up(small.shape[0], 8)
    small = jnp.pad(small, ((0, small_rows - small.shape[0]), (0, 0)))
    b_at = 8 + 2 * bq_rows

    x_all, weights, small = arrive(groups, line, block_input, qkv_out, small)
    small = small.reshape(line, groups, small_rows, LANES)
    vectors = jnp.transpose(small[:, :, :8, :own_width], (2, 1, 0, 3)).reshape(8, width)
    qv_bias = jnp.transpose(
        small[:, :, 8:b_at, :bq_cols].reshape(line, groups, 2, bq_rows, bq_cols), (2, 0, 4, 1, 3)
    ).reshape(2, 1, width)
    fc1_bias = jnp.transpose(
        small[:, :, b_at : b_at + f_rows, :f_cols], (0, 3, 1, 2)
    ).reshape(1, -1)

    length = jnp.where(active, lengths[jnp.minimum(mine, images - 1)], 0).astype(jnp.int32)
    flags = jnp.stack([length, active.astype(jnp.int32)])
    pieces = (line, part_rows, width)

    zero = jnp.zeros((1, 1, width), f32)
    qkv, x_all, normed1_t = project(
        flags,
        x_all.reshape(rows, width),
        vectors,
        weights,
        jnp.concatenate([qv_bias[:1], zero, qv_bias[1:]]),
    )
    x_all = x_all.reshape(pieces)
    context, query_stats, fc_weights, cot = attend_forward(
        groups, line, flags, qkv, fc_both, cotangent
    )
    context3 = context.reshape(pieces)
    hidden, normed2, grad_mlp = middle(flags, context3, x_all, cot, vectors, weights)
    mlp, grad_normed2, grad_fc, grad_bfc1 = feed_forward(
        normed2.reshape(rows, width), grad_mlp.reshape(rows, width), fc_weights, fc1_bias, tile
    )
    block_out, grad_hidden, grad_context, grad_wout, sums = turn(
        flags,
        mlp.reshape(pieces),
        grad_normed2.reshape(pieces),
        hidden,
        x_all,
        cot,
        context3,
        vectors,
        weights,
    )
    grad_query, grad_key, grad_value, grad_bqv, block_out, shard_fc, shard_wout = attend_backward(
        groups,
        line,
        images,
        flags,
        query_stats,
        qkv,
        grad_context.reshape(rows, width),
        context,
        block_out,
        grad_fc,
        grad_wout,
    )

    wide = width // groups
    none = jnp.zeros((1, width), f32)
    by_vector = jnp.concatenate(
        [none, sums[0:1], none, sums[1:2], sums[2:6]], axis=0
    ).reshape(8, groups, wide)
    by_vector = jnp.pad(jnp.transpose(by_vector, (1, 0, 2)), ((0, 0), (0, 0), (0, LANES - wide)))
    by_vector = jnp.broadcast_to(by_vector[None], (line, groups, 8, LANES))
    by_head = jnp.transpose(grad_bqv[:, :2], (1, 0, 2)).reshape(2, line, bq_cols, groups, bq_rows)
    by_head = jnp.transpose(by_head, (1, 3, 0, 4, 2)).reshape(line, groups, 2 * bq_rows, bq_cols)
    by_unit = jnp.transpose(grad_bfc1.reshape(line, f_cols, groups, f_rows), (0, 2, 3, 1))

    def wider(x):
        return jnp.pad(x, ((0, 0), (0, 0), (0, 0), (0, LANES - x.shape[3])))

    smalls = jnp.concatenate([by_vector, wider(by_head), wider(by_unit)], axis=2)
    smalls = jnp.pad(smalls, ((0, 0), (0, 0), (0, small_rows - smalls.shape[2]), (0, 0)))
    grad_input, shard_weights, shard_small = leave(
        groups,
        line,
        images,
        grad_query,
        grad_key,
        grad_value,
        weights,
        normed1_t,
        x_all,
        grad_hidden,
        vectors,
        smalls.reshape(line, groups * small_rows, LANES),
    )
    grad_input = grad_input.astype(f32)
    cols = width // line
    shard_wqkv = jnp.stack([shard_weights[:, n * cols : (n + 1) * cols] for n in range(3)])
    shard_wout = shard_wout.T
    shard_fc = shard_fc.reshape(shard_fc.shape[0], -1, 2, tile)
    shard_fc1 = shard_fc[:, :, 0].reshape(w_fc1.shape)
    shard_fc2 = shard_fc[:, :, 1].reshape(w_fc1.shape).T
    own = lax.dynamic_slice_in_dim(shard_small[:8], place * own_width, own_width, 1)
    shard_gain, shard_shift, shard_scale, shard_bias = (own[2 * n : 2 * n + 2] for n in range(4))
    shard_bqv = shard_small[8:b_at, :bq_cols].reshape(b_qv.shape)
    shard_bfc1 = shard_small[b_at : b_at + f_rows, :f_cols]
    return (
        block_out,
        grad_input,
        shard_wqkv,
        shard_bqv,
        shard_wout,
        shard_fc1,
        shard_bfc1,
        shard_fc2,
        shard_gain,
        shard_shift,
        shard_scale,
        shard_bias,
    )


def solution(mesh):
    rows = P("dp", "tensor", None)
    vector = P(None, ("dp", "tensor"))
    weights = (
        P(None, "dp", "tensor"),
        P(None, "dp", "tensor"),
        P("tensor", "dp"),
        P("dp", "tensor"),
        P("dp", "tensor"),
        P("tensor", "dp"),
    )
    return jax.shard_map(
        body,
        mesh=mesh,
        in_specs=(rows, rows, P("dp")) + weights + (vector,) * 4,
        out_specs=(rows, rows) + weights + (vector,) * 4,
        check_vma=False,
    )
```

```python
import functools
import math

import jax
import jax.numpy as jnp
from jax import lax
from jax.experimental import pallas as pl
from jax.experimental.pallas import tpu as pltpu
from jax.sharding import PartitionSpec as P

HD = 64
LANES = 128
LOG2E = math.log2(math.e)
NEG = -1e30
NT = (((1,), (1,)), ((), ()))
NN = (((1,), (0,)), ((), ()))
TN = (((0,), (0,)), ((), ()))
f32 = jnp.float32
bf16 = jnp.bfloat16


def round_up(n, m):
    return (n + m - 1) // m * m


def parts(x):
    hi = x.astype(bf16).astype(f32)
    rest = x - hi
    mid = rest.astype(bf16).astype(f32)
    return hi, mid, rest - mid


def keys_with_bias(keys, lane, row, length, own, spare):
    bias = jnp.where(row < length, 0.0, NEG)
    ones = jnp.where((lane >= spare) & (lane < spare + 3), 1.0, 0.0)
    return jnp.where(own, keys, jnp.where(lane == spare + 3, bias, ones)).astype(bf16)


MESH = pl.DeviceIdType.MESH
ANY = pl.BlockSpec(memory_space=pl.ANY)
DMA = pltpu.SemaphoreType.DMA


def flipped(g, mask):
    bit = 1
    while bit <= mask:
        if mask & bit:
            g = g + bit * (1 - 2 * ((g // bit) % 2))
        bit *= 2
    return g


class Place:
    def __init__(self, groups, line):
        self.groups, self.line = groups, line
        self.g, self.z = lax.axis_index("dp"), lax.axis_index("tensor")
        self.masks = list(range(0, groups, 2))
        self.square = groups == 8
        self.direct = [2, 4] if self.square else self.masks[1:]

    def image(self, z):
        odd = self.g % 2
        return z + odd * (self.line - 1 - 2 * z)

    def near(self, k):
        place = 0
        if not isinstance(k, int):
            for i in range(self.line):
                place = jnp.where(k == i, self.near(i), place)
            return place
        for z in range(self.line):
            order = sorted(range(self.line), key=lambda t: (abs(t - z), t))
            place = jnp.where(self.z == z, order[k], place)
        return place

    def up(self, k):
        return lax.rem(self.z + k, self.line)

    def down(self, k):
        return lax.rem(self.z + self.line - k, self.line)

    def barrier(self):
        semaphore = pltpu.get_barrier_semaphore()
        peers = [(self.g, self.up(s)) for s in range(1, self.line)]
        peers += [(flipped(self.g, m), self.z) for m in self.direct + [1]]
        for peer in peers:
            pl.semaphore_signal(semaphore, inc=1, device_id=peer, device_id_type=MESH)
        pl.semaphore_wait(semaphore, len(peers))


def remote(src, dst, send, recv, device):
    return pltpu.make_async_remote_copy(
        src_ref=src, dst_ref=dst, send_sem=send, recv_sem=recv, device_id=device, device_id_type=MESH
    )


class Gather:
    @staticmethod
    def sems(groups, line):
        chips = groups // 2
        return [DMA((line,))] * 2 + [DMA((chips, line))] * 4

    def __init__(self, at, shard, full, sems):
        self.at, self.shard, self.full = at, shard, full
        self.zs, self.zr, self.ds, self.dr, self.cs, self.cr = sems
        self.rows = shard.shape[0]

    def piece(self, mask, t):
        rows = pl.ds(pl.multiple_of(flipped(self.at.g, mask) * self.rows, 8), self.rows)
        return self.full.at[t, rows, :]

    def source(self, mask, k):
        own = mask == 0 and k == 0
        return self.shard if own else self.piece(mask, self.at.near(k))

    def local(self):
        return pltpu.make_async_copy(self.shard, self.piece(0, self.at.z), self.zr.at[self.at.z])

    def along(self, k):
        at = self.at
        t = at.near(k)
        return remote(
            self.shard, self.piece(0, at.z), self.zs.at[t], self.zr.at[at.z], (at.g, t)
        )

    def across(self, mask, k):
        at = self.at
        via, peer = 0, mask
        if at.square and mask == 6:
            via, peer = (2, 4) if k % 2 == 0 else (4, 2)
        t = at.near(k)
        m = mask // 2
        return remote(
            self.source(via, k), self.piece(via, t), self.ds.at[m, t], self.dr.at[m, t],
            (flipped(at.g, peer), at.z),
        )

    def core(self, mask, k):
        at = self.at
        t = at.near(k)
        m = mask // 2
        return remote(
            self.source(mask, k), self.piece(mask, t), self.cs.at[m, t], self.cr.at[m, t],
            (flipped(at.g, 1), at.z),
        )

    def arrived(self, mask, t, sem):
        piece = self.piece(mask, t)
        remote(piece, piece, sem, sem, (flipped(self.at.g, 1), self.at.z)).wait_recv()

    def start(self):
        self.local().start()
        for k in range(1, self.at.line):
            self.along(k).start()
        self.spread(0)

    def spread(self, k):
        at = self.at
        if k:
            t = at.near(k)
            self.arrived(0, t, self.zr.at[t])
        for mask in at.direct:
            self.across(mask, k).start()
        self.core(0, k).start()

    def passing(self, k):
        at = self.at
        t = at.near(k)
        for mask in at.direct:
            self.arrived(mask, t, self.dr.at[mask // 2, t])
            if at.square and mask == (2 if k % 2 == 0 else 4):
                self.across(6, k).start()
            self.core(mask, k).start()

    def last(self, k):
        at = self.at
        if at.square:
            t = at.near(k)
            self.arrived(6, t, self.dr.at[3, t])
            self.core(6, k).start()

    def finish(self):
        at = self.at
        for k in range(at.line):
            t = at.near(k)
            if k:
                self.along(k).wait_send()
            for mask in at.masks:
                self.arrived(mask ^ 1, t, self.cr.at[mask // 2, t])
                self.core(mask, k).wait_send()
                if mask:
                    self.across(mask, k).wait_send()
        self.local().wait()

    def steps(self):
        line = self.at.line
        out = []
        for i in range(line + 2):
            for work, k in ((self.spread, i), (self.passing, i - 1), (self.last, i - 2)):
                if 0 <= k < line:
                    out.append(functools.partial(work, k) if i else self.start)
        return out + [self.finish]


class ToOwner:
    @staticmethod
    def sems(groups, line):
        return [DMA((line,)), DMA((line,))]

    def __init__(self, at, rows, image, sems):
        self.at, self.rows, self.image = at, rows, image
        self.send, self.recv = sems
        self.count = rows.shape[0]

    def local(self):
        at = self.at
        return pltpu.make_async_copy(
            self.rows.at[jnp.minimum(at.image(at.z), self.count - 1)], self.image.at[at.z], self.send.at[0]
        )

    def copy(self, k, arriving=False):
        at = self.at
        to = at.near(k)
        src = self.rows.at[jnp.minimum(at.image(to), self.count - 1)]
        slot = to if arriving else at.z
        return remote(src, self.image.at[slot], self.send.at[k], self.recv.at[slot], (at.g, to))

    def start_one(self, k):
        at = self.at
        if k == 0:
            self.local().start()
        else:
            pl.when(at.image(at.near(k)) < self.count)(self.copy(k).start)

    def start(self):
        for k in range(self.at.line):
            self.start_one(k)

    def finish(self):
        at = self.at
        for k in range(1, at.line):
            pl.when(at.image(at.near(k)) < self.count)(self.copy(k).wait_send)
            pl.when(at.image(at.z) < self.count)(self.copy(k, True).wait_recv)
        self.local().wait()


class FromOwner:
    sems = ToOwner.sems

    def __init__(self, at, image, rows, sems):
        self.at, self.rows, self.image = at, rows, image
        self.send, self.recv = sems
        self.count = rows.shape[0]

    def local(self):
        at = self.at
        return pltpu.make_async_copy(
            self.image.at[at.z], self.rows.at[jnp.minimum(at.image(at.z), self.count - 1)], self.send.at[0]
        )

    def copy(self, k, arriving=False):
        at = self.at
        owner = at.down(k) if arriving else at.z
        dst = self.rows.at[jnp.minimum(at.image(owner), self.count - 1)]
        return remote(self.image.at[at.up(k)], dst, self.send.at[k], self.recv.at[k], (at.g, at.up(k)))

    def start_piece(self, p):
        at = self.at
        own = at.image(at.z) < self.count
        k = lax.rem(p - at.z + at.line, at.line)
        pl.when(own & (k == 0))(lambda: self.local().start())
        pl.when(own & (k > 0))(lambda: self.copy(k).start())

    def start(self):
        for p in range(self.at.line):
            self.start_piece(p)

    def finish(self):
        at = self.at

        @pl.when(at.image(at.z) < self.count)
        def _():
            for k in range(1, at.line):
                self.copy(k).wait_send()
            self.local().wait()

        for k in range(1, at.line):
            pl.when(at.image(at.down(k)) < self.count)(self.copy(k, True).wait_recv)


class Reduce:
    @staticmethod
    def scratch(groups, line, r, c, dtype):
        chips = groups // 2
        return [
            pltpu.VMEM((chips, line, r, c), dtype),
            pltpu.VMEM((chips, line, r, c), dtype),
            pltpu.VMEM((chips - 1, line, r, c), dtype),
            pltpu.VMEM((line, r, c), dtype),
        ] + [DMA((chips, line))] * 5 + [DMA((line,))] * 2

    def __init__(self, at, full, scratch, rows):
        self.at, self.full, self.rows, self.apart = at, full, rows, False
        self.cbuf, self.sums, self.dbuf, self.zbuf = scratch[:4]
        self.ls, self.cs, self.cr, self.ds, self.dr, self.zs, self.zr = scratch[4:]
        self.order = [6, 2, 4, 0] if at.square else at.masks[1:] + [0]

    def far(self, k):
        return self.at.near(self.at.line - 1 - k)

    def piece(self, mask, t):
        rows = pl.ds(pl.multiple_of(flipped(self.at.g, mask) * self.rows, 8), self.rows)
        return self.full.at[t, rows, :]

    def local(self, mask, t):
        m = mask // 2
        return pltpu.make_async_copy(self.piece(mask, t), self.sums.at[m, t], self.ls.at[m, t])

    def core(self, mask, t):
        at, m = self.at, mask // 2
        return remote(
            self.piece(mask ^ 1, t), self.cbuf.at[m, t], self.cs.at[m, t], self.cr.at[m, t],
            (flipped(at.g, 1), at.z),
        )

    def across(self, mask, k):
        at, m = self.at, mask // 2
        peer, t = mask, self.far(k)
        if at.square and mask == 6:
            peer = 4 if k % 2 == 0 else 2
        return remote(
            self.sums.at[m, t], self.dbuf.at[m - 1, t], self.ds.at[m, t], self.dr.at[m, t],
            (flipped(at.g, peer), at.z),
        )

    def along(self, t):
        at = self.at
        return remote(
            self.sums.at[0, t], self.zbuf.at[at.z], self.zs.at[t], self.zr.at[at.z], (at.g, t)
        )

    def add(self, m, t, other):
        self.sums[m, t] = self.sums[m, t] + other

    def begin(self, k):
        t = self.far(k)
        for mask in self.order:
            self.core(mask, t).start()
            self.local(mask, t).start()

    def pair(self, k):
        at = self.at
        t = self.far(k)
        for mask in self.order:
            m = mask // 2
            self.local(mask, t).wait()
            self.core(mask, t).wait_recv()
            self.add(m, t, self.cbuf[m, t])
            waits = at.square and mask == (2 if k % 2 == 0 else 4)
            if mask and not waits:
                self.across(mask, k).start()
        if k + 2 < at.line and not self.apart:
            self.begin(k + 2)

    def joined(self, k):
        at = self.at
        if at.square:
            mask = 2 if k % 2 == 0 else 4
            t = self.far(k)
            self.across(6, k).wait_recv()
            self.add(mask // 2, t, self.dbuf[2, t])
            self.across(mask, k).start()

    def own(self, k):
        at = self.at
        t = self.far(k)
        for mask in at.direct:
            self.across(mask, k).wait_recv()
            self.add(0, t, self.dbuf[mask // 2 - 1, t])
        if k < at.line - 1:
            self.along(t).start()

    def finish(self, out_ref):
        at = self.at
        total = self.sums[0, at.z].astype(f32)
        for k in range(1, at.line):
            t = at.near(k)
            buf, sem = self.zbuf.at[t], self.zr.at[t]
            remote(buf, buf, sem, sem, (flipped(at.g, 1), at.z)).wait_recv()
            total += self.zbuf[t].astype(f32)
        out_ref[...] = total
        for k in range(at.line):
            t = self.far(k)
            for mask in at.masks:
                self.core(mask, t).wait_send()
                if mask:
                    self.across(mask, k).wait_send()
            if k < at.line - 1:
                self.along(t).wait_send()

    def early(self):
        self.apart = True
        line = self.at.line
        out = []
        for i in range(line):
            todo = [functools.partial(self.begin, i)]
            for work, late in ((self.pair, 1), (self.joined, 3)):
                if i >= late:
                    todo.append(functools.partial(work, i - late))
            out.append(todo)
        return out

    def late(self):
        line = self.at.line
        out = [functools.partial(self.pair, line - 1)]
        done = max(line - 3, 0)
        for i in range(line):
            if done + i < line:
                out.append(functools.partial(self.joined, done + i))
            out.append(functools.partial(self.own, i))
        return out

    def start(self):
        self.begin(0)
        self.begin(1)

    def steps(self):
        line = self.at.line
        out = [self.start]
        for i in range(line + 4):
            for work, late in ((self.pair, 0), (self.joined, 2), (self.own, 4)):
                if 0 <= i - late < line:
                    out.append(functools.partial(work, i - late))
        return out


FWD = (3, 4, 7, 8, 8, 11, 12, 12, 15, 16)
COT = 4
ARRIVE = (0, 0, 1, 3)
FFC = 2
BACK = 6
BWD = (2, 2, 7, 7, 7, 7, 16, 16, 16, 16, 27, 27)


def run_ticks(ticks, step, part, parts):
    for at, work in ticks:
        if at % parts == part:
            pl.when(step == at // parts)(work)


def arrive_kernel(groups, line, x_ref, shard_ref, small_ref, xo_ref, full_ref, smalls_ref, *sems):
    at = Place(groups, line)
    n = len(Gather.sems(groups, line))
    rows = ToOwner(at, x_ref, xo_ref, sems[2 * n :])
    weights = Gather(at, shard_ref, full_ref, sems[:n])
    small = Gather(at, small_ref, smalls_ref, sems[n : 2 * n])
    at.barrier()
    for i, (one, two) in enumerate(zip(small.steps(), weights.steps())):
        one()
        two()
        for k in range(line):
            if ARRIVE[min(k, 3)] == i:
                rows.start_one(k)
    rows.finish()


def arrive(groups, line, x, shard, small):
    images, part_rows, width = x.shape
    return pl.pallas_call(
        functools.partial(arrive_kernel, groups, line),
        in_specs=[ANY] * 3,
        out_specs=[ANY] * 3,
        out_shape=[
            jax.ShapeDtypeStruct((line, part_rows, width), x.dtype),
            jax.ShapeDtypeStruct((line, groups * shard.shape[0], shard.shape[1]), shard.dtype),
            jax.ShapeDtypeStruct((line, groups * small.shape[0], small.shape[1]), small.dtype),
        ],
        scratch_shapes=Gather.sems(groups, line) * 2 + ToOwner.sems(groups, line),
        compiler_params=pltpu.CompilerParams(collective_id=1, has_side_effects=True),
        name="arrive",
    )(x, shard, small)


def leave_kernel(
    groups, line, gq_ref, gk_ref, gv_ref, w_ref, n1t_ref, x_ref, gh_ref, v_ref, smalls_ref,
    yo_ref, shard_ref, small_ref, gn, y, full, smalls, sums, *scratch
):
    at = Place(groups, line)
    n = len(ToOwner.sems(groups, line))
    m = (len(scratch) - n) // 2
    rows = FromOwner(at, y, yo_ref, scratch[:n])
    weights = Reduce(at, full, scratch[n : n + m], shard_ref.shape[0])
    small = Reduce(at, smalls, scratch[n + m :], small_ref.shape[0])
    step = pl.program_id(0)
    cols = gq_ref.shape[1]
    grads = (gq_ref, gk_ref, gv_ref)

    @pl.when(step == 0)
    def _():
        at.barrier()
        smalls[...] = smalls_ref[...]
        gn[...] = jnp.zeros_like(gn)

    @pl.when(step < line)
    def _():
        for i, ref in enumerate(grads):
            gn[...] += lax.dot_general(
                ref[...], w_ref[0, :, i * cols : (i + 1) * cols], NT, preferred_element_type=f32
            )

    @pl.when(step == line - 1)
    def _():
        part = x_ref.shape[1]
        sums[...] = jnp.zeros_like(sums)
        for p in range(line):

            def work(r, first, count, p=p):
                at_rows = slice(p * part + first, p * part + first + count)
                hat, inverse = norm_stats(x_ref[p, r].astype(f32))
                g = gn[at_rows, :]
                y[p, r] = (gh_ref[p, r] + norm_back(g, hat, inverse, v_ref[0:1])).astype(bf16)
                add_rows(sums, 0, g * hat)
                add_rows(sums, 8, g)

            work(slice(0, part), 0, part)
            rows.start_piece(p)
        carry = [jnp.sum(sums[8 * j : 8 * j + 8], axis=0, keepdims=True) for j in range(2)]
        wide = gn.shape[1] // groups
        for j, total in enumerate(carry):
            for g in range(groups):
                row = total[:, g * wide : (g + 1) * wide]
                if wide < LANES:
                    row = jnp.concatenate([row, jnp.zeros((1, LANES - wide), f32)], axis=1)
                at_row = g * small_ref.shape[0] + 2 * j
                for t in range(line):
                    smalls[t, at_row : at_row + 1, :] = row
        small.start()

    @pl.when(step >= line)
    def _():
        t = weights.far(step - line)
        for i, ref in enumerate(grads):
            full[t, :, i * cols : (i + 1) * cols] = lax.dot_general(
                n1t_ref[...], ref[...], NN, preferred_element_type=f32
            ).astype(bf16)

    for i, todo in enumerate(weights.early()):

        @pl.when(step == line + i)
        def _(todo=todo):
            for work in todo:
                work()

    @pl.when(step == 2 * line - 1)
    def _():
        for work in small.steps()[1:]:
            work()
        for work in weights.late():
            work()
        weights.finish(shard_ref)
        small.finish(small_ref)
        rows.finish()


def leave(groups, line, images, gq, gk, gv, weights, n1t, x, ghid, vectors, smalls):
    _, part, width = x.shape
    rows = line * part
    cols = width // line
    r, c = width // groups, 3 * cols
    sr, sc = smalls.shape[1] // groups, smalls.shape[2]

    def column(j):
        far = Place(groups, line).near(jnp.clip(2 * line - 1 - j, 0, line - 1))
        return 0, jnp.where(j < line, j, far)

    grad = pl.BlockSpec((rows, cols), column)
    return pl.pallas_call(
        functools.partial(leave_kernel, groups, line),
        grid=(2 * line,),
        in_specs=[
            grad,
            grad,
            grad,
            pl.BlockSpec((1, width, c), lambda j: (jnp.minimum(j, line - 1), 0, 0)),
            whole(width, rows),
            whole(line, part, width),
            whole(line, part, width),
            whole(*vectors.shape),
            whole(*smalls.shape),
        ],
        out_specs=[ANY, whole(r, c), whole(sr, sc)],
        out_shape=[
            jax.ShapeDtypeStruct((images, part, width), bf16),
            jax.ShapeDtypeStruct((r, c), f32),
            jax.ShapeDtypeStruct((sr, sc), f32),
        ],
        scratch_shapes=[
            pltpu.VMEM((rows, width), f32),
            pltpu.VMEM((line, part, width), bf16),
            pltpu.VMEM((line, width, c), bf16),
            pltpu.VMEM(smalls.shape, f32),
            pltpu.VMEM((16, width), f32),
        ]
        + ToOwner.sems(groups, line)
        + Reduce.scratch(groups, line, r, c, bf16)
        + Reduce.scratch(groups, line, sr, sc, f32),
        compiler_params=pltpu.CompilerParams(
            collective_id=2, has_side_effects=True, vmem_limit_bytes=62 * 2**20
        ),
        name="leave",
    )(gq, gk, gv, weights, n1t, x, ghid, vectors, smalls)


def norm_stats(values):
    center = values - jnp.mean(values, axis=-1, keepdims=True)
    inverse = lax.rsqrt(jnp.mean(center * center, axis=-1, keepdims=True) + 1e-06)
    return center * inverse, inverse


def norm_back(grad_norm, normed, inverse, gain):
    scaled = grad_norm * gain
    return inverse * (
        scaled
        - jnp.mean(scaled, axis=-1, keepdims=True)
        - normed * jnp.mean(scaled * normed, axis=-1, keepdims=True)
    )


def project_kernel(flag_ref, x_ref, v_ref, w_ref, b_ref, out_ref, xc_ref, n1t_ref, n1):
    @pl.when(pl.program_id(0) == 0)
    def _():
        rows = x_ref.shape[0]
        size = 32 if rows % 32 == 0 else 16

        def chunk(i, carry):
            r = pl.ds(pl.multiple_of(i * size, 16), size)
            x = jnp.where(flag_ref[1] > 0, x_ref[r, :].astype(f32), 0.0)
            xc_ref[r, :] = x.astype(bf16)
            hat, _ = norm_stats(x)
            n1[r, :] = (hat * v_ref[0:1] + v_ref[2:3]).astype(bf16)
            return carry

        lax.fori_loop(0, rows // size, chunk, 0)
    cols = out_ref.shape[2]
    part = pl.ds(pl.multiple_of(pl.program_id(0) * cols, LANES), cols)
    n1t_ref[part, :] = n1[:, part].T
    for i in range(3):
        w = w_ref[0, :, i * cols : (i + 1) * cols]
        out = lax.dot_general(n1[...], w, NN, preferred_element_type=f32) + b_ref[i]
        if i == 0:
            out = out * (HD ** (-0.5) * LOG2E)
        out_ref[i] = out.astype(bf16)


def whole(*shape):
    return pl.BlockSpec(shape, lambda *_: (0,) * len(shape), pipeline_mode=pl.Buffered(1))


def add_rows(ref, first, x):
    ref[first : first + 1] += jnp.sum(x, axis=0, keepdims=True)


SMEM = pl.BlockSpec(memory_space=pltpu.SMEM)


def project(flags, x, vectors, weights, bias):
    rows, width = x.shape
    line = weights.shape[0]
    cols = width // line
    return pl.pallas_call(
        project_kernel,
        grid=(line,),
        in_specs=[
            SMEM,
            whole(rows, width),
            whole(*vectors.shape),
            pl.BlockSpec((1, width, 3 * cols), lambda t: (t, 0, 0)),
            pl.BlockSpec((3, 1, cols), lambda t: (0, 0, t)),
        ],
        out_specs=[
            pl.BlockSpec((3, rows, cols), lambda t: (0, 0, t)),
            whole(rows, width),
            whole(width, rows),
        ],
        out_shape=[
            jax.ShapeDtypeStruct((3, rows, width), bf16),
            jax.ShapeDtypeStruct((rows, width), bf16),
            jax.ShapeDtypeStruct((width, rows), bf16),
        ],
        scratch_shapes=[pltpu.VMEM((rows, width), bf16)],
        compiler_params=pltpu.CompilerParams(vmem_limit_bytes=62 * 2**20),
        cost_estimate=pl.CostEstimate(
            flops=6 * rows * width * width, bytes_accessed=16 * rows * width, transcendentals=0
        ),
        name="project",
    )(flags, x, vectors, weights, bias)


def valid_rows(flag_ref, shape):
    row = pl.program_id(0) * shape[0] + lax.broadcasted_iota(jnp.int32, shape, 0)
    return row < flag_ref[0]


def middle_kernel(flag_ref, ctx_ref, x_ref, cot_ref, v_ref, w_ref, hid_ref, n2_ref, gm_ref):
    line, _, cols = w_ref.shape
    attn = v_ref[6:7]
    for t in range(line):
        part = ctx_ref[0, :, t * cols : (t + 1) * cols]
        attn = attn + lax.dot_general(part, w_ref[t], NT, preferred_element_type=f32)
    hidden = x_ref[0].astype(f32) + v_ref[4:5] * attn
    hid_ref[0] = hidden
    hat, _ = norm_stats(hidden)
    n2_ref[0] = (hat * v_ref[1:2] + v_ref[3:4]).astype(bf16)
    gout = jnp.where(valid_rows(flag_ref, hidden.shape), cot_ref[0].astype(f32), 0.0)
    gm_ref[0] = (gout * v_ref[5:6]).astype(bf16)


def middle(flags, context, x, cot, vectors, weights):
    line, part, width = x.shape
    cols = width // line
    piece = pl.BlockSpec((1, part, width), lambda p: (p, 0, 0))
    return pl.pallas_call(
        middle_kernel,
        grid=(line,),
        in_specs=[
            SMEM,
            piece,
            piece,
            piece,
            whole(*vectors.shape),
            pl.BlockSpec(
                (line, width, cols), lambda p: (0, 0, 3), pipeline_mode=pl.Buffered(1)
            ),
        ],
        out_specs=[piece] * 3,
        out_shape=[
            jax.ShapeDtypeStruct(x.shape, f32),
            jax.ShapeDtypeStruct(x.shape, bf16),
            jax.ShapeDtypeStruct(x.shape, bf16),
        ],
        compiler_params=pltpu.CompilerParams(vmem_limit_bytes=62 * 2**20),
        name="middle",
    )(flags, context, x, cot, vectors, weights)


def turn_kernel(
    flag_ref, mlp_ref, gn_ref, hid_ref, x_ref, cot_ref, ctx_ref, v_ref, w_ref,
    out_ref, gh_ref, gc_ref, gw_ref, sum_ref, acc, gattn, sums
):
    step = pl.program_id(0)
    line, _, cols = w_ref.shape
    part = hid_ref.shape[1]

    @pl.when(step == 0)
    def _():
        sums[...] = jnp.zeros_like(sums)
        acc[...] = jnp.zeros_like(acc)

    def work(r, first, count):
        hidden = hid_ref[0, r]
        mlp = mlp_ref[0, r] + v_ref[7:8]
        gn = gn_ref[0, r]
        row = step * part + first + lax.broadcasted_iota(jnp.int32, hidden.shape, 0)
        valid = row < flag_ref[0]
        out_ref[0, r] = jnp.where(valid, hidden + v_ref[5:6] * mlp, 0.0).astype(bf16)
        gout = jnp.where(valid, cot_ref[0, r].astype(f32), 0.0)
        hat, inverse = norm_stats(hidden)
        ghid = gout + norm_back(gn, hat, inverse, v_ref[1:2])
        gh_ref[0, r] = ghid
        attn = (hidden - x_ref[0, r].astype(f32)) / v_ref[4:5]
        grad = ghid * v_ref[4:5]
        gattn[r] = grad.astype(bf16)
        terms = (gn * hat, gn, ghid * attn, gout * mlp, grad, gout * v_ref[5:6])
        for j, term in enumerate(terms):
            add_rows(sums, 8 * j, term)

    work(slice(0, part), 0, part)

    @pl.when(step == line - 1)
    def _():
        rows = [jnp.sum(sums[8 * j : 8 * j + 8], axis=0, keepdims=True) for j in range(6)]
        sum_ref[...] = jnp.concatenate(rows + [jnp.zeros((2, sums.shape[1]), f32)], axis=0)

    for t in range(line):
        ctx = ctx_ref[0, :, t * cols : (t + 1) * cols]
        gc_ref[0, :, t * cols : (t + 1) * cols] = lax.dot_general(
            gattn[...], w_ref[t], NN, preferred_element_type=f32
        ).astype(bf16)
        acc[t] += lax.dot_general(gattn[...], ctx, TN, preferred_element_type=f32)

    @pl.when(step == line - 1)
    def _():
        gw_ref[...] = acc[...].astype(bf16)


def turn(flags, mlp, gn, hidden, x, cot, context, vectors, weights):
    line, part, width = x.shape
    cols = width // line
    piece = pl.BlockSpec((1, part, width), lambda p: (p, 0, 0))
    return pl.pallas_call(
        turn_kernel,
        grid=(line,),
        in_specs=[SMEM]
        + [piece] * 6
        + [
            whole(*vectors.shape),
            pl.BlockSpec(
                (line, width, cols), lambda p: (0, 0, 3), pipeline_mode=pl.Buffered(1)
            ),
        ],
        out_specs=[piece] * 3 + [whole(line, width, cols), whole(8, width)],
        out_shape=[
            jax.ShapeDtypeStruct(x.shape, bf16),
            jax.ShapeDtypeStruct(x.shape, f32),
            jax.ShapeDtypeStruct(x.shape, bf16),
            jax.ShapeDtypeStruct((line, width, cols), bf16),
            jax.ShapeDtypeStruct((8, width), f32),
        ],
        scratch_shapes=[
            pltpu.VMEM((line, width, cols), f32),
            pltpu.VMEM((part, width), bf16),
            pltpu.VMEM((48, width), f32),
        ],
        compiler_params=pltpu.CompilerParams(vmem_limit_bytes=62 * 2**20),
        name="turn",
    )(flags, mlp, gn, hidden, x, cot, context, vectors, weights)


def attend_forward_kernel(
    groups, line, rows, padded, len_ref, q_ref, k_ref, v_ref, shard_ref, cot_ref,
    ctx_ref, qa_ref, full_ref, coto_ref, ka, va, *sems
):
    at = Place(groups, line)
    n = len(Gather.sems(groups, line))
    weights = Gather(at, shard_ref, full_ref, sems[:n])
    cot = ToOwner(at, cot_ref, coto_ref, sems[n:])
    steps = weights.steps()

    def begin():
        at.barrier()
        steps[0]()

    ticks = [(0, begin), (COT, cot.start)]
    for i, work in enumerate(steps[1:]):
        ticks.append((FWD[min(i, len(FWD) - 1)], work))
    step = pl.program_id(0)
    length = len_ref[0]
    lane = lax.broadcasted_iota(jnp.int32, (padded, LANES), 1)
    row = lax.broadcasted_iota(jnp.int32, (padded, LANES), 0)
    lb = lane[:rows]
    if padded > rows:
        va[rows:] = jnp.zeros((padded - rows, LANES), bf16)
    for half in range(2):
        run_ticks(ticks, step, half, 2)
        own = (lb < HD) if half == 0 else (lb >= HD)
        spare = HD if half == 0 else 0
        ka[:rows] = keys_with_bias(k_ref[...].astype(f32), lb, row[:rows], length, own, spare)
        if padded > rows:
            ka[rows:] = jnp.where(lane[rows:] == spare + 3, NEG, 0.0).astype(bf16)
        va[:rows] = jnp.where(
            own, v_ref[...].astype(f32), jnp.where(lb == spare, 1.0, 0.0)
        ).astype(bf16)
        qa = jnp.where(own, q_ref[...].astype(f32), jnp.where(lb == spare + 3, 1.0, 0.0))
        s = lax.dot_general(qa.astype(bf16), ka[...], NT, preferred_element_type=f32)
        m = jnp.max(s, axis=1, keepdims=True)
        p = jnp.exp2(s - m).astype(bf16)
        o = lax.dot_general(p, va[...], NN, preferred_element_type=f32)
        total = o[:, spare : spare + 1]
        o = o / total
        hi, mid, lo = parts(-(m + jnp.log2(total)))
        if half == 0:
            ctx_ref[...] = o.astype(bf16)
        else:
            ctx_ref[...] = jnp.where(own, o, ctx_ref[...].astype(f32)).astype(bf16)
        stats = jnp.where(lb == spare + 2, lo, qa)
        stats = jnp.where(lb == spare + 1, mid, stats)
        qa_ref[half] = jnp.where(lb == spare, hi, stats).astype(bf16)

    @pl.when(step == pl.num_programs(0) - 1)
    def _():
        for at_tick, work in ticks:
            if at_tick > 15:
                work()
        cot.finish()


def attend_forward(groups, line, length, qkv, shard, cot):
    _, rows, width = qkv.shape
    padded = round_up(rows, LANES)
    spec = pl.BlockSpec((rows, LANES), lambda j: (0, j))

    def third(n):
        return pl.BlockSpec((None, rows, LANES), lambda j: (n, 0, j))

    return pl.pallas_call(
        functools.partial(attend_forward_kernel, groups, line, rows, padded),
        grid=(width // LANES,),
        in_specs=[pl.BlockSpec(memory_space=pltpu.SMEM), third(0), third(1), third(2), ANY, ANY],
        out_specs=[spec, pl.BlockSpec((2, rows, LANES), lambda j: (j, 0, 0)), ANY, ANY],
        out_shape=[
            jax.ShapeDtypeStruct((rows, width), bf16),
            jax.ShapeDtypeStruct((width // HD, rows, LANES), bf16),
            jax.ShapeDtypeStruct((line, groups * shard.shape[0], shard.shape[1]), shard.dtype),
            jax.ShapeDtypeStruct((line,) + cot.shape[1:], cot.dtype),
        ],
        scratch_shapes=[pltpu.VMEM((padded, LANES), bf16), pltpu.VMEM((padded, LANES), bf16)]
        + Gather.sems(groups, line)
        + ToOwner.sems(groups, line),
        compiler_params=pltpu.CompilerParams(
            collective_id=3, has_side_effects=True, vmem_limit_bytes=62 * 2**20
        ),
        cost_estimate=pl.CostEstimate(
            flops=16 * rows * rows * width,
            bytes_accessed=12 * rows * width,
            transcendentals=rows * rows * width // HD,
        ),
        name="attend_forward",
    )(length, qkv, qkv, qkv, shard, cot)


def attend_backward_kernel(
    groups, line, rows, padded, blocks, len_ref, qa_ref, k_ref, v_ref, gc_ref, ctx_ref, y_ref, full_ref,
    out_ref, gq_ref, gk_ref, gv_ref, gb_ref, yo_ref, shard_ref, oshard_ref, ka, va, qs, ga, acc, *scratch
):
    at = Place(groups, line)
    n = len(ToOwner.sems(groups, line))
    back = FromOwner(at, y_ref, yo_ref, scratch[:n])
    m = (len(scratch) - n) // 2
    weights = Reduce(at, full_ref, scratch[n : n + m], shard_ref.shape[0])
    out_weights = Reduce(at, out_ref, scratch[n + m :], oshard_ref.shape[0])
    pairs = list(zip(weights.steps(), out_weights.steps()))

    def both(i):
        def run():
            for work in pairs[i]:
                work()

        return run

    steps = [both(i) for i in range(len(pairs))]

    def begin():
        at.barrier()
        steps[0]()

    ticks = [(0, begin), (BACK * blocks // 2, back.start)]
    for i, work in enumerate(steps[1:]):
        ticks.append((BWD[min(i, len(BWD) - 1)] * blocks // 2, work))
    step = pl.program_id(0)
    length = len_ref[0]
    lane = lax.broadcasted_iota(jnp.int32, (padded, LANES), 1)
    row = lax.broadcasted_iota(jnp.int32, (padded, LANES), 0)
    size = rows // blocks
    ls = lane[:rows]
    for half in range(2):
        own = (ls < HD) if half == 0 else (ls >= HD)
        spare = HD if half == 0 else 0
        ownb = own[:size]
        gc = gc_ref[...].astype(f32)
        corr = jnp.sum(
            jnp.where(own, gc * ctx_ref[...].astype(f32), 0.0), axis=1, keepdims=True
        )
        hi, mid, lo = parts(-corr)
        extra = jnp.where(ls == spare + 1, mid, jnp.where(ls == spare + 2, lo, 0.0))
        ga[:rows] = jnp.where(own, gc, jnp.where(ls == spare, hi, extra)).astype(bf16)
        qs[:rows] = qa_ref[half]
        if padded > rows:
            ga[rows:] = jnp.zeros((padded - rows, LANES), bf16)
            qs[rows:] = jnp.where(lane[rows:] == spare, NEG, 0.0).astype(bf16)
        ka[...] = keys_with_bias(k_ref[...].astype(f32), ls, row[:rows], length, own, spare)
        ones = jnp.where((ls >= spare) & (ls < spare + 3), 1.0, 0.0)
        va[...] = jnp.where(own, v_ref[...].astype(f32), ones).astype(bf16)
        bv = jnp.zeros((1, LANES), f32)
        for b in range(blocks):
            run_ticks(ticks, step, half * blocks + b, 2 * blocks)
            r = slice(b * size, (b + 1) * size)
            kb = ka[r]
            p = jnp.exp2(lax.dot_general(kb, qs[...], NT, preferred_element_type=f32))
            gp = lax.dot_general(va[r], ga[...], NT, preferred_element_type=f32)
            ds = (p * gp).astype(bf16)
            gv = lax.dot_general(p.astype(bf16), ga[...], NN, preferred_element_type=f32)
            gk = lax.dot_general(ds, qs[...], NN, preferred_element_type=f32) * (1.0 / LOG2E)
            gqt = lax.dot_general(kb.T, ds, NN, preferred_element_type=f32)
            acc[...] = gqt if b == 0 else acc[...] + gqt
            bv += jnp.sum(gv, axis=0, keepdims=True)
            if half == 0:
                gv_ref[r] = gv.astype(bf16)
                gk_ref[r] = gk.astype(bf16)
            else:
                gv_ref[r] = jnp.where(ownb, gv, gv_ref[r].astype(f32)).astype(bf16)
                gk_ref[r] = jnp.where(ownb, gk, gk_ref[r].astype(f32)).astype(bf16)
        gq = acc[...].T[:rows] * HD ** (-0.5)
        sums = jnp.concatenate(
            [jnp.sum(gq, axis=0, keepdims=True), bv, jnp.zeros((6, LANES), f32)], axis=0
        )
        if half == 0:
            gb_ref[0] = sums
        else:
            gb_ref[0] = jnp.where(own[:8], sums, gb_ref[0])
        if half == 0:
            gq_ref[...] = gq.astype(bf16)
        else:
            gq_ref[...] = jnp.where(own, gq, gq_ref[...].astype(f32)).astype(bf16)

    @pl.when(step == pl.num_programs(0) - 1)
    def _():
        for at_tick, work in ticks:
            if at_tick >= 2 * blocks * 8:
                work()
        weights.finish(shard_ref)
        out_weights.finish(oshard_ref)
        back.finish()


def attend_backward(groups, line, images, length, qa, qkv, gc, ctx, y, full, out_full):
    _, rows, width = qkv.shape
    padded = round_up(rows, LANES)
    blocks = 2 if rows % 32 == 0 else 1
    spec = pl.BlockSpec((rows, LANES), lambda j: (0, j))
    r, c, oc = full.shape[1] // groups, full.shape[2], out_full.shape[2]

    def third(n):
        return pl.BlockSpec((None, rows, LANES), lambda j: (n, 0, j))

    return pl.pallas_call(
        functools.partial(attend_backward_kernel, groups, line, rows, padded, blocks),
        grid=(width // LANES,),
        in_specs=[
            pl.BlockSpec(memory_space=pltpu.SMEM),
            pl.BlockSpec((2, rows, LANES), lambda j: (j, 0, 0)),
            third(1),
            third(2),
            spec,
            spec,
            ANY,
            ANY,
            ANY,
        ],
        out_specs=[spec] * 3
        + [pl.BlockSpec((1, 8, LANES), lambda j: (j, 0, 0)), ANY, whole(r, c), whole(r, oc)],
        out_shape=[jax.ShapeDtypeStruct((rows, width), bf16)] * 3
        + [
            jax.ShapeDtypeStruct((width // LANES, 8, LANES), f32),
            jax.ShapeDtypeStruct((images,) + y.shape[1:], y.dtype),
            jax.ShapeDtypeStruct((r, c), f32),
            jax.ShapeDtypeStruct((r, oc), f32),
        ],
        scratch_shapes=[
            pltpu.VMEM((rows, LANES), bf16),
            pltpu.VMEM((rows, LANES), bf16),
            pltpu.VMEM((padded, LANES), bf16),
            pltpu.VMEM((padded, LANES), bf16),
            pltpu.VMEM((LANES, padded), f32),
        ]
        + ToOwner.sems(groups, line)
        + Reduce.scratch(groups, line, r, c, full.dtype)
        + Reduce.scratch(groups, line, r, oc, full.dtype),
        compiler_params=pltpu.CompilerParams(
            collective_id=4, has_side_effects=True, vmem_limit_bytes=62 * 2**20
        ),
        cost_estimate=pl.CostEstimate(
            flops=40 * rows * rows * width,
            bytes_accessed=16 * rows * width,
            transcendentals=rows * rows * width // HD,
        ),
        name="attend_backward",
    )(length, qa, qkv, qkv, gc, ctx, y, full, out_full)


def feed_forward_kernel(
    tile, chunks, n2_ref, gm_ref, w_ref, b1_ref, mlp_ref, gn_ref, gw_ref, gb_ref, n2t, gmt, act_s, gpre_s
):
    @pl.when(pl.program_id(0) == 0)
    def _():
        n2t[...] = n2_ref[...].T
        gmt[...] = gm_ref[...].T
        mlp_ref[...] = jnp.zeros_like(mlp_ref)
        gn_ref[...] = jnp.zeros_like(gn_ref)

    w1 = w_ref[0, :, :tile]
    w2t = w_ref[0, :, tile:]
    size = n2_ref.shape[0] // chunks
    for c in range(chunks):
        r = slice(c * size, (c + 1) * size)
        pre = lax.dot_general(n2_ref[r], w1, NN, preferred_element_type=f32) + b1_ref[...]
        gact = lax.dot_general(gm_ref[r], w2t, NN, preferred_element_type=f32)
        cdf = 0.5 * (1.0 + lax.erf(pre * (1 / math.sqrt(2))))
        act_s[r] = (pre * cdf).astype(bf16)
        pdf = jnp.exp2(pre * pre * (-0.5 * LOG2E)) * (1 / math.sqrt(2 * math.pi))
        gpre = gact * (cdf + pre * pdf)
        total = jnp.sum(gpre, axis=0, keepdims=True)
        gb_ref[...] = total if c == 0 else gb_ref[...] + total
        gpre_s[r] = gpre.astype(bf16)
        mlp_ref[r] += lax.dot_general(act_s[r], w2t, NT, preferred_element_type=f32)
        gn_ref[r] += lax.dot_general(gpre_s[r], w1, NT, preferred_element_type=f32)
    gw_ref[0, :, :tile] = lax.dot_general(
        n2t[...], gpre_s[...], NN, preferred_element_type=f32
    ).astype(bf16)
    gw_ref[0, :, tile:] = lax.dot_general(
        gmt[...], act_s[...], NN, preferred_element_type=f32
    ).astype(bf16)


def feed_forward(n2, gm, weights, b1, tile):
    rows, width = n2.shape
    units = b1.shape[1]
    per = weights.shape[2] // (2 * tile)

    both = pl.BlockSpec((1, width, 2 * tile), lambda j: (j // per, 0, j % per))
    return pl.pallas_call(
        functools.partial(feed_forward_kernel, tile, FFC if rows % (16 * FFC) == 0 else 1),
        grid=(units // tile,),
        in_specs=[
            whole(rows, width),
            whole(rows, width),
            both,
            pl.BlockSpec((1, tile), lambda j: (0, j)),
        ],
        out_specs=[
            whole(rows, width),
            whole(rows, width),
            both,
            pl.BlockSpec((1, tile), lambda j: (0, j)),
        ],
        out_shape=[
            jax.ShapeDtypeStruct((rows, width), f32),
            jax.ShapeDtypeStruct((rows, width), f32),
            jax.ShapeDtypeStruct(weights.shape, bf16),
            jax.ShapeDtypeStruct((1, units), f32),
        ],
        scratch_shapes=[pltpu.VMEM((width, rows), bf16)] * 2 + [pltpu.VMEM((rows, tile), bf16)] * 2,
        compiler_params=pltpu.CompilerParams(vmem_limit_bytes=62 * 2**20),
        cost_estimate=pl.CostEstimate(
            flops=16 * rows * width * units,
            bytes_accessed=8 * width * units,
            transcendentals=2 * rows * units,
        ),
        name="feed_forward",
    )(n2, gm, weights, b1)


def body(
    block_input,
    cotangent,
    lengths,
    w_qkv,
    b_qv,
    w_out,
    w_fc1,
    b_fc1,
    w_fc2,
    ln_gain,
    ln_shift,
    layer_scale,
    out_bias,
):
    images, part_rows, width = block_input.shape
    groups = lax.axis_size("dp")
    line = lax.axis_size("tensor")
    rows = part_rows * line
    group = lax.axis_index("dp")
    place = lax.axis_index("tensor")
    mine = place + (group % 2) * (line - 1 - 2 * place)
    active = mine < images

    tile = min(512, w_fc1.shape[1])
    qkv_out = jnp.concatenate([w_qkv[0], w_qkv[1], w_qkv[2], w_out.T], axis=1)
    w_fc2_t = w_fc2.T
    fc_both = jnp.concatenate(
        [
            w[:, at : at + tile]
            for at in range(0, w_fc1.shape[1], tile)
            for w in (w_fc1, w_fc2_t)
        ],
        axis=1,
    )

    def lanes(x):
        return jnp.pad(x, ((0, 0), (0, LANES - x.shape[1])))

    own_width = ln_gain.shape[1]
    _, bq_rows, bq_cols = b_qv.shape
    f_rows, f_cols = b_fc1.shape
    small = jnp.concatenate([ln_gain, ln_shift, layer_scale, out_bias], axis=0)
    small = [small, b_qv.reshape(-1, bq_cols).astype(f32), b_fc1.astype(f32)]
    small = jnp.concatenate([lanes(x) for x in small], axis=0)
    small_rows = round_up(small.shape[0], 8)
    small = jnp.pad(small, ((0, small_rows - small.shape[0]), (0, 0)))
    b_at = 8 + 2 * bq_rows

    x_all, weights, small = arrive(groups, line, block_input, qkv_out, small)
    small = small.reshape(line, groups, small_rows, LANES)
    vectors = jnp.transpose(small[:, :, :8, :own_width], (2, 1, 0, 3)).reshape(8, width)
    qv_bias = jnp.transpose(
        small[:, :, 8:b_at, :bq_cols].reshape(line, groups, 2, bq_rows, bq_cols), (2, 0, 4, 1, 3)
    ).reshape(2, 1, width)
    fc1_bias = jnp.transpose(
        small[:, :, b_at : b_at + f_rows, :f_cols], (0, 3, 1, 2)
    ).reshape(1, -1)

    length = jnp.where(active, lengths[jnp.minimum(mine, images - 1)], 0).astype(jnp.int32)
    flags = jnp.stack([length, active.astype(jnp.int32)])
    pieces = (line, part_rows, width)

    zero = jnp.zeros((1, 1, width), f32)
    qkv, x_all, normed1_t = project(
        flags,
        x_all.reshape(rows, width),
        vectors,
        weights,
        jnp.concatenate([qv_bias[:1], zero, qv_bias[1:]]),
    )
    x_all = x_all.reshape(pieces)
    context, query_stats, fc_weights, cot = attend_forward(
        groups, line, flags, qkv, fc_both, cotangent
    )
    context3 = context.reshape(pieces)
    hidden, normed2, grad_mlp = middle(flags, context3, x_all, cot, vectors, weights)
    mlp, grad_normed2, grad_fc, grad_bfc1 = feed_forward(
        normed2.reshape(rows, width), grad_mlp.reshape(rows, width), fc_weights, fc1_bias, tile
    )
    block_out, grad_hidden, grad_context, grad_wout, sums = turn(
        flags,
        mlp.reshape(pieces),
        grad_normed2.reshape(pieces),
        hidden,
        x_all,
        cot,
        context3,
        vectors,
        weights,
    )
    grad_query, grad_key, grad_value, grad_bqv, block_out, shard_fc, shard_wout = attend_backward(
        groups,
        line,
        images,
        flags,
        query_stats,
        qkv,
        grad_context.reshape(rows, width),
        context,
        block_out,
        grad_fc,
        grad_wout,
    )

    wide = width // groups
    none = jnp.zeros((1, width), f32)
    by_vector = jnp.concatenate(
        [none, sums[0:1], none, sums[1:2], sums[2:6]], axis=0
    ).reshape(8, groups, wide)
    by_vector = jnp.pad(jnp.transpose(by_vector, (1, 0, 2)), ((0, 0), (0, 0), (0, LANES - wide)))
    by_vector = jnp.broadcast_to(by_vector[None], (line, groups, 8, LANES))
    by_head = jnp.transpose(grad_bqv[:, :2], (1, 0, 2)).reshape(2, line, bq_cols, groups, bq_rows)
    by_head = jnp.transpose(by_head, (1, 3, 0, 4, 2)).reshape(line, groups, 2 * bq_rows, bq_cols)
    by_unit = jnp.transpose(grad_bfc1.reshape(line, f_cols, groups, f_rows), (0, 2, 3, 1))

    def wider(x):
        return jnp.pad(x, ((0, 0), (0, 0), (0, 0), (0, LANES - x.shape[3])))

    smalls = jnp.concatenate([by_vector, wider(by_head), wider(by_unit)], axis=2)
    smalls = jnp.pad(smalls, ((0, 0), (0, 0), (0, small_rows - smalls.shape[2]), (0, 0)))
    grad_input, shard_weights, shard_small = leave(
        groups,
        line,
        images,
        grad_query,
        grad_key,
        grad_value,
        weights,
        normed1_t,
        x_all,
        grad_hidden,
        vectors,
        smalls.reshape(line, groups * small_rows, LANES),
    )
    grad_input = grad_input.astype(f32)
    cols = width // line
    shard_wqkv = jnp.stack([shard_weights[:, n * cols : (n + 1) * cols] for n in range(3)])
    shard_wout = shard_wout.T
    shard_fc1, shard_fc2 = (
        jnp.concatenate(
            [
                shard_fc[:, at : at + tile]
                for at in range(first, shard_fc.shape[1], 2 * tile)
            ],
            axis=1,
        )
        for first in (0, tile)
    )
    shard_fc2 = shard_fc2.T
    own = lax.dynamic_slice_in_dim(shard_small[:8], place * own_width, own_width, 1)
    shard_gain, shard_shift, shard_scale, shard_bias = (own[2 * n : 2 * n + 2] for n in range(4))
    shard_bqv = shard_small[8:b_at, :bq_cols].reshape(b_qv.shape)
    shard_bfc1 = shard_small[b_at : b_at + f_rows, :f_cols]
    return (
        block_out,
        grad_input,
        shard_wqkv,
        shard_bqv,
        shard_wout,
        shard_fc1,
        shard_bfc1,
        shard_fc2,
        shard_gain,
        shard_shift,
        shard_scale,
        shard_bias,
    )


def solution(mesh):
    rows = P("dp", "tensor", None)
    vector = P(None, ("dp", "tensor"))
    weights = (
        P(None, "dp", "tensor"),
        P(None, "dp", "tensor"),
        P("tensor", "dp"),
        P("dp", "tensor"),
        P("dp", "tensor"),
        P("tensor", "dp"),
    )
    return jax.shard_map(
        body,
        mesh=mesh,
        in_specs=(rows, rows, P("dp")) + weights + (vector,) * 4,
        out_specs=(rows, rows) + weights + (vector,) * 4,
        check_vma=False,
    )
```

```python
import functools
import math

import jax
import jax.numpy as jnp
from jax import lax
from jax.experimental import pallas as pl
from jax.experimental.pallas import tpu as pltpu
from jax.sharding import PartitionSpec as P

HD = 64
LANES = 128
LOG2E = math.log2(math.e)
NEG = -1e30
NT = (((1,), (1,)), ((), ()))
NN = (((1,), (0,)), ((), ()))
f32 = jnp.float32
bf16 = jnp.bfloat16


def round_up(n, m):
    return (n + m - 1) // m * m


def parts(x):
    hi = x.astype(bf16).astype(f32)
    rest = x - hi
    mid = rest.astype(bf16).astype(f32)
    return hi, mid, rest - mid


def keys_with_bias(keys, lane, row, length, own, spare):
    bias = jnp.where(row < length, 0.0, NEG)
    ones = jnp.where((lane >= spare) & (lane < spare + 3), 1.0, 0.0)
    return jnp.where(own, keys, jnp.where(lane == spare + 3, bias, ones)).astype(bf16)


MESH = pl.DeviceIdType.MESH
ANY = pl.BlockSpec(memory_space=pl.ANY)
DMA = pltpu.SemaphoreType.DMA


def flipped(g, mask):
    bit = 1
    while bit <= mask:
        if mask & bit:
            g = g + bit * (1 - 2 * ((g // bit) % 2))
        bit *= 2
    return g


class Place:
    def __init__(self, groups, line):
        self.groups, self.line = groups, line
        self.g, self.z = lax.axis_index("dp"), lax.axis_index("tensor")
        self.masks = list(range(0, groups, 2))
        self.square = groups == 8
        self.direct = [2, 4] if self.square else self.masks[1:]

    def image(self, z):
        odd = self.g % 2
        return z + odd * (self.line - 1 - 2 * z)

    def near(self, k):
        place = 0
        if not isinstance(k, int):
            for i in range(self.line):
                place = jnp.where(k == i, self.near(i), place)
            return place
        for z in range(self.line):
            order = sorted(range(self.line), key=lambda t: (abs(t - z), t))
            place = jnp.where(self.z == z, order[k], place)
        return place

    def up(self, k):
        return lax.rem(self.z + k, self.line)

    def down(self, k):
        return lax.rem(self.z + self.line - k, self.line)

    def barrier(self):
        semaphore = pltpu.get_barrier_semaphore()
        peers = [(self.g, self.up(s)) for s in range(1, self.line)]
        peers += [(flipped(self.g, m), self.z) for m in self.direct + [1]]
        for peer in peers:
            pl.semaphore_signal(semaphore, inc=1, device_id=peer, device_id_type=MESH)
        pl.semaphore_wait(semaphore, len(peers))


def remote(src, dst, send, recv, device):
    return pltpu.make_async_remote_copy(
        src_ref=src, dst_ref=dst, send_sem=send, recv_sem=recv, device_id=device, device_id_type=MESH
    )


class Gather:
    @staticmethod
    def sems(groups, line):
        chips = groups // 2
        return [DMA((line,))] * 2 + [DMA((chips, line))] * 4

    def __init__(self, at, shard, full, sems):
        self.at, self.shard, self.full = at, shard, full
        self.zs, self.zr, self.ds, self.dr, self.cs, self.cr = sems
        self.rows = shard.shape[0]

    def piece(self, mask, t):
        rows = pl.ds(pl.multiple_of(flipped(self.at.g, mask) * self.rows, 8), self.rows)
        return self.full.at[t, rows, :]

    def source(self, mask, k):
        own = mask == 0 and k == 0
        return self.shard if own else self.piece(mask, self.at.near(k))

    def local(self):
        return pltpu.make_async_copy(self.shard, self.piece(0, self.at.z), self.zr.at[self.at.z])

    def along(self, k):
        at = self.at
        t = at.near(k)
        return remote(
            self.shard, self.piece(0, at.z), self.zs.at[t], self.zr.at[at.z], (at.g, t)
        )

    def across(self, mask, k):
        at = self.at
        via, peer = 0, mask
        if at.square and mask == 6:
            via, peer = (2, 4) if k % 2 == 0 else (4, 2)
        t = at.near(k)
        m = mask // 2
        return remote(
            self.source(via, k), self.piece(via, t), self.ds.at[m, t], self.dr.at[m, t],
            (flipped(at.g, peer), at.z),
        )

    def core(self, mask, k):
        at = self.at
        t = at.near(k)
        m = mask // 2
        return remote(
            self.source(mask, k), self.piece(mask, t), self.cs.at[m, t], self.cr.at[m, t],
            (flipped(at.g, 1), at.z),
        )

    def arrived(self, mask, t, sem):
        piece = self.piece(mask, t)
        remote(piece, piece, sem, sem, (flipped(self.at.g, 1), self.at.z)).wait_recv()

    def start(self):
        self.local().start()
        for k in range(1, self.at.line):
            self.along(k).start()
        self.spread(0)

    def spread(self, k):
        at = self.at
        if k:
            t = at.near(k)
            self.arrived(0, t, self.zr.at[t])
        for mask in at.direct:
            self.across(mask, k).start()
        self.core(0, k).start()

    def passing(self, k):
        at = self.at
        t = at.near(k)
        for mask in at.direct:
            self.arrived(mask, t, self.dr.at[mask // 2, t])
            if at.square and mask == (2 if k % 2 == 0 else 4):
                self.across(6, k).start()
            self.core(mask, k).start()

    def last(self, k):
        at = self.at
        if at.square:
            t = at.near(k)
            self.arrived(6, t, self.dr.at[3, t])
            self.core(6, k).start()

    def finish(self):
        at = self.at
        for k in range(at.line):
            t = at.near(k)
            if k:
                self.along(k).wait_send()
            for mask in at.masks:
                self.arrived(mask ^ 1, t, self.cr.at[mask // 2, t])
                self.core(mask, k).wait_send()
                if mask:
                    self.across(mask, k).wait_send()
        self.local().wait()

    def steps(self):
        line = self.at.line
        out = []
        for i in range(line + 2):
            for work, k in ((self.spread, i), (self.passing, i - 1), (self.last, i - 2)):
                if 0 <= k < line:
                    out.append(functools.partial(work, k) if i else self.start)
        return out + [self.finish]


class ToOwner:
    @staticmethod
    def sems(groups, line):
        return [DMA((line,)), DMA((line,))]

    def __init__(self, at, rows, image, sems):
        self.at, self.rows, self.image = at, rows, image
        self.send, self.recv = sems
        self.count = rows.shape[0]

    def local(self):
        at = self.at
        return pltpu.make_async_copy(
            self.rows.at[jnp.minimum(at.image(at.z), self.count - 1)], self.image.at[at.z], self.send.at[0]
        )

    def copy(self, k, arriving=False):
        at = self.at
        to = at.near(k)
        src = self.rows.at[jnp.minimum(at.image(to), self.count - 1)]
        slot = to if arriving else at.z
        return remote(src, self.image.at[slot], self.send.at[k], self.recv.at[slot], (at.g, to))

    def start_one(self, k):
        at = self.at
        if k == 0:
            self.local().start()
        else:
            pl.when(at.image(at.near(k)) < self.count)(self.copy(k).start)

    def start(self):
        for k in range(self.at.line):
            self.start_one(k)

    def finish(self):
        at = self.at
        for k in range(1, at.line):
            pl.when(at.image(at.near(k)) < self.count)(self.copy(k).wait_send)
            pl.when(at.image(at.z) < self.count)(self.copy(k, True).wait_recv)
        self.local().wait()


class FromOwner:
    sems = ToOwner.sems

    def __init__(self, at, image, rows, sems):
        self.at, self.rows, self.image = at, rows, image
        self.send, self.recv = sems
        self.count = rows.shape[0]

    def local(self):
        at = self.at
        return pltpu.make_async_copy(
            self.image.at[at.z], self.rows.at[jnp.minimum(at.image(at.z), self.count - 1)], self.send.at[0]
        )

    def copy(self, k, arriving=False):
        at = self.at
        owner = at.down(k) if arriving else at.z
        dst = self.rows.at[jnp.minimum(at.image(owner), self.count - 1)]
        return remote(self.image.at[at.up(k)], dst, self.send.at[k], self.recv.at[k], (at.g, at.up(k)))

    def start_piece(self, p):
        at = self.at
        own = at.image(at.z) < self.count
        k = lax.rem(p - at.z + at.line, at.line)
        pl.when(own & (k == 0))(lambda: self.local().start())
        pl.when(own & (k > 0))(lambda: self.copy(k).start())

    def start(self):
        for p in range(self.at.line):
            self.start_piece(p)

    def finish(self):
        at = self.at

        @pl.when(at.image(at.z) < self.count)
        def _():
            for k in range(1, at.line):
                self.copy(k).wait_send()
            self.local().wait()

        for k in range(1, at.line):
            pl.when(at.image(at.down(k)) < self.count)(self.copy(k, True).wait_recv)


class Reduce:
    @staticmethod
    def scratch(groups, line, r, c, dtype):
        chips = groups // 2
        return [
            pltpu.VMEM((chips, line, r, c), dtype),
            pltpu.VMEM((chips, line, r, c), dtype),
            pltpu.VMEM((chips - 1, line, r, c), dtype),
            pltpu.VMEM((line, r, c), dtype),
        ] + [DMA((chips, line))] * 5 + [DMA((line,))] * 2

    def __init__(self, at, full, scratch, rows):
        self.at, self.full, self.rows, self.apart = at, full, rows, False
        self.cbuf, self.sums, self.dbuf, self.zbuf = scratch[:4]
        self.ls, self.cs, self.cr, self.ds, self.dr, self.zs, self.zr = scratch[4:]
        self.order = [6, 2, 4, 0] if at.square else at.masks[1:] + [0]

    def far(self, k):
        return self.at.near(self.at.line - 1 - k)

    def piece(self, mask, t):
        rows = pl.ds(pl.multiple_of(flipped(self.at.g, mask) * self.rows, 8), self.rows)
        return self.full.at[t, rows, :]

    def local(self, mask, t):
        m = mask // 2
        return pltpu.make_async_copy(self.piece(mask, t), self.sums.at[m, t], self.ls.at[m, t])

    def core(self, mask, t):
        at, m = self.at, mask // 2
        return remote(
            self.piece(mask ^ 1, t), self.cbuf.at[m, t], self.cs.at[m, t], self.cr.at[m, t],
            (flipped(at.g, 1), at.z),
        )

    def across(self, mask, k):
        at, m = self.at, mask // 2
        peer, t = mask, self.far(k)
        if at.square and mask == 6:
            peer = 4 if k % 2 == 0 else 2
        return remote(
            self.sums.at[m, t], self.dbuf.at[m - 1, t], self.ds.at[m, t], self.dr.at[m, t],
            (flipped(at.g, peer), at.z),
        )

    def along(self, t):
        at = self.at
        return remote(
            self.sums.at[0, t], self.zbuf.at[at.z], self.zs.at[t], self.zr.at[at.z], (at.g, t)
        )

    def add(self, m, t, other):
        self.sums[m, t] = self.sums[m, t] + other

    def begin(self, k):
        t = self.far(k)
        for mask in self.order:
            self.core(mask, t).start()
            self.local(mask, t).start()

    def pair(self, k):
        at = self.at
        t = self.far(k)
        for mask in self.order:
            m = mask // 2
            self.local(mask, t).wait()
            self.core(mask, t).wait_recv()
            self.add(m, t, self.cbuf[m, t])
            waits = at.square and mask == (2 if k % 2 == 0 else 4)
            if mask and not waits:
                self.across(mask, k).start()
        if k + 2 < at.line and not self.apart:
            self.begin(k + 2)

    def joined(self, k):
        at = self.at
        if at.square:
            mask = 2 if k % 2 == 0 else 4
            t = self.far(k)
            self.across(6, k).wait_recv()
            self.add(mask // 2, t, self.dbuf[2, t])
            self.across(mask, k).start()

    def own(self, k):
        at = self.at
        t = self.far(k)
        for mask in at.direct:
            self.across(mask, k).wait_recv()
            self.add(0, t, self.dbuf[mask // 2 - 1, t])
        if k < at.line - 1:
            self.along(t).start()

    def finish(self, out_ref):
        at = self.at
        total = self.sums[0, at.z].astype(f32)
        for k in range(1, at.line):
            t = at.near(k)
            buf, sem = self.zbuf.at[t], self.zr.at[t]
            remote(buf, buf, sem, sem, (flipped(at.g, 1), at.z)).wait_recv()
            total += self.zbuf[t].astype(f32)
        out_ref[...] = total
        for k in range(at.line):
            t = self.far(k)
            for mask in at.masks:
                self.core(mask, t).wait_send()
                if mask:
                    self.across(mask, k).wait_send()
            if k < at.line - 1:
                self.along(t).wait_send()

    def early(self):
        self.apart = True
        line = self.at.line
        out = []
        for i in range(line):
            todo = [functools.partial(self.begin, i)]
            for work, late in ((self.pair, 1), (self.joined, 3)):
                if i >= late:
                    todo.append(functools.partial(work, i - late))
            out.append(todo)
        return out

    def late(self):
        line = self.at.line
        out = [functools.partial(self.pair, line - 1)]
        done = max(line - 3, 0)
        for i in range(line):
            if done + i < line:
                out.append(functools.partial(self.joined, done + i))
            out.append(functools.partial(self.own, i))
        return out

    def start(self):
        self.begin(0)
        self.begin(1)

    def steps(self):
        line = self.at.line
        out = [self.start]
        for i in range(line + 4):
            for work, late in ((self.pair, 0), (self.joined, 2), (self.own, 4)):
                if 0 <= i - late < line:
                    out.append(functools.partial(work, i - late))
        return out


FWD = (3, 4, 7, 8, 8, 11, 12, 12, 15, 16)
COT = 4
ARRIVE = (0, 0, 1, 3)
FFC = 2
BACK = 6
BWD = (2, 2, 7, 7, 7, 7, 16, 16, 16, 16, 27, 27)


def run_ticks(ticks, step, part, parts):
    for at, work in ticks:
        if at % parts == part:
            pl.when(step == at // parts)(work)


def arrive_kernel(groups, line, x_ref, shard_ref, small_ref, xo_ref, full_ref, smalls_ref, *sems):
    at = Place(groups, line)
    n = len(Gather.sems(groups, line))
    rows = ToOwner(at, x_ref, xo_ref, sems[2 * n :])
    weights = Gather(at, shard_ref, full_ref, sems[:n])
    small = Gather(at, small_ref, smalls_ref, sems[n : 2 * n])
    at.barrier()
    for i, (one, two) in enumerate(zip(small.steps(), weights.steps())):
        one()
        two()
        for k in range(line):
            if ARRIVE[min(k, 3)] == i:
                rows.start_one(k)
    rows.finish()


def arrive(groups, line, x, shard, small):
    images, part_rows, width = x.shape
    return pl.pallas_call(
        functools.partial(arrive_kernel, groups, line),
        in_specs=[ANY] * 3,
        out_specs=[ANY] * 3,
        out_shape=[
            jax.ShapeDtypeStruct((line, part_rows, width), x.dtype),
            jax.ShapeDtypeStruct((line, groups * shard.shape[0], shard.shape[1]), shard.dtype),
            jax.ShapeDtypeStruct((line, groups * small.shape[0], small.shape[1]), small.dtype),
        ],
        scratch_shapes=Gather.sems(groups, line) * 2 + ToOwner.sems(groups, line),
        compiler_params=pltpu.CompilerParams(collective_id=1, has_side_effects=True),
        name="arrive",
    )(x, shard, small)


def leave_kernel(
    groups, line, gq_ref, gk_ref, gv_ref, w_ref, n1t_hbm, x_hbm, gh_hbm, v_ref, smalls_ref,
    yo_ref, shard_ref, small_ref, gn, y, full, smalls, sums, n1t_ref, x_ref, gh_ref, loads, *scratch
):
    at = Place(groups, line)
    n = len(ToOwner.sems(groups, line))
    m = (len(scratch) - n) // 2
    rows = FromOwner(at, y, yo_ref, scratch[:n])
    weights = Reduce(at, full, scratch[n : n + m], shard_ref.shape[0])
    small = Reduce(at, smalls, scratch[n + m :], small_ref.shape[0])
    step = pl.program_id(0)
    cols = gq_ref.shape[1]
    grads = (gq_ref, gk_ref, gv_ref)
    pairs = ((x_hbm, x_ref), (gh_hbm, gh_ref), (n1t_hbm, n1t_ref))
    copies = [pltpu.make_async_copy(a, b, loads.at[i]) for i, (a, b) in enumerate(pairs)]

    @pl.when(step == 0)
    def _():
        for copy in copies:
            copy.start()
        at.barrier()
        smalls[...] = smalls_ref[...]
        gn[...] = jnp.zeros_like(gn)

    @pl.when(step < line)
    def _():
        g = jnp.concatenate([ref[...] for ref in grads], axis=1)
        gn[...] += lax.dot_general(g, w_ref[0], NT, preferred_element_type=f32)

    @pl.when(step == line - 1)
    def _():
        part = x_ref.shape[1]
        copies[0].wait()
        copies[1].wait()
        sums[...] = jnp.zeros_like(sums)
        for p in range(line):

            def work(r, first, count, p=p):
                at_rows = slice(p * part + first, p * part + first + count)
                hat, inverse = norm_stats(x_ref[p, r].astype(f32))
                g = gn[at_rows, :]
                y[p, r] = (gh_ref[p, r] + norm_back(g, hat, inverse, v_ref[0:1])).astype(bf16)
                add_rows(sums, 0, g * hat)
                add_rows(sums, 8, g)

            work(slice(0, part), 0, part)
            rows.start_piece(p)
        carry = [jnp.sum(sums[8 * j : 8 * j + 8], axis=0, keepdims=True) for j in range(2)]
        wide = gn.shape[1] // groups
        for j, total in enumerate(carry):
            for g in range(groups):
                row = total[:, g * wide : (g + 1) * wide]
                if wide < LANES:
                    row = jnp.concatenate([row, jnp.zeros((1, LANES - wide), f32)], axis=1)
                at_row = g * small_ref.shape[0] + 2 * j
                for t in range(line):
                    smalls[t, at_row : at_row + 1, :] = row
        small.start()

    @pl.when(step == line)
    def _():
        copies[2].wait()

    @pl.when(step >= line)
    def _():
        t = weights.far(step - line)
        for i, ref in enumerate(grads):
            full[t, :, i * cols : (i + 1) * cols] = lax.dot_general(
                n1t_ref[...], ref[...], NN, preferred_element_type=f32
            ).astype(bf16)

    for i, todo in enumerate(weights.early()):

        @pl.when(step == line + i)
        def _(todo=todo):
            for work in todo:
                work()

    @pl.when(step == 2 * line - 1)
    def _():
        for work in small.steps()[1:]:
            work()
        for work in weights.late():
            work()
        weights.finish(shard_ref)
        small.finish(small_ref)
        rows.finish()


def leave(groups, line, images, gq, gk, gv, weights, n1t, x, ghid, vectors, smalls):
    _, part, width = x.shape
    rows = line * part
    cols = width // line
    r, c = width // groups, 3 * cols
    sr, sc = smalls.shape[1] // groups, smalls.shape[2]

    def column(j):
        far = Place(groups, line).near(jnp.clip(2 * line - 1 - j, 0, line - 1))
        return 0, jnp.where(j < line, j, far)

    grad = pl.BlockSpec((rows, cols), column)
    return pl.pallas_call(
        functools.partial(leave_kernel, groups, line),
        grid=(2 * line,),
        in_specs=[
            grad,
            grad,
            grad,
            pl.BlockSpec((1, width, c), lambda j: (jnp.minimum(j, line - 1), 0, 0)),
            ANY,
            ANY,
            ANY,
            whole(*vectors.shape),
            whole(*smalls.shape),
        ],
        out_specs=[ANY, whole(r, c), whole(sr, sc)],
        out_shape=[
            jax.ShapeDtypeStruct((images, part, width), bf16),
            jax.ShapeDtypeStruct((r, c), f32),
            jax.ShapeDtypeStruct((sr, sc), f32),
        ],
        scratch_shapes=[
            pltpu.VMEM((rows, width), f32),
            pltpu.VMEM((line, part, width), bf16),
            pltpu.VMEM((line, width, c), bf16),
            pltpu.VMEM(smalls.shape, f32),
            pltpu.VMEM((16, width), f32),
            pltpu.VMEM((width, rows), bf16),
            pltpu.VMEM((line, part, width), bf16),
            pltpu.VMEM((line, part, width), f32),
            DMA((3,)),
        ]
        + ToOwner.sems(groups, line)
        + Reduce.scratch(groups, line, r, c, bf16)
        + Reduce.scratch(groups, line, sr, sc, f32),
        compiler_params=pltpu.CompilerParams(
            collective_id=2, has_side_effects=True, vmem_limit_bytes=62 * 2**20
        ),
        name="leave",
    )(gq, gk, gv, weights, n1t, x, ghid, vectors, smalls)


def norm_stats(values):
    center = values - jnp.mean(values, axis=-1, keepdims=True)
    inverse = lax.rsqrt(jnp.mean(center * center, axis=-1, keepdims=True) + 1e-06)
    return center * inverse, inverse


def norm_back(grad_norm, normed, inverse, gain):
    scaled = grad_norm * gain
    return inverse * (
        scaled
        - jnp.mean(scaled, axis=-1, keepdims=True)
        - normed * jnp.mean(scaled * normed, axis=-1, keepdims=True)
    )


def project_kernel(flag_ref, x_ref, v_ref, w_ref, b_ref, out_ref, xc_ref, n1t_ref, n1):
    @pl.when(pl.program_id(0) == 0)
    def _():
        rows = x_ref.shape[0]
        size = rows // 2 if rows % 32 == 0 else rows
        for first in range(0, rows, size):
            r = slice(first, first + size)
            x = jnp.where(flag_ref[1] > 0, x_ref[r].astype(f32), 0.0)
            xc_ref[r] = x.astype(bf16)
            hat, _ = norm_stats(x)
            n1[r] = (hat * v_ref[0:1] + v_ref[2:3]).astype(bf16)

    cols = out_ref.shape[2]
    part = pl.ds(pl.multiple_of(pl.program_id(0) * cols, LANES), cols)
    n1t_ref[part, :] = n1[:, part].T
    for i in range(3):
        w = w_ref[0, :, i * cols : (i + 1) * cols]
        out = lax.dot_general(n1[...], w, NN, preferred_element_type=f32) + b_ref[i]
        if i == 0:
            out = out * (HD ** (-0.5) * LOG2E)
        out_ref[i] = out.astype(bf16)


def whole(*shape):
    return pl.BlockSpec(shape, lambda *_: (0,) * len(shape), pipeline_mode=pl.Buffered(1))


def add_rows(ref, first, x):
    ref[first : first + 1] += jnp.sum(x, axis=0, keepdims=True)


SMEM = pl.BlockSpec(memory_space=pltpu.SMEM)


def project(flags, x, vectors, weights, bias):
    rows, width = x.shape
    line = weights.shape[0]
    cols = width // line
    return pl.pallas_call(
        project_kernel,
        grid=(line,),
        in_specs=[
            SMEM,
            whole(rows, width),
            whole(*vectors.shape),
            pl.BlockSpec((1, width, 3 * cols), lambda t: (t, 0, 0)),
            pl.BlockSpec((3, 1, cols), lambda t: (0, 0, t)),
        ],
        out_specs=[
            pl.BlockSpec((3, rows, cols), lambda t: (0, 0, t)),
            whole(rows, width),
            whole(width, rows),
        ],
        out_shape=[
            jax.ShapeDtypeStruct((3, rows, width), bf16),
            jax.ShapeDtypeStruct((rows, width), bf16),
            jax.ShapeDtypeStruct((width, rows), bf16),
        ],
        scratch_shapes=[pltpu.VMEM((rows, width), bf16)],
        compiler_params=pltpu.CompilerParams(vmem_limit_bytes=62 * 2**20),
        cost_estimate=pl.CostEstimate(
            flops=6 * rows * width * width, bytes_accessed=16 * rows * width, transcendentals=0
        ),
        name="project",
    )(flags, x, vectors, weights, bias)


def valid_rows(flag_ref, shape):
    row = pl.program_id(0) * shape[0] + lax.broadcasted_iota(jnp.int32, shape, 0)
    return row < flag_ref[0]


def middle_kernel(flag_ref, ctx_ref, x_ref, cot_ref, v_ref, w_ref, hid_ref, n2_ref, gm_ref):
    line, _, cols = w_ref.shape
    attn = v_ref[6:7]
    for t in range(line):
        part = ctx_ref[0, :, t * cols : (t + 1) * cols]
        attn = attn + lax.dot_general(part, w_ref[t], NT, preferred_element_type=f32)
    hidden = x_ref[0].astype(f32) + v_ref[4:5] * attn
    hid_ref[0] = hidden
    hat, _ = norm_stats(hidden)
    n2_ref[0] = (hat * v_ref[1:2] + v_ref[3:4]).astype(bf16)
    gout = jnp.where(valid_rows(flag_ref, hidden.shape), cot_ref[0].astype(f32), 0.0)
    gm_ref[0] = (gout * v_ref[5:6]).astype(bf16)


def middle(flags, context, x, cot, vectors, weights):
    line, part, width = x.shape
    cols = width // line
    piece = pl.BlockSpec((1, part, width), lambda p: (p, 0, 0))
    return pl.pallas_call(
        middle_kernel,
        grid=(line,),
        in_specs=[
            SMEM,
            piece,
            piece,
            piece,
            whole(*vectors.shape),
            pl.BlockSpec(
                (line, width, cols), lambda p: (0, 0, 3), pipeline_mode=pl.Buffered(1)
            ),
        ],
        out_specs=[piece] * 3,
        out_shape=[
            jax.ShapeDtypeStruct(x.shape, f32),
            jax.ShapeDtypeStruct(x.shape, bf16),
            jax.ShapeDtypeStruct(x.shape, bf16),
        ],
        compiler_params=pltpu.CompilerParams(vmem_limit_bytes=62 * 2**20),
        name="middle",
    )(flags, context, x, cot, vectors, weights)


def turn_kernel(
    flag_ref, mlp_ref, gn_ref, hid_ref, x_ref, cot_ref, ctx_ref, v_ref, w_ref,
    out_ref, gh_ref, gc_ref, gw_ref, sum_ref, acc, gattn, sums
):
    step = pl.program_id(0)
    line, _, cols = w_ref.shape
    part = hid_ref.shape[1]

    @pl.when(step == 0)
    def _():
        sums[...] = jnp.zeros_like(sums)
        acc[...] = jnp.zeros_like(acc)

    def work(r, first, count):
        hidden = hid_ref[0, r]
        mlp = mlp_ref[0, r] + v_ref[7:8]
        gn = gn_ref[0, r]
        row = step * part + first + lax.broadcasted_iota(jnp.int32, hidden.shape, 0)
        valid = row < flag_ref[0]
        out_ref[0, r] = jnp.where(valid, hidden + v_ref[5:6] * mlp, 0.0).astype(bf16)
        gout = jnp.where(valid, cot_ref[0, r].astype(f32), 0.0)
        hat, inverse = norm_stats(hidden)
        ghid = gout + norm_back(gn, hat, inverse, v_ref[1:2])
        gh_ref[0, r] = ghid
        attn = (hidden - x_ref[0, r].astype(f32)) * (1.0 / v_ref[4:5])
        grad = ghid * v_ref[4:5]
        gattn[r] = grad.astype(bf16)
        terms = (gn * hat, gn, ghid * attn, gout * mlp, grad, gout * v_ref[5:6])
        for j, term in enumerate(terms):
            add_rows(sums, 8 * j, term)

    work(slice(0, part), 0, part)

    @pl.when(step == line - 1)
    def _():
        rows = [jnp.sum(sums[8 * j : 8 * j + 8], axis=0, keepdims=True) for j in range(6)]
        sum_ref[...] = jnp.concatenate(rows + [jnp.zeros((2, sums.shape[1]), f32)], axis=0)

    gattn_t = gattn[...].T
    for t in range(line):
        ctx = ctx_ref[0, :, t * cols : (t + 1) * cols]
        gc_ref[0, :, t * cols : (t + 1) * cols] = lax.dot_general(
            gattn[...], w_ref[t], NN, preferred_element_type=f32
        ).astype(bf16)
        acc[t] += lax.dot_general(gattn_t, ctx, NN, preferred_element_type=f32)

    @pl.when(step == line - 1)
    def _():
        gw_ref[...] = acc[...].astype(bf16)


def turn(flags, mlp, gn, hidden, x, cot, context, vectors, weights):
    line, part, width = x.shape
    cols = width // line
    piece = pl.BlockSpec((1, part, width), lambda p: (p, 0, 0))
    return pl.pallas_call(
        turn_kernel,
        grid=(line,),
        in_specs=[SMEM]
        + [piece] * 6
        + [
            whole(*vectors.shape),
            pl.BlockSpec(
                (line, width, cols), lambda p: (0, 0, 3), pipeline_mode=pl.Buffered(1)
            ),
        ],
        out_specs=[piece] * 3 + [whole(line, width, cols), whole(8, width)],
        out_shape=[
            jax.ShapeDtypeStruct(x.shape, bf16),
            jax.ShapeDtypeStruct(x.shape, f32),
            jax.ShapeDtypeStruct(x.shape, bf16),
            jax.ShapeDtypeStruct((line, width, cols), bf16),
            jax.ShapeDtypeStruct((8, width), f32),
        ],
        scratch_shapes=[
            pltpu.VMEM((line, width, cols), f32),
            pltpu.VMEM((part, width), bf16),
            pltpu.VMEM((48, width), f32),
        ],
        compiler_params=pltpu.CompilerParams(vmem_limit_bytes=62 * 2**20),
        name="turn",
    )(flags, mlp, gn, hidden, x, cot, context, vectors, weights)


def attend_forward_kernel(
    groups, line, rows, padded, len_ref, q_ref, k_ref, v_ref, shard_ref, cot_ref,
    ctx_ref, qa_ref, full_ref, coto_ref, ka, va, *sems
):
    at = Place(groups, line)
    n = len(Gather.sems(groups, line))
    weights = Gather(at, shard_ref, full_ref, sems[:n])
    cot = ToOwner(at, cot_ref, coto_ref, sems[n:])
    steps = weights.steps()

    def begin():
        at.barrier()
        steps[0]()

    ticks = [(0, begin), (COT, cot.start)]
    for i, work in enumerate(steps[1:]):
        ticks.append((FWD[min(i, len(FWD) - 1)], work))
    step = pl.program_id(0)
    length = len_ref[0]
    lane = lax.broadcasted_iota(jnp.int32, (padded, LANES), 1)
    row = lax.broadcasted_iota(jnp.int32, (padded, LANES), 0)
    lb = lane[:rows]
    if padded > rows:
        va[rows:] = jnp.zeros((padded - rows, LANES), bf16)
    for half in range(2):
        run_ticks(ticks, step, half, 2)
        own = (lb < HD) if half == 0 else (lb >= HD)
        spare = HD if half == 0 else 0
        ka[:rows] = keys_with_bias(k_ref[...].astype(f32), lb, row[:rows], length, own, spare)
        if padded > rows:
            ka[rows:] = jnp.where(lane[rows:] == spare + 3, NEG, 0.0).astype(bf16)
        va[:rows] = jnp.where(
            own, v_ref[...].astype(f32), jnp.where(lb == spare, 1.0, 0.0)
        ).astype(bf16)
        qa = jnp.where(own, q_ref[...].astype(f32), jnp.where(lb == spare + 3, 1.0, 0.0))
        s = lax.dot_general(qa.astype(bf16), ka[...], NT, preferred_element_type=f32)
        m = jnp.max(s, axis=1, keepdims=True)
        p = jnp.exp2(s - m).astype(bf16)
        o = lax.dot_general(p, va[...], NN, preferred_element_type=f32)
        total = o[:, spare : spare + 1]
        o = o / total
        hi, mid, lo = parts(-(m + jnp.log2(total)))
        if half == 0:
            ctx_ref[...] = o.astype(bf16)
        else:
            ctx_ref[...] = jnp.where(own, o, ctx_ref[...].astype(f32)).astype(bf16)
        stats = jnp.where(lb == spare + 2, lo, qa)
        stats = jnp.where(lb == spare + 1, mid, stats)
        qa_ref[half] = jnp.where(lb == spare, hi, stats).astype(bf16)

    @pl.when(step == pl.num_programs(0) - 1)
    def _():
        for at_tick, work in ticks:
            if at_tick > 15:
                work()
        cot.finish()


def attend_forward(groups, line, length, qkv, shard, cot):
    _, rows, width = qkv.shape
    padded = round_up(rows, LANES)
    spec = pl.BlockSpec((rows, LANES), lambda j: (0, j))

    def third(n):
        return pl.BlockSpec((None, rows, LANES), lambda j: (n, 0, j))

    return pl.pallas_call(
        functools.partial(attend_forward_kernel, groups, line, rows, padded),
        grid=(width // LANES,),
        in_specs=[pl.BlockSpec(memory_space=pltpu.SMEM), third(0), third(1), third(2), ANY, ANY],
        out_specs=[spec, pl.BlockSpec((2, rows, LANES), lambda j: (j, 0, 0)), ANY, ANY],
        out_shape=[
            jax.ShapeDtypeStruct((rows, width), bf16),
            jax.ShapeDtypeStruct((width // HD, rows, LANES), bf16),
            jax.ShapeDtypeStruct((line, groups * shard.shape[0], shard.shape[1]), shard.dtype),
            jax.ShapeDtypeStruct((line,) + cot.shape[1:], cot.dtype),
        ],
        scratch_shapes=[pltpu.VMEM((padded, LANES), bf16), pltpu.VMEM((padded, LANES), bf16)]
        + Gather.sems(groups, line)
        + ToOwner.sems(groups, line),
        compiler_params=pltpu.CompilerParams(
            collective_id=3, has_side_effects=True, vmem_limit_bytes=62 * 2**20
        ),
        cost_estimate=pl.CostEstimate(
            flops=16 * rows * rows * width,
            bytes_accessed=12 * rows * width,
            transcendentals=rows * rows * width // HD,
        ),
        name="attend_forward",
    )(length, qkv, qkv, qkv, shard, cot)


def attend_backward_kernel(
    groups, line, rows, padded, blocks, len_ref, qa_ref, k_ref, v_ref, gc_ref, ctx_ref, y_ref, full_ref,
    out_ref, gq_ref, gk_ref, gv_ref, gb_ref, yo_ref, shard_ref, oshard_ref, ka, va, qs, ga, acc, *scratch
):
    at = Place(groups, line)
    n = len(ToOwner.sems(groups, line))
    back = FromOwner(at, y_ref, yo_ref, scratch[:n])
    m = (len(scratch) - n) // 2
    weights = Reduce(at, full_ref, scratch[n : n + m], shard_ref.shape[0])
    out_weights = Reduce(at, out_ref, scratch[n + m :], oshard_ref.shape[0])
    pairs = list(zip(weights.steps(), out_weights.steps()))

    def both(i):
        def run():
            for work in pairs[i]:
                work()

        return run

    steps = [both(i) for i in range(len(pairs))]

    def begin():
        at.barrier()
        steps[0]()

    ticks = [(0, begin), (BACK * blocks // 2, back.start)]
    for i, work in enumerate(steps[1:]):
        ticks.append((BWD[min(i, len(BWD) - 1)] * blocks // 2, work))
    step = pl.program_id(0)
    length = len_ref[0]
    lane = lax.broadcasted_iota(jnp.int32, (padded, LANES), 1)
    row = lax.broadcasted_iota(jnp.int32, (padded, LANES), 0)
    size = rows // blocks
    ls = lane[:rows]
    for half in range(2):
        own = (ls < HD) if half == 0 else (ls >= HD)
        spare = HD if half == 0 else 0
        ownb = own[:size]
        gc = gc_ref[...].astype(f32)
        corr = jnp.sum(
            jnp.where(own, gc * ctx_ref[...].astype(f32), 0.0), axis=1, keepdims=True
        )
        hi, mid, lo = parts(-corr)
        extra = jnp.where(ls == spare + 1, mid, jnp.where(ls == spare + 2, lo, 0.0))
        ga[:rows] = jnp.where(own, gc, jnp.where(ls == spare, hi, extra)).astype(bf16)
        qs[:rows] = qa_ref[half]
        if padded > rows:
            ga[rows:] = jnp.zeros((padded - rows, LANES), bf16)
            qs[rows:] = jnp.where(lane[rows:] == spare, NEG, 0.0).astype(bf16)
        ka[...] = keys_with_bias(k_ref[...].astype(f32), ls, row[:rows], length, own, spare)
        ones = jnp.where((ls >= spare) & (ls < spare + 3), 1.0, 0.0)
        va[...] = jnp.where(own, v_ref[...].astype(f32), ones).astype(bf16)
        bv = jnp.zeros((1, LANES), f32)
        for b in range(blocks):
            run_ticks(ticks, step, half * blocks + b, 2 * blocks)
            r = slice(b * size, (b + 1) * size)
            kb = ka[r]
            p = jnp.exp2(lax.dot_general(kb, qs[...], NT, preferred_element_type=f32))
            gp = lax.dot_general(va[r], ga[...], NT, preferred_element_type=f32)
            ds = (p * gp).astype(bf16)
            gv = lax.dot_general(p.astype(bf16), ga[...], NN, preferred_element_type=f32)
            gk = lax.dot_general(ds, qs[...], NN, preferred_element_type=f32) * (1.0 / LOG2E)
            gqt = lax.dot_general(kb.T, ds, NN, preferred_element_type=f32)
            acc[...] = gqt if b == 0 else acc[...] + gqt
            bv += jnp.sum(gv, axis=0, keepdims=True)
            if half == 0:
                gv_ref[r] = gv.astype(bf16)
                gk_ref[r] = gk.astype(bf16)
            else:
                gv_ref[r] = jnp.where(ownb, gv, gv_ref[r].astype(f32)).astype(bf16)
                gk_ref[r] = jnp.where(ownb, gk, gk_ref[r].astype(f32)).astype(bf16)
        gq = acc[...].T[:rows] * HD ** (-0.5)
        sums = jnp.concatenate(
            [jnp.sum(gq, axis=0, keepdims=True), bv, jnp.zeros((6, LANES), f32)], axis=0
        )
        if half == 0:
            gb_ref[0] = sums
        else:
            gb_ref[0] = jnp.where(own[:8], sums, gb_ref[0])
        if half == 0:
            gq_ref[...] = gq.astype(bf16)
        else:
            gq_ref[...] = jnp.where(own, gq, gq_ref[...].astype(f32)).astype(bf16)

    @pl.when(step == pl.num_programs(0) - 1)
    def _():
        for at_tick, work in ticks:
            if at_tick >= 2 * blocks * 8:
                work()
        weights.finish(shard_ref)
        out_weights.finish(oshard_ref)
        back.finish()


def attend_backward(groups, line, images, length, qa, qkv, gc, ctx, y, full, out_full):
    _, rows, width = qkv.shape
    padded = round_up(rows, LANES)
    blocks = 2 if rows % 32 == 0 else 1
    spec = pl.BlockSpec((rows, LANES), lambda j: (0, j))
    r, c, oc = full.shape[1] // groups, full.shape[2], out_full.shape[2]

    def third(n):
        return pl.BlockSpec((None, rows, LANES), lambda j: (n, 0, j))

    return pl.pallas_call(
        functools.partial(attend_backward_kernel, groups, line, rows, padded, blocks),
        grid=(width // LANES,),
        in_specs=[
            pl.BlockSpec(memory_space=pltpu.SMEM),
            pl.BlockSpec((2, rows, LANES), lambda j: (j, 0, 0)),
            third(1),
            third(2),
            spec,
            spec,
            ANY,
            ANY,
            ANY,
        ],
        out_specs=[spec] * 3
        + [pl.BlockSpec((1, 8, LANES), lambda j: (j, 0, 0)), ANY, whole(r, c), whole(r, oc)],
        out_shape=[jax.ShapeDtypeStruct((rows, width), bf16)] * 3
        + [
            jax.ShapeDtypeStruct((width // LANES, 8, LANES), f32),
            jax.ShapeDtypeStruct((images,) + y.shape[1:], y.dtype),
            jax.ShapeDtypeStruct((r, c), f32),
            jax.ShapeDtypeStruct((r, oc), f32),
        ],
        scratch_shapes=[
            pltpu.VMEM((rows, LANES), bf16),
            pltpu.VMEM((rows, LANES), bf16),
            pltpu.VMEM((padded, LANES), bf16),
            pltpu.VMEM((padded, LANES), bf16),
            pltpu.VMEM((LANES, padded), f32),
        ]
        + ToOwner.sems(groups, line)
        + Reduce.scratch(groups, line, r, c, full.dtype)
        + Reduce.scratch(groups, line, r, oc, full.dtype),
        compiler_params=pltpu.CompilerParams(
            collective_id=4, has_side_effects=True, vmem_limit_bytes=62 * 2**20
        ),
        cost_estimate=pl.CostEstimate(
            flops=40 * rows * rows * width,
            bytes_accessed=16 * rows * width,
            transcendentals=rows * rows * width // HD,
        ),
        name="attend_backward",
    )(length, qa, qkv, qkv, gc, ctx, y, full, out_full)


def feed_forward_kernel(
    tile, chunks, n2_ref, gm_ref, w_ref, b1_ref, mlp_ref, gn_ref, gw_ref, gb_ref, n2t, gmt, act_s, gpre_s
):
    @pl.when(pl.program_id(0) == 0)
    def _():
        n2t[...] = n2_ref[...].T
        gmt[...] = gm_ref[...].T
        mlp_ref[...] = jnp.zeros_like(mlp_ref)
        gn_ref[...] = jnp.zeros_like(gn_ref)

    w1 = w_ref[0, :, :tile]
    w2t = w_ref[0, :, tile:]
    size = n2_ref.shape[0] // chunks
    for c in range(chunks):
        r = slice(c * size, (c + 1) * size)
        pre = lax.dot_general(n2_ref[r], w1, NN, preferred_element_type=f32) + b1_ref[...]
        gact = lax.dot_general(gm_ref[r], w2t, NN, preferred_element_type=f32)
        cdf = 0.5 * (1.0 + lax.erf(pre * (1 / math.sqrt(2))))
        act_s[r] = (pre * cdf).astype(bf16)
        pdf = jnp.exp2(pre * pre * (-0.5 * LOG2E)) * (1 / math.sqrt(2 * math.pi))
        gpre = gact * (cdf + pre * pdf)
        total = jnp.sum(gpre, axis=0, keepdims=True)
        gb_ref[...] = total if c == 0 else gb_ref[...] + total
        gpre_s[r] = gpre.astype(bf16)
        mlp_ref[r] += lax.dot_general(act_s[r], w2t, NT, preferred_element_type=f32)
        gn_ref[r] += lax.dot_general(gpre_s[r], w1, NT, preferred_element_type=f32)
    gw_ref[0, :, :tile] = lax.dot_general(
        n2t[...], gpre_s[...], NN, preferred_element_type=f32
    ).astype(bf16)
    gw_ref[0, :, tile:] = lax.dot_general(
        gmt[...], act_s[...], NN, preferred_element_type=f32
    ).astype(bf16)


def feed_forward(n2, gm, weights, b1, tile):
    rows, width = n2.shape
    units = b1.shape[1]
    per = weights.shape[2] // (2 * tile)

    both = pl.BlockSpec((1, width, 2 * tile), lambda j: (j // per, 0, j % per))
    return pl.pallas_call(
        functools.partial(feed_forward_kernel, tile, FFC if rows % (16 * FFC) == 0 else 1),
        grid=(units // tile,),
        in_specs=[
            whole(rows, width),
            whole(rows, width),
            both,
            pl.BlockSpec((1, tile), lambda j: (0, j)),
        ],
        out_specs=[
            whole(rows, width),
            whole(rows, width),
            both,
            pl.BlockSpec((1, tile), lambda j: (0, j)),
        ],
        out_shape=[
            jax.ShapeDtypeStruct((rows, width), f32),
            jax.ShapeDtypeStruct((rows, width), f32),
            jax.ShapeDtypeStruct(weights.shape, bf16),
            jax.ShapeDtypeStruct((1, units), f32),
        ],
        scratch_shapes=[pltpu.VMEM((width, rows), bf16)] * 2 + [pltpu.VMEM((rows, tile), bf16)] * 2,
        compiler_params=pltpu.CompilerParams(vmem_limit_bytes=62 * 2**20),
        cost_estimate=pl.CostEstimate(
            flops=16 * rows * width * units,
            bytes_accessed=8 * width * units,
            transcendentals=2 * rows * units,
        ),
        name="feed_forward",
    )(n2, gm, weights, b1)


def body(
    block_input,
    cotangent,
    lengths,
    w_qkv,
    b_qv,
    w_out,
    w_fc1,
    b_fc1,
    w_fc2,
    ln_gain,
    ln_shift,
    layer_scale,
    out_bias,
):
    images, part_rows, width = block_input.shape
    groups = lax.axis_size("dp")
    line = lax.axis_size("tensor")
    rows = part_rows * line
    group = lax.axis_index("dp")
    place = lax.axis_index("tensor")
    mine = place + (group % 2) * (line - 1 - 2 * place)
    active = mine < images

    tile = min(512, w_fc1.shape[1])
    qkv_out = jnp.concatenate([w_qkv[0], w_qkv[1], w_qkv[2], w_out.T], axis=1)
    w_fc2_t = w_fc2.T
    fc_both = jnp.concatenate(
        [
            w[:, at : at + tile]
            for at in range(0, w_fc1.shape[1], tile)
            for w in (w_fc1, w_fc2_t)
        ],
        axis=1,
    )

    def lanes(x):
        return jnp.pad(x, ((0, 0), (0, LANES - x.shape[1])))

    own_width = ln_gain.shape[1]
    _, bq_rows, bq_cols = b_qv.shape
    f_rows, f_cols = b_fc1.shape
    small = jnp.concatenate([ln_gain, ln_shift, layer_scale, out_bias], axis=0)
    small = [small, b_qv.reshape(-1, bq_cols).astype(f32), b_fc1.astype(f32)]
    small = jnp.concatenate([lanes(x) for x in small], axis=0)
    small_rows = round_up(small.shape[0], 8)
    small = jnp.pad(small, ((0, small_rows - small.shape[0]), (0, 0)))
    b_at = 8 + 2 * bq_rows

    x_all, weights, small = arrive(groups, line, block_input, qkv_out, small)
    small = small.reshape(line, groups, small_rows, LANES)
    vectors = jnp.transpose(small[:, :, :8, :own_width], (2, 1, 0, 3)).reshape(8, width)
    qv_bias = jnp.transpose(
        small[:, :, 8:b_at, :bq_cols].reshape(line, groups, 2, bq_rows, bq_cols), (2, 0, 4, 1, 3)
    ).reshape(2, 1, width)
    fc1_bias = jnp.transpose(
        small[:, :, b_at : b_at + f_rows, :f_cols], (0, 3, 1, 2)
    ).reshape(1, -1)

    length = jnp.where(active, lengths[jnp.minimum(mine, images - 1)], 0).astype(jnp.int32)
    flags = jnp.stack([length, active.astype(jnp.int32)])
    pieces = (line, part_rows, width)

    zero = jnp.zeros((1, 1, width), f32)
    qkv, x_all, normed1_t = project(
        flags,
        x_all.reshape(rows, width),
        vectors,
        weights,
        jnp.concatenate([qv_bias[:1], zero, qv_bias[1:]]),
    )
    x_all = x_all.reshape(pieces)
    context, query_stats, fc_weights, cot = attend_forward(
        groups, line, flags, qkv, fc_both, cotangent
    )
    context3 = context.reshape(pieces)
    hidden, normed2, grad_mlp = middle(flags, context3, x_all, cot, vectors, weights)
    mlp, grad_normed2, grad_fc, grad_bfc1 = feed_forward(
        normed2.reshape(rows, width), grad_mlp.reshape(rows, width), fc_weights, fc1_bias, tile
    )
    block_out, grad_hidden, grad_context, grad_wout, sums = turn(
        flags,
        mlp.reshape(pieces),
        grad_normed2.reshape(pieces),
        hidden,
        x_all,
        cot,
        context3,
        vectors,
        weights,
    )
    grad_query, grad_key, grad_value, grad_bqv, block_out, shard_fc, shard_wout = attend_backward(
        groups,
        line,
        images,
        flags,
        query_stats,
        qkv,
        grad_context.reshape(rows, width),
        context,
        block_out,
        grad_fc,
        grad_wout,
    )

    wide = width // groups
    none = jnp.zeros((1, width), f32)
    by_vector = jnp.concatenate(
        [none, sums[0:1], none, sums[1:2], sums[2:6]], axis=0
    ).reshape(8, groups, wide)
    by_vector = jnp.pad(jnp.transpose(by_vector, (1, 0, 2)), ((0, 0), (0, 0), (0, LANES - wide)))
    by_vector = jnp.broadcast_to(by_vector[None], (line, groups, 8, LANES))
    by_head = jnp.transpose(grad_bqv[:, :2], (1, 0, 2)).reshape(2, line, bq_cols, groups, bq_rows)
    by_head = jnp.transpose(by_head, (1, 3, 0, 4, 2)).reshape(line, groups, 2 * bq_rows, bq_cols)
    by_unit = jnp.transpose(grad_bfc1.reshape(line, f_cols, groups, f_rows), (0, 2, 3, 1))

    def wider(x):
        return jnp.pad(x, ((0, 0), (0, 0), (0, 0), (0, LANES - x.shape[3])))

    smalls = jnp.concatenate([by_vector, wider(by_head), wider(by_unit)], axis=2)
    smalls = jnp.pad(smalls, ((0, 0), (0, 0), (0, small_rows - smalls.shape[2]), (0, 0)))
    grad_input, shard_weights, shard_small = leave(
        groups,
        line,
        images,
        grad_query,
        grad_key,
        grad_value,
        weights,
        normed1_t,
        x_all,
        grad_hidden,
        vectors,
        smalls.reshape(line, groups * small_rows, LANES),
    )
    grad_input = grad_input.astype(f32)
    cols = width // line
    shard_wqkv = jnp.stack([shard_weights[:, n * cols : (n + 1) * cols] for n in range(3)])
    shard_wout = shard_wout.T
    shard_fc1, shard_fc2 = (
        jnp.concatenate(
            [
                shard_fc[:, at : at + tile]
                for at in range(first, shard_fc.shape[1], 2 * tile)
            ],
            axis=1,
        )
        for first in (0, tile)
    )
    shard_fc2 = shard_fc2.T
    own = lax.dynamic_slice_in_dim(shard_small[:8], place * own_width, own_width, 1)
    shard_gain, shard_shift, shard_scale, shard_bias = (own[2 * n : 2 * n + 2] for n in range(4))
    shard_bqv = shard_small[8:b_at, :bq_cols].reshape(b_qv.shape)
    shard_bfc1 = shard_small[b_at : b_at + f_rows, :f_cols]
    return (
        block_out,
        grad_input,
        shard_wqkv,
        shard_bqv,
        shard_wout,
        shard_fc1,
        shard_bfc1,
        shard_fc2,
        shard_gain,
        shard_shift,
        shard_scale,
        shard_bias,
    )


def solution(mesh):
    rows = P("dp", "tensor", None)
    vector = P(None, ("dp", "tensor"))
    weights = (
        P(None, "dp", "tensor"),
        P(None, "dp", "tensor"),
        P("tensor", "dp"),
        P("dp", "tensor"),
        P("dp", "tensor"),
        P("tensor", "dp"),
    )
    return jax.shard_map(
        body,
        mesh=mesh,
        in_specs=(rows, rows, P("dp")) + weights + (vector,) * 4,
        out_specs=(rows, rows) + weights + (vector,) * 4,
        check_vma=False,
    )
```

```python
import functools
import math

import jax
import jax.numpy as jnp
from jax import lax
from jax.experimental import pallas as pl
from jax.experimental.pallas import tpu as pltpu
from jax.sharding import PartitionSpec as P

HD = 64
LANES = 128
LOG2E = math.log2(math.e)
NEG = -1e30
NT = (((1,), (1,)), ((), ()))
NN = (((1,), (0,)), ((), ()))
f32 = jnp.float32
bf16 = jnp.bfloat16


def round_up(n, m):
    return (n + m - 1) // m * m


def parts(x):
    hi = x.astype(bf16).astype(f32)
    rest = x - hi
    mid = rest.astype(bf16).astype(f32)
    return hi, mid, rest - mid


def keys_with_bias(keys, lane, row, length, own, spare):
    bias = jnp.where(row < length, 0.0, NEG)
    ones = jnp.where((lane >= spare) & (lane < spare + 3), 1.0, 0.0)
    return jnp.where(own, keys, jnp.where(lane == spare + 3, bias, ones)).astype(bf16)


MESH = pl.DeviceIdType.MESH
ANY = pl.BlockSpec(memory_space=pl.ANY)
DMA = pltpu.SemaphoreType.DMA


def flipped(g, mask):
    bit = 1
    while bit <= mask:
        if mask & bit:
            g = g + bit * (1 - 2 * ((g // bit) % 2))
        bit *= 2
    return g


class Place:
    def __init__(self, groups, line):
        self.groups, self.line = groups, line
        self.g, self.z = lax.axis_index("dp"), lax.axis_index("tensor")
        self.masks = list(range(0, groups, 2))
        self.square = groups == 8
        self.direct = [2, 4] if self.square else self.masks[1:]

    def image(self, z):
        odd = self.g % 2
        return z + odd * (self.line - 1 - 2 * z)

    def near(self, k):
        place = 0
        if not isinstance(k, int):
            for i in range(self.line):
                place = jnp.where(k == i, self.near(i), place)
            return place
        for z in range(self.line):
            order = sorted(range(self.line), key=lambda t: (abs(t - z), t))
            place = jnp.where(self.z == z, order[k], place)
        return place

    def up(self, k):
        return lax.rem(self.z + k, self.line)

    def down(self, k):
        return lax.rem(self.z + self.line - k, self.line)

    def barrier(self):
        semaphore = pltpu.get_barrier_semaphore()
        peers = [(self.g, self.up(s)) for s in range(1, self.line)]
        peers += [(flipped(self.g, m), self.z) for m in self.direct + [1]]
        for peer in peers:
            pl.semaphore_signal(semaphore, inc=1, device_id=peer, device_id_type=MESH)
        pl.semaphore_wait(semaphore, len(peers))


def remote(src, dst, send, recv, device):
    return pltpu.make_async_remote_copy(
        src_ref=src, dst_ref=dst, send_sem=send, recv_sem=recv, device_id=device, device_id_type=MESH
    )


class Gather:
    @staticmethod
    def sems(groups, line):
        chips = groups // 2
        return [DMA((line,))] * 2 + [DMA((chips, line))] * 4

    def __init__(self, at, shard, full, sems):
        self.at, self.shard, self.full = at, shard, full
        self.zs, self.zr, self.ds, self.dr, self.cs, self.cr = sems
        self.rows = shard.shape[0]

    def piece(self, mask, t):
        rows = pl.ds(pl.multiple_of(flipped(self.at.g, mask) * self.rows, 8), self.rows)
        return self.full.at[t, rows, :]

    def source(self, mask, k):
        own = mask == 0 and k == 0
        return self.shard if own else self.piece(mask, self.at.near(k))

    def local(self):
        return pltpu.make_async_copy(self.shard, self.piece(0, self.at.z), self.zr.at[self.at.z])

    def along(self, k):
        at = self.at
        t = at.near(k)
        return remote(
            self.shard, self.piece(0, at.z), self.zs.at[t], self.zr.at[at.z], (at.g, t)
        )

    def across(self, mask, k):
        at = self.at
        via, peer = 0, mask
        if at.square and mask == 6:
            via, peer = (2, 4) if k % 2 == 0 else (4, 2)
        t = at.near(k)
        m = mask // 2
        return remote(
            self.source(via, k), self.piece(via, t), self.ds.at[m, t], self.dr.at[m, t],
            (flipped(at.g, peer), at.z),
        )

    def core(self, mask, k):
        at = self.at
        t = at.near(k)
        m = mask // 2
        return remote(
            self.source(mask, k), self.piece(mask, t), self.cs.at[m, t], self.cr.at[m, t],
            (flipped(at.g, 1), at.z),
        )

    def arrived(self, mask, t, sem):
        piece = self.piece(mask, t)
        remote(piece, piece, sem, sem, (flipped(self.at.g, 1), self.at.z)).wait_recv()

    def start(self):
        self.local().start()
        for k in range(1, self.at.line):
            self.along(k).start()
        self.spread(0)

    def spread(self, k):
        at = self.at
        if k:
            t = at.near(k)
            self.arrived(0, t, self.zr.at[t])
        for mask in at.direct:
            self.across(mask, k).start()
        self.core(0, k).start()

    def passing(self, k):
        at = self.at
        t = at.near(k)
        for mask in at.direct:
            self.arrived(mask, t, self.dr.at[mask // 2, t])
            if at.square and mask == (2 if k % 2 == 0 else 4):
                self.across(6, k).start()
            self.core(mask, k).start()

    def last(self, k):
        at = self.at
        if at.square:
            t = at.near(k)
            self.arrived(6, t, self.dr.at[3, t])
            self.core(6, k).start()

    def finish(self):
        at = self.at
        for k in range(at.line):
            t = at.near(k)
            if k:
                self.along(k).wait_send()
            for mask in at.masks:
                self.arrived(mask ^ 1, t, self.cr.at[mask // 2, t])
                self.core(mask, k).wait_send()
                if mask:
                    self.across(mask, k).wait_send()
        self.local().wait()

    def steps(self):
        line = self.at.line
        out = []
        for i in range(line + 2):
            for work, k in ((self.spread, i), (self.passing, i - 1), (self.last, i - 2)):
                if 0 <= k < line:
                    out.append(functools.partial(work, k) if i else self.start)
        return out + [self.finish]


class ToOwner:
    @staticmethod
    def sems(groups, line):
        return [DMA((line,)), DMA((line,))]

    def __init__(self, at, rows, image, sems):
        self.at, self.rows, self.image = at, rows, image
        self.send, self.recv = sems
        self.count = rows.shape[0]

    def local(self):
        at = self.at
        return pltpu.make_async_copy(
            self.rows.at[jnp.minimum(at.image(at.z), self.count - 1)], self.image.at[at.z], self.send.at[0]
        )

    def copy(self, k, arriving=False):
        at = self.at
        to = at.near(k)
        src = self.rows.at[jnp.minimum(at.image(to), self.count - 1)]
        slot = to if arriving else at.z
        return remote(src, self.image.at[slot], self.send.at[k], self.recv.at[slot], (at.g, to))

    def start_one(self, k):
        at = self.at
        if k == 0:
            self.local().start()
        else:
            pl.when(at.image(at.near(k)) < self.count)(self.copy(k).start)

    def start(self):
        for k in range(self.at.line):
            self.start_one(k)

    def finish(self):
        at = self.at
        for k in range(1, at.line):
            pl.when(at.image(at.near(k)) < self.count)(self.copy(k).wait_send)
            pl.when(at.image(at.z) < self.count)(self.copy(k, True).wait_recv)
        self.local().wait()


class FromOwner:
    sems = ToOwner.sems

    def __init__(self, at, image, rows, sems):
        self.at, self.rows, self.image = at, rows, image
        self.send, self.recv = sems
        self.count = rows.shape[0]

    def local(self):
        at = self.at
        return pltpu.make_async_copy(
            self.image.at[at.z], self.rows.at[jnp.minimum(at.image(at.z), self.count - 1)], self.send.at[0]
        )

    def copy(self, k, arriving=False):
        at = self.at
        owner = at.down(k) if arriving else at.z
        dst = self.rows.at[jnp.minimum(at.image(owner), self.count - 1)]
        return remote(self.image.at[at.up(k)], dst, self.send.at[k], self.recv.at[k], (at.g, at.up(k)))

    def start_piece(self, p):
        at = self.at
        own = at.image(at.z) < self.count
        k = lax.rem(p - at.z + at.line, at.line)
        pl.when(own & (k == 0))(lambda: self.local().start())
        pl.when(own & (k > 0))(lambda: self.copy(k).start())

    def start(self):
        for p in range(self.at.line):
            self.start_piece(p)

    def finish(self):
        at = self.at

        @pl.when(at.image(at.z) < self.count)
        def _():
            for k in range(1, at.line):
                self.copy(k).wait_send()
            self.local().wait()

        for k in range(1, at.line):
            pl.when(at.image(at.down(k)) < self.count)(self.copy(k, True).wait_recv)


class Reduce:
    @staticmethod
    def scratch(groups, line, r, c, dtype):
        chips = groups // 2
        return [
            pltpu.VMEM((chips, line, r, c), dtype),
            pltpu.VMEM((chips, line, r, c), dtype),
            pltpu.VMEM((chips - 1, line, r, c), dtype),
            pltpu.VMEM((line, r, c), dtype),
        ] + [DMA((chips, line))] * 5 + [DMA((line,))] * 2

    def __init__(self, at, full, scratch, rows):
        self.at, self.full, self.rows, self.apart = at, full, rows, False
        self.cbuf, self.sums, self.dbuf, self.zbuf = scratch[:4]
        self.ls, self.cs, self.cr, self.ds, self.dr, self.zs, self.zr = scratch[4:]
        self.order = [6, 2, 4, 0] if at.square else at.masks[1:] + [0]

    def far(self, k):
        return self.at.near(self.at.line - 1 - k)

    def piece(self, mask, t):
        rows = pl.ds(pl.multiple_of(flipped(self.at.g, mask) * self.rows, 8), self.rows)
        return self.full.at[t, rows, :]

    def local(self, mask, t):
        m = mask // 2
        return pltpu.make_async_copy(self.piece(mask, t), self.sums.at[m, t], self.ls.at[m, t])

    def core(self, mask, t):
        at, m = self.at, mask // 2
        return remote(
            self.piece(mask ^ 1, t), self.cbuf.at[m, t], self.cs.at[m, t], self.cr.at[m, t],
            (flipped(at.g, 1), at.z),
        )

    def across(self, mask, k):
        at, m = self.at, mask // 2
        peer, t = mask, self.far(k)
        if at.square and mask == 6:
            peer = 4 if k % 2 == 0 else 2
        return remote(
            self.sums.at[m, t], self.dbuf.at[m - 1, t], self.ds.at[m, t], self.dr.at[m, t],
            (flipped(at.g, peer), at.z),
        )

    def along(self, t):
        at = self.at
        return remote(
            self.sums.at[0, t], self.zbuf.at[at.z], self.zs.at[t], self.zr.at[at.z], (at.g, t)
        )

    def add(self, m, t, other):
        self.sums[m, t] = self.sums[m, t] + other

    def begin(self, k):
        t = self.far(k)
        for mask in self.order:
            self.core(mask, t).start()
            self.local(mask, t).start()

    def pair(self, k):
        at = self.at
        t = self.far(k)
        for mask in self.order:
            m = mask // 2
            self.local(mask, t).wait()
            self.core(mask, t).wait_recv()
            self.add(m, t, self.cbuf[m, t])
            waits = at.square and mask == (2 if k % 2 == 0 else 4)
            if mask and not waits:
                self.across(mask, k).start()
        if k + 2 < at.line and not self.apart:
            self.begin(k + 2)

    def joined(self, k):
        at = self.at
        if at.square:
            mask = 2 if k % 2 == 0 else 4
            t = self.far(k)
            self.across(6, k).wait_recv()
            self.add(mask // 2, t, self.dbuf[2, t])
            self.across(mask, k).start()

    def own(self, k):
        at = self.at
        t = self.far(k)
        for mask in at.direct:
            self.across(mask, k).wait_recv()
            self.add(0, t, self.dbuf[mask // 2 - 1, t])
        if k < at.line - 1:
            self.along(t).start()

    def finish(self, out_ref):
        at = self.at
        total = self.sums[0, at.z].astype(f32)
        for k in range(1, at.line):
            t = at.near(k)
            buf, sem = self.zbuf.at[t], self.zr.at[t]
            remote(buf, buf, sem, sem, (flipped(at.g, 1), at.z)).wait_recv()
            total += self.zbuf[t].astype(f32)
        out_ref[...] = total
        for k in range(at.line):
            t = self.far(k)
            for mask in at.masks:
                self.core(mask, t).wait_send()
                if mask:
                    self.across(mask, k).wait_send()
            if k < at.line - 1:
                self.along(t).wait_send()

    def early(self):
        self.apart = True
        line = self.at.line
        out = []
        for i in range(line):
            todo = [functools.partial(self.begin, i)]
            for work, late in ((self.pair, 1), (self.joined, 3)):
                if i >= late:
                    todo.append(functools.partial(work, i - late))
            out.append(todo)
        return out

    def late(self):
        line = self.at.line
        out = [functools.partial(self.pair, line - 1)]
        done = max(line - 3, 0)
        for i in range(line):
            if done + i < line:
                out.append(functools.partial(self.joined, done + i))
            out.append(functools.partial(self.own, i))
        return out

    def start(self):
        self.begin(0)
        self.begin(1)

    def steps(self):
        line = self.at.line
        out = [self.start]
        for i in range(line + 4):
            for work, late in ((self.pair, 0), (self.joined, 2), (self.own, 4)):
                if 0 <= i - late < line:
                    out.append(functools.partial(work, i - late))
        return out


FWD = (3, 4, 7, 8, 8, 11, 12, 12, 15, 16)
COT = 4
ARRIVE = (0, 0, 1, 3)
FFC = 2
BACK = 6
BWD = (2, 3, 7, 11, 8, 11, 19, 23, 19, 23, 28, 28)


def run_ticks(ticks, step, part, parts):
    for at, work in ticks:
        if at % parts == part:
            pl.when(step == at // parts)(work)


def arrive_kernel(groups, line, x_ref, shard_ref, small_ref, xo_ref, full_ref, smalls_ref, *sems):
    at = Place(groups, line)
    n = len(Gather.sems(groups, line))
    rows = ToOwner(at, x_ref, xo_ref, sems[2 * n :])
    weights = Gather(at, shard_ref, full_ref, sems[:n])
    small = Gather(at, small_ref, smalls_ref, sems[n : 2 * n])
    at.barrier()
    for i, (one, two) in enumerate(zip(small.steps(), weights.steps())):
        one()
        two()
        for k in range(line):
            if ARRIVE[min(k, 3)] == i:
                rows.start_one(k)
    rows.finish()


def arrive(groups, line, x, shard, small):
    images, part_rows, width = x.shape
    return pl.pallas_call(
        functools.partial(arrive_kernel, groups, line),
        in_specs=[ANY] * 3,
        out_specs=[ANY] * 3,
        out_shape=[
            jax.ShapeDtypeStruct((line, part_rows, width), x.dtype),
            jax.ShapeDtypeStruct((line, groups * shard.shape[0], shard.shape[1]), shard.dtype),
            jax.ShapeDtypeStruct((line, groups * small.shape[0], small.shape[1]), small.dtype),
        ],
        scratch_shapes=Gather.sems(groups, line) * 2 + ToOwner.sems(groups, line),
        compiler_params=pltpu.CompilerParams(collective_id=1, has_side_effects=True),
        name="arrive",
    )(x, shard, small)


def leave_kernel(
    groups, line, gq_ref, gk_ref, gv_ref, w_ref, n1t_hbm, x_hbm, gh_hbm, v_ref, smalls_ref,
    yo_ref, shard_ref, small_ref, gn, y, full, smalls, sums, n1t_ref, x_ref, gh_ref, loads, *scratch
):
    at = Place(groups, line)
    n = len(ToOwner.sems(groups, line))
    m = (len(scratch) - n) // 2
    rows = FromOwner(at, y, yo_ref, scratch[:n])
    weights = Reduce(at, full, scratch[n : n + m], shard_ref.shape[0])
    small = Reduce(at, smalls, scratch[n + m :], small_ref.shape[0])
    step = pl.program_id(0)
    cols = gq_ref.shape[1]
    grads = (gq_ref, gk_ref, gv_ref)
    pairs = ((x_hbm, x_ref), (gh_hbm, gh_ref), (n1t_hbm, n1t_ref))
    copies = [pltpu.make_async_copy(a, b, loads.at[i]) for i, (a, b) in enumerate(pairs)]

    @pl.when(step == 0)
    def _():
        for copy in copies:
            copy.start()
        at.barrier()
        smalls[...] = smalls_ref[...]
        gn[...] = jnp.zeros_like(gn)

    @pl.when(step < line)
    def _():
        g = jnp.concatenate([ref[...] for ref in grads], axis=1)
        gn[...] += lax.dot_general(g, w_ref[0], NT, preferred_element_type=f32)

    @pl.when(step == line - 1)
    def _():
        part = x_ref.shape[1]
        copies[0].wait()
        copies[1].wait()
        sums[...] = jnp.zeros_like(sums)
        for p in range(line):

            def work(r, first, count, p=p):
                at_rows = slice(p * part + first, p * part + first + count)
                hat, inverse = norm_stats(x_ref[p, r].astype(f32))
                g = gn[at_rows, :]
                y[p, r] = (gh_ref[p, r] + norm_back(g, hat, inverse, v_ref[0:1])).astype(bf16)
                add_rows(sums, 0, g * hat)
                add_rows(sums, 8, g)

            work(slice(0, part), 0, part)
            rows.start_piece(p)
        carry = [jnp.sum(sums[8 * j : 8 * j + 8], axis=0, keepdims=True) for j in range(2)]
        wide = gn.shape[1] // groups
        for j, total in enumerate(carry):
            for g in range(groups):
                row = total[:, g * wide : (g + 1) * wide]
                if wide < LANES:
                    row = jnp.concatenate([row, jnp.zeros((1, LANES - wide), f32)], axis=1)
                at_row = g * small_ref.shape[0] + 2 * j
                for t in range(line):
                    smalls[t, at_row : at_row + 1, :] = row
        small.start()

    @pl.when(step == line)
    def _():
        copies[2].wait()

    @pl.when(step >= line)
    def _():
        t = weights.far(step - line)
        for i, ref in enumerate(grads):
            full[t, :, i * cols : (i + 1) * cols] = lax.dot_general(
                n1t_ref[...], ref[...], NN, preferred_element_type=f32
            ).astype(bf16)

    for i, todo in enumerate(weights.early()):

        @pl.when(step == line + i)
        def _(todo=todo):
            for work in todo:
                work()

    @pl.when(step == 2 * line - 1)
    def _():
        for work in small.steps()[1:]:
            work()
        for work in weights.late():
            work()
        weights.finish(shard_ref)
        small.finish(small_ref)
        rows.finish()


def leave(groups, line, images, gq, gk, gv, weights, n1t, x, ghid, vectors, smalls):
    _, part, width = x.shape
    rows = line * part
    cols = width // line
    r, c = width // groups, 3 * cols
    sr, sc = smalls.shape[1] // groups, smalls.shape[2]

    def column(j):
        far = Place(groups, line).near(jnp.clip(2 * line - 1 - j, 0, line - 1))
        return 0, jnp.where(j < line, j, far)

    grad = pl.BlockSpec((rows, cols), column)
    return pl.pallas_call(
        functools.partial(leave_kernel, groups, line),
        grid=(2 * line,),
        in_specs=[
            grad,
            grad,
            grad,
            pl.BlockSpec((1, width, c), lambda j: (jnp.minimum(j, line - 1), 0, 0)),
            ANY,
            ANY,
            ANY,
            whole(*vectors.shape),
            whole(*smalls.shape),
        ],
        out_specs=[ANY, whole(r, c), whole(sr, sc)],
        out_shape=[
            jax.ShapeDtypeStruct((images, part, width), bf16),
            jax.ShapeDtypeStruct((r, c), f32),
            jax.ShapeDtypeStruct((sr, sc), f32),
        ],
        scratch_shapes=[
            pltpu.VMEM((rows, width), f32),
            pltpu.VMEM((line, part, width), bf16),
            pltpu.VMEM((line, width, c), bf16),
            pltpu.VMEM(smalls.shape, f32),
            pltpu.VMEM((16, width), f32),
            pltpu.VMEM((width, rows), bf16),
            pltpu.VMEM((line, part, width), bf16),
            pltpu.VMEM((line, part, width), f32),
            DMA((3,)),
        ]
        + ToOwner.sems(groups, line)
        + Reduce.scratch(groups, line, r, c, bf16)
        + Reduce.scratch(groups, line, sr, sc, f32),
        compiler_params=pltpu.CompilerParams(
            collective_id=2, has_side_effects=True, vmem_limit_bytes=62 * 2**20
        ),
        name="leave",
    )(gq, gk, gv, weights, n1t, x, ghid, vectors, smalls)


def norm_stats(values):
    center = values - jnp.mean(values, axis=-1, keepdims=True)
    inverse = lax.rsqrt(jnp.mean(center * center, axis=-1, keepdims=True) + 1e-06)
    return center * inverse, inverse


def norm_back(grad_norm, normed, inverse, gain):
    scaled = grad_norm * gain
    return inverse * (
        scaled
        - jnp.mean(scaled, axis=-1, keepdims=True)
        - normed * jnp.mean(scaled * normed, axis=-1, keepdims=True)
    )


def project_kernel(flag_ref, x_ref, v_ref, w_ref, b_ref, out_ref, xc_ref, n1t_ref, n1):
    @pl.when(pl.program_id(0) == 0)
    def _():
        rows = x_ref.shape[0]
        size = rows // 2 if rows % 32 == 0 else rows
        for first in range(0, rows, size):
            r = slice(first, first + size)
            x = jnp.where(flag_ref[1] > 0, x_ref[r].astype(f32), 0.0)
            xc_ref[r] = x.astype(bf16)
            hat, _ = norm_stats(x)
            n1[r] = (hat * v_ref[0:1] + v_ref[2:3]).astype(bf16)

    cols = out_ref.shape[2]
    part = pl.ds(pl.multiple_of(pl.program_id(0) * cols, LANES), cols)
    n1t_ref[part, :] = n1[:, part].T
    for i in range(3):
        w = w_ref[0, :, i * cols : (i + 1) * cols]
        out = lax.dot_general(n1[...], w, NN, preferred_element_type=f32) + b_ref[i]
        if i == 0:
            out = out * (HD ** (-0.5) * LOG2E)
        out_ref[i] = out.astype(bf16)


def whole(*shape):
    return pl.BlockSpec(shape, lambda *_: (0,) * len(shape), pipeline_mode=pl.Buffered(1))


def add_rows(ref, first, x):
    ref[first : first + 1] += jnp.sum(x, axis=0, keepdims=True)


SMEM = pl.BlockSpec(memory_space=pltpu.SMEM)


def project(flags, x, vectors, weights, bias):
    rows, width = x.shape
    line = weights.shape[0]
    cols = width // line
    return pl.pallas_call(
        project_kernel,
        grid=(line,),
        in_specs=[
            SMEM,
            whole(rows, width),
            whole(*vectors.shape),
            pl.BlockSpec((1, width, 3 * cols), lambda t: (t, 0, 0)),
            pl.BlockSpec((3, 1, cols), lambda t: (0, 0, t)),
        ],
        out_specs=[
            pl.BlockSpec((3, rows, cols), lambda t: (0, 0, t)),
            whole(rows, width),
            whole(width, rows),
        ],
        out_shape=[
            jax.ShapeDtypeStruct((3, rows, width), bf16),
            jax.ShapeDtypeStruct((rows, width), bf16),
            jax.ShapeDtypeStruct((width, rows), bf16),
        ],
        scratch_shapes=[pltpu.VMEM((rows, width), bf16)],
        compiler_params=pltpu.CompilerParams(vmem_limit_bytes=62 * 2**20),
        cost_estimate=pl.CostEstimate(
            flops=6 * rows * width * width, bytes_accessed=16 * rows * width, transcendentals=0
        ),
        name="project",
    )(flags, x, vectors, weights, bias)


def valid_rows(flag_ref, shape):
    row = pl.program_id(0) * shape[0] + lax.broadcasted_iota(jnp.int32, shape, 0)
    return row < flag_ref[0]


def middle_kernel(flag_ref, ctx_ref, x_ref, cot_ref, v_ref, w_ref, hid_ref, n2_ref, gm_ref):
    line, _, cols = w_ref.shape
    attn = v_ref[6:7]
    for t in range(line):
        part = ctx_ref[0, :, t * cols : (t + 1) * cols]
        attn = attn + lax.dot_general(part, w_ref[t], NT, preferred_element_type=f32)
    hidden = x_ref[0].astype(f32) + v_ref[4:5] * attn
    hid_ref[0] = hidden
    hat, _ = norm_stats(hidden)
    n2_ref[0] = (hat * v_ref[1:2] + v_ref[3:4]).astype(bf16)
    gout = jnp.where(valid_rows(flag_ref, hidden.shape), cot_ref[0].astype(f32), 0.0)
    gm_ref[0] = (gout * v_ref[5:6]).astype(bf16)


def middle(flags, context, x, cot, vectors, weights):
    line, part, width = x.shape
    cols = width // line
    piece = pl.BlockSpec((1, part, width), lambda p: (p, 0, 0))
    return pl.pallas_call(
        middle_kernel,
        grid=(line,),
        in_specs=[
            SMEM,
            piece,
            piece,
            piece,
            whole(*vectors.shape),
            pl.BlockSpec(
                (line, width, cols), lambda p: (0, 0, 3), pipeline_mode=pl.Buffered(1)
            ),
        ],
        out_specs=[piece] * 3,
        out_shape=[
            jax.ShapeDtypeStruct(x.shape, f32),
            jax.ShapeDtypeStruct(x.shape, bf16),
            jax.ShapeDtypeStruct(x.shape, bf16),
        ],
        compiler_params=pltpu.CompilerParams(vmem_limit_bytes=62 * 2**20),
        name="middle",
    )(flags, context, x, cot, vectors, weights)


def turn_kernel(
    flag_ref, mlp_ref, gn_ref, hid_ref, x_ref, cot_ref, ctx_ref, v_ref, w_ref,
    out_ref, gh_ref, gc_ref, gw_ref, sum_ref, acc, gattn, sums
):
    step = pl.program_id(0)
    line, _, cols = w_ref.shape
    part = hid_ref.shape[1]

    @pl.when(step == 0)
    def _():
        sums[...] = jnp.zeros_like(sums)
        acc[...] = jnp.zeros_like(acc)

    def work(r, first, count):
        hidden = hid_ref[0, r]
        mlp = mlp_ref[0, r] + v_ref[7:8]
        gn = gn_ref[0, r]
        row = step * part + first + lax.broadcasted_iota(jnp.int32, hidden.shape, 0)
        valid = row < flag_ref[0]
        out_ref[0, r] = jnp.where(valid, hidden + v_ref[5:6] * mlp, 0.0).astype(bf16)
        gout = jnp.where(valid, cot_ref[0, r].astype(f32), 0.0)
        hat, inverse = norm_stats(hidden)
        ghid = gout + norm_back(gn, hat, inverse, v_ref[1:2])
        gh_ref[0, r] = ghid
        attn = (hidden - x_ref[0, r].astype(f32)) * (1.0 / v_ref[4:5])
        grad = ghid * v_ref[4:5]
        gattn[r] = grad.astype(bf16)
        terms = (gn * hat, gn, ghid * attn, gout * mlp, grad, gout * v_ref[5:6])
        for j, term in enumerate(terms):
            add_rows(sums, 8 * j, term)

    work(slice(0, part), 0, part)

    @pl.when(step == line - 1)
    def _():
        rows = [jnp.sum(sums[8 * j : 8 * j + 8], axis=0, keepdims=True) for j in range(6)]
        sum_ref[...] = jnp.concatenate(rows + [jnp.zeros((2, sums.shape[1]), f32)], axis=0)

    gattn_t = gattn[...].T
    for t in range(line):
        ctx = ctx_ref[0, :, t * cols : (t + 1) * cols]
        gc_ref[0, :, t * cols : (t + 1) * cols] = lax.dot_general(
            gattn[...], w_ref[t], NN, preferred_element_type=f32
        ).astype(bf16)
        acc[t] += lax.dot_general(gattn_t, ctx, NN, preferred_element_type=f32)

    @pl.when(step == line - 1)
    def _():
        gw_ref[...] = acc[...].astype(bf16)


def turn(flags, mlp, gn, hidden, x, cot, context, vectors, weights):
    line, part, width = x.shape
    cols = width // line
    piece = pl.BlockSpec((1, part, width), lambda p: (p, 0, 0))
    return pl.pallas_call(
        turn_kernel,
        grid=(line,),
        in_specs=[SMEM]
        + [piece] * 6
        + [
            whole(*vectors.shape),
            pl.BlockSpec(
                (line, width, cols), lambda p: (0, 0, 3), pipeline_mode=pl.Buffered(1)
            ),
        ],
        out_specs=[piece] * 3 + [whole(line, width, cols), whole(8, width)],
        out_shape=[
            jax.ShapeDtypeStruct(x.shape, bf16),
            jax.ShapeDtypeStruct(x.shape, f32),
            jax.ShapeDtypeStruct(x.shape, bf16),
            jax.ShapeDtypeStruct((line, width, cols), bf16),
            jax.ShapeDtypeStruct((8, width), f32),
        ],
        scratch_shapes=[
            pltpu.VMEM((line, width, cols), f32),
            pltpu.VMEM((part, width), bf16),
            pltpu.VMEM((48, width), f32),
        ],
        compiler_params=pltpu.CompilerParams(vmem_limit_bytes=62 * 2**20),
        name="turn",
    )(flags, mlp, gn, hidden, x, cot, context, vectors, weights)


def attend_forward_kernel(
    groups, line, rows, padded, len_ref, q_ref, k_ref, v_ref, shard_ref, cot_ref,
    ctx_ref, qa_ref, full_ref, coto_ref, ka, va, *sems
):
    at = Place(groups, line)
    n = len(Gather.sems(groups, line))
    weights = Gather(at, shard_ref, full_ref, sems[:n])
    cot = ToOwner(at, cot_ref, coto_ref, sems[n:])
    steps = weights.steps()

    def begin():
        at.barrier()
        steps[0]()

    ticks = [(0, begin), (COT, cot.start)]
    for i, work in enumerate(steps[1:]):
        ticks.append((FWD[min(i, len(FWD) - 1)], work))
    step = pl.program_id(0)
    length = len_ref[0]
    lane = lax.broadcasted_iota(jnp.int32, (padded, LANES), 1)
    row = lax.broadcasted_iota(jnp.int32, (padded, LANES), 0)
    lb = lane[:rows]
    if padded > rows:
        va[rows:] = jnp.zeros((padded - rows, LANES), bf16)
    for half in range(2):
        run_ticks(ticks, step, half, 2)
        own = (lb < HD) if half == 0 else (lb >= HD)
        spare = HD if half == 0 else 0
        ka[:rows] = keys_with_bias(k_ref[...].astype(f32), lb, row[:rows], length, own, spare)
        if padded > rows:
            ka[rows:] = jnp.where(lane[rows:] == spare + 3, NEG, 0.0).astype(bf16)
        va[:rows] = jnp.where(
            own, v_ref[...].astype(f32), jnp.where(lb == spare, 1.0, 0.0)
        ).astype(bf16)
        qa = jnp.where(own, q_ref[...].astype(f32), jnp.where(lb == spare + 3, 1.0, 0.0))
        s = lax.dot_general(qa.astype(bf16), ka[...], NT, preferred_element_type=f32)
        m = jnp.max(s, axis=1, keepdims=True)
        p = jnp.exp2(s - m).astype(bf16)
        o = lax.dot_general(p, va[...], NN, preferred_element_type=f32)
        total = o[:, spare : spare + 1]
        o = o / total
        hi, mid, lo = parts(-(m + jnp.log2(total)))
        if half == 0:
            ctx_ref[...] = o.astype(bf16)
        else:
            ctx_ref[...] = jnp.where(own, o, ctx_ref[...].astype(f32)).astype(bf16)
        stats = jnp.where(lb == spare + 2, lo, qa)
        stats = jnp.where(lb == spare + 1, mid, stats)
        qa_ref[half] = jnp.where(lb == spare, hi, stats).astype(bf16)

    @pl.when(step == pl.num_programs(0) - 1)
    def _():
        for at_tick, work in ticks:
            if at_tick > 15:
                work()
        cot.finish()


def attend_forward(groups, line, length, qkv, shard, cot):
    _, rows, width = qkv.shape
    padded = round_up(rows, LANES)
    spec = pl.BlockSpec((rows, LANES), lambda j: (0, j))

    def third(n):
        return pl.BlockSpec((None, rows, LANES), lambda j: (n, 0, j))

    return pl.pallas_call(
        functools.partial(attend_forward_kernel, groups, line, rows, padded),
        grid=(width // LANES,),
        in_specs=[pl.BlockSpec(memory_space=pltpu.SMEM), third(0), third(1), third(2), ANY, ANY],
        out_specs=[spec, pl.BlockSpec((2, rows, LANES), lambda j: (j, 0, 0)), ANY, ANY],
        out_shape=[
            jax.ShapeDtypeStruct((rows, width), bf16),
            jax.ShapeDtypeStruct((width // HD, rows, LANES), bf16),
            jax.ShapeDtypeStruct((line, groups * shard.shape[0], shard.shape[1]), shard.dtype),
            jax.ShapeDtypeStruct((line,) + cot.shape[1:], cot.dtype),
        ],
        scratch_shapes=[pltpu.VMEM((padded, LANES), bf16), pltpu.VMEM((padded, LANES), bf16)]
        + Gather.sems(groups, line)
        + ToOwner.sems(groups, line),
        compiler_params=pltpu.CompilerParams(
            collective_id=3, has_side_effects=True, vmem_limit_bytes=62 * 2**20
        ),
        cost_estimate=pl.CostEstimate(
            flops=16 * rows * rows * width,
            bytes_accessed=12 * rows * width,
            transcendentals=rows * rows * width // HD,
        ),
        name="attend_forward",
    )(length, qkv, qkv, qkv, shard, cot)


def attend_backward_kernel(
    groups, line, rows, padded, blocks, len_ref, qa_ref, k_ref, v_ref, gc_ref, ctx_ref, y_ref, full_ref,
    out_ref, gq_ref, gk_ref, gv_ref, gb_ref, yo_ref, shard_ref, oshard_ref, ka, va, qs, ga, acc, *scratch
):
    at = Place(groups, line)
    n = len(ToOwner.sems(groups, line))
    back = FromOwner(at, y_ref, yo_ref, scratch[:n])
    m = (len(scratch) - n) // 2
    weights = Reduce(at, full_ref, scratch[n : n + m], shard_ref.shape[0])
    out_weights = Reduce(at, out_ref, scratch[n + m :], oshard_ref.shape[0])
    pairs = list(zip(weights.steps(), out_weights.steps()))

    def both(i):
        def run():
            for work in pairs[i]:
                work()

        return run

    steps = [both(i) for i in range(len(pairs))]

    def begin():
        at.barrier()
        steps[0]()

    ticks = [(0, begin), (BACK * blocks // 2, back.start)]
    for i, work in enumerate(steps[1:]):
        ticks.append((BWD[min(i, len(BWD) - 1)] * blocks // 2, work))
    step = pl.program_id(0)
    length = len_ref[0]
    lane = lax.broadcasted_iota(jnp.int32, (padded, LANES), 1)
    row = lax.broadcasted_iota(jnp.int32, (padded, LANES), 0)
    size = rows // blocks
    ls = lane[:rows]
    for half in range(2):
        own = (ls < HD) if half == 0 else (ls >= HD)
        spare = HD if half == 0 else 0
        ownb = own[:size]
        gc = gc_ref[...].astype(f32)
        corr = jnp.sum(
            jnp.where(own, gc * ctx_ref[...].astype(f32), 0.0), axis=1, keepdims=True
        )
        hi, mid, lo = parts(-corr)
        extra = jnp.where(ls == spare + 1, mid, jnp.where(ls == spare + 2, lo, 0.0))
        ga[:rows] = jnp.where(own, gc, jnp.where(ls == spare, hi, extra)).astype(bf16)
        qs[:rows] = qa_ref[half]
        if padded > rows:
            ga[rows:] = jnp.zeros((padded - rows, LANES), bf16)
            qs[rows:] = jnp.where(lane[rows:] == spare, NEG, 0.0).astype(bf16)
        ka[...] = keys_with_bias(k_ref[...].astype(f32), ls, row[:rows], length, own, spare)
        ones = jnp.where((ls >= spare) & (ls < spare + 3), 1.0, 0.0)
        va[...] = jnp.where(own, v_ref[...].astype(f32), ones).astype(bf16)
        bv = jnp.zeros((1, LANES), f32)
        for b in range(blocks):
            run_ticks(ticks, step, half * blocks + b, 2 * blocks)
            r = slice(b * size, (b + 1) * size)
            kb = ka[r]
            p = jnp.exp2(lax.dot_general(kb, qs[...], NT, preferred_element_type=f32))
            gp = lax.dot_general(va[r], ga[...], NT, preferred_element_type=f32)
            ds = (p * gp).astype(bf16)
            gv = lax.dot_general(p.astype(bf16), ga[...], NN, preferred_element_type=f32)
            gk = lax.dot_general(ds, qs[...], NN, preferred_element_type=f32) * (1.0 / LOG2E)
            gqt = lax.dot_general(kb.T, ds, NN, preferred_element_type=f32)
            acc[...] = gqt if b == 0 else acc[...] + gqt
            bv += jnp.sum(gv, axis=0, keepdims=True)
            if half == 0:
                gv_ref[r] = gv.astype(bf16)
                gk_ref[r] = gk.astype(bf16)
            else:
                gv_ref[r] = jnp.where(ownb, gv, gv_ref[r].astype(f32)).astype(bf16)
                gk_ref[r] = jnp.where(ownb, gk, gk_ref[r].astype(f32)).astype(bf16)
        gq = acc[...].T[:rows] * HD ** (-0.5)
        sums = jnp.concatenate(
            [jnp.sum(gq, axis=0, keepdims=True), bv, jnp.zeros((6, LANES), f32)], axis=0
        )
        if half == 0:
            gb_ref[0] = sums
        else:
            gb_ref[0] = jnp.where(own[:8], sums, gb_ref[0])
        if half == 0:
            gq_ref[...] = gq.astype(bf16)
        else:
            gq_ref[...] = jnp.where(own, gq, gq_ref[...].astype(f32)).astype(bf16)

    @pl.when(step == pl.num_programs(0) - 1)
    def _():
        for at_tick, work in ticks:
            if at_tick >= 2 * blocks * 8:
                work()
        weights.finish(shard_ref)
        out_weights.finish(oshard_ref)
        back.finish()


def attend_backward(groups, line, images, length, qa, qkv, gc, ctx, y, full, out_full):
    _, rows, width = qkv.shape
    padded = round_up(rows, LANES)
    blocks = 2 if rows % 32 == 0 else 1
    spec = pl.BlockSpec((rows, LANES), lambda j: (0, j))
    r, c, oc = full.shape[1] // groups, full.shape[2], out_full.shape[2]

    def third(n):
        return pl.BlockSpec((None, rows, LANES), lambda j: (n, 0, j))

    return pl.pallas_call(
        functools.partial(attend_backward_kernel, groups, line, rows, padded, blocks),
        grid=(width // LANES,),
        in_specs=[
            pl.BlockSpec(memory_space=pltpu.SMEM),
            pl.BlockSpec((2, rows, LANES), lambda j: (j, 0, 0)),
            third(1),
            third(2),
            spec,
            spec,
            ANY,
            ANY,
            ANY,
        ],
        out_specs=[spec] * 3
        + [pl.BlockSpec((1, 8, LANES), lambda j: (j, 0, 0)), ANY, whole(r, c), whole(r, oc)],
        out_shape=[jax.ShapeDtypeStruct((rows, width), bf16)] * 3
        + [
            jax.ShapeDtypeStruct((width // LANES, 8, LANES), f32),
            jax.ShapeDtypeStruct((images,) + y.shape[1:], y.dtype),
            jax.ShapeDtypeStruct((r, c), f32),
            jax.ShapeDtypeStruct((r, oc), f32),
        ],
        scratch_shapes=[
            pltpu.VMEM((rows, LANES), bf16),
            pltpu.VMEM((rows, LANES), bf16),
            pltpu.VMEM((padded, LANES), bf16),
            pltpu.VMEM((padded, LANES), bf16),
            pltpu.VMEM((LANES, padded), f32),
        ]
        + ToOwner.sems(groups, line)
        + Reduce.scratch(groups, line, r, c, full.dtype)
        + Reduce.scratch(groups, line, r, oc, full.dtype),
        compiler_params=pltpu.CompilerParams(
            collective_id=4, has_side_effects=True, vmem_limit_bytes=62 * 2**20
        ),
        cost_estimate=pl.CostEstimate(
            flops=40 * rows * rows * width,
            bytes_accessed=16 * rows * width,
            transcendentals=rows * rows * width // HD,
        ),
        name="attend_backward",
    )(length, qa, qkv, qkv, gc, ctx, y, full, out_full)


def feed_forward_kernel(
    tile, chunks, n2_ref, gm_ref, w_ref, b1_ref, mlp_ref, gn_ref, gw_ref, gb_ref, n2t, gmt, act_s, gpre_s
):
    @pl.when(pl.program_id(0) == 0)
    def _():
        n2t[...] = n2_ref[...].T
        gmt[...] = gm_ref[...].T
        mlp_ref[...] = jnp.zeros_like(mlp_ref)
        gn_ref[...] = jnp.zeros_like(gn_ref)

    w1 = w_ref[0, :, :tile]
    w2t = w_ref[0, :, tile:]
    size = n2_ref.shape[0] // chunks
    for c in range(chunks):
        r = slice(c * size, (c + 1) * size)
        pre = lax.dot_general(n2_ref[r], w1, NN, preferred_element_type=f32) + b1_ref[...]
        gact = lax.dot_general(gm_ref[r], w2t, NN, preferred_element_type=f32)
        cdf = 0.5 * (1.0 + lax.erf(pre * (1 / math.sqrt(2))))
        act_s[r] = (pre * cdf).astype(bf16)
        pdf = jnp.exp2(pre * pre * (-0.5 * LOG2E)) * (1 / math.sqrt(2 * math.pi))
        gpre = gact * (cdf + pre * pdf)
        total = jnp.sum(gpre, axis=0, keepdims=True)
        gb_ref[...] = total if c == 0 else gb_ref[...] + total
        gpre_s[r] = gpre.astype(bf16)
        mlp_ref[r] += lax.dot_general(act_s[r], w2t, NT, preferred_element_type=f32)
        gn_ref[r] += lax.dot_general(gpre_s[r], w1, NT, preferred_element_type=f32)
    gw_ref[0, :, :tile] = lax.dot_general(
        n2t[...], gpre_s[...], NN, preferred_element_type=f32
    ).astype(bf16)
    gw_ref[0, :, tile:] = lax.dot_general(
        gmt[...], act_s[...], NN, preferred_element_type=f32
    ).astype(bf16)


def feed_forward(n2, gm, weights, b1, tile):
    rows, width = n2.shape
    units = b1.shape[1]
    per = weights.shape[2] // (2 * tile)

    both = pl.BlockSpec((1, width, 2 * tile), lambda j: (j // per, 0, j % per))
    return pl.pallas_call(
        functools.partial(feed_forward_kernel, tile, FFC if rows % (16 * FFC) == 0 else 1),
        grid=(units // tile,),
        in_specs=[
            whole(rows, width),
            whole(rows, width),
            both,
            pl.BlockSpec((1, tile), lambda j: (0, j)),
        ],
        out_specs=[
            whole(rows, width),
            whole(rows, width),
            both,
            pl.BlockSpec((1, tile), lambda j: (0, j)),
        ],
        out_shape=[
            jax.ShapeDtypeStruct((rows, width), f32),
            jax.ShapeDtypeStruct((rows, width), f32),
            jax.ShapeDtypeStruct(weights.shape, bf16),
            jax.ShapeDtypeStruct((1, units), f32),
        ],
        scratch_shapes=[pltpu.VMEM((width, rows), bf16)] * 2 + [pltpu.VMEM((rows, tile), bf16)] * 2,
        compiler_params=pltpu.CompilerParams(vmem_limit_bytes=62 * 2**20),
        cost_estimate=pl.CostEstimate(
            flops=16 * rows * width * units,
            bytes_accessed=8 * width * units,
            transcendentals=2 * rows * units,
        ),
        name="feed_forward",
    )(n2, gm, weights, b1)


def body(
    block_input,
    cotangent,
    lengths,
    w_qkv,
    b_qv,
    w_out,
    w_fc1,
    b_fc1,
    w_fc2,
    ln_gain,
    ln_shift,
    layer_scale,
    out_bias,
):
    images, part_rows, width = block_input.shape
    groups = lax.axis_size("dp")
    line = lax.axis_size("tensor")
    rows = part_rows * line
    group = lax.axis_index("dp")
    place = lax.axis_index("tensor")
    mine = place + (group % 2) * (line - 1 - 2 * place)
    active = mine < images

    tile = min(512, w_fc1.shape[1])
    qkv_out = jnp.concatenate([w_qkv[0], w_qkv[1], w_qkv[2], w_out.T], axis=1)
    w_fc2_t = w_fc2.T
    fc_both = jnp.concatenate(
        [
            w[:, at : at + tile]
            for at in range(0, w_fc1.shape[1], tile)
            for w in (w_fc1, w_fc2_t)
        ],
        axis=1,
    )

    def lanes(x):
        return jnp.pad(x, ((0, 0), (0, LANES - x.shape[1])))

    own_width = ln_gain.shape[1]
    _, bq_rows, bq_cols = b_qv.shape
    f_rows, f_cols = b_fc1.shape
    small = jnp.concatenate([ln_gain, ln_shift, layer_scale, out_bias], axis=0)
    small = [small, b_qv.reshape(-1, bq_cols).astype(f32), b_fc1.astype(f32)]
    small = jnp.concatenate([lanes(x) for x in small], axis=0)
    small_rows = round_up(small.shape[0], 8)
    small = jnp.pad(small, ((0, small_rows - small.shape[0]), (0, 0)))
    b_at = 8 + 2 * bq_rows

    x_all, weights, small = arrive(groups, line, block_input, qkv_out, small)
    small = small.reshape(line, groups, small_rows, LANES)
    vectors = jnp.transpose(small[:, :, :8, :own_width], (2, 1, 0, 3)).reshape(8, width)
    qv_bias = jnp.transpose(
        small[:, :, 8:b_at, :bq_cols].reshape(line, groups, 2, bq_rows, bq_cols), (2, 0, 4, 1, 3)
    ).reshape(2, 1, width)
    fc1_bias = jnp.transpose(
        small[:, :, b_at : b_at + f_rows, :f_cols], (0, 3, 1, 2)
    ).reshape(1, -1)

    length = jnp.where(active, lengths[jnp.minimum(mine, images - 1)], 0).astype(jnp.int32)
    flags = jnp.stack([length, active.astype(jnp.int32)])
    pieces = (line, part_rows, width)

    zero = jnp.zeros((1, 1, width), f32)
    qkv, x_all, normed1_t = project(
        flags,
        x_all.reshape(rows, width),
        vectors,
        weights,
        jnp.concatenate([qv_bias[:1], zero, qv_bias[1:]]),
    )
    x_all = x_all.reshape(pieces)
    context, query_stats, fc_weights, cot = attend_forward(
        groups, line, flags, qkv, fc_both, cotangent
    )
    context3 = context.reshape(pieces)
    hidden, normed2, grad_mlp = middle(flags, context3, x_all, cot, vectors, weights)
    mlp, grad_normed2, grad_fc, grad_bfc1 = feed_forward(
        normed2.reshape(rows, width), grad_mlp.reshape(rows, width), fc_weights, fc1_bias, tile
    )
    block_out, grad_hidden, grad_context, grad_wout, sums = turn(
        flags,
        mlp.reshape(pieces),
        grad_normed2.reshape(pieces),
        hidden,
        x_all,
        cot,
        context3,
        vectors,
        weights,
    )
    grad_query, grad_key, grad_value, grad_bqv, block_out, shard_fc, shard_wout = attend_backward(
        groups,
        line,
        images,
        flags,
        query_stats,
        qkv,
        grad_context.reshape(rows, width),
        context,
        block_out,
        grad_fc,
        grad_wout,
    )

    wide = width // groups
    none = jnp.zeros((1, width), f32)
    by_vector = jnp.concatenate(
        [none, sums[0:1], none, sums[1:2], sums[2:6]], axis=0
    ).reshape(8, groups, wide)
    by_vector = jnp.pad(jnp.transpose(by_vector, (1, 0, 2)), ((0, 0), (0, 0), (0, LANES - wide)))
    by_vector = jnp.broadcast_to(by_vector[None], (line, groups, 8, LANES))
    by_head = jnp.transpose(grad_bqv[:, :2], (1, 0, 2)).reshape(2, line, bq_cols, groups, bq_rows)
    by_head = jnp.transpose(by_head, (1, 3, 0, 4, 2)).reshape(line, groups, 2 * bq_rows, bq_cols)
    by_unit = jnp.transpose(grad_bfc1.reshape(line, f_cols, groups, f_rows), (0, 2, 3, 1))

    def wider(x):
        return jnp.pad(x, ((0, 0), (0, 0), (0, 0), (0, LANES - x.shape[3])))

    smalls = jnp.concatenate([by_vector, wider(by_head), wider(by_unit)], axis=2)
    smalls = jnp.pad(smalls, ((0, 0), (0, 0), (0, small_rows - smalls.shape[2]), (0, 0)))
    grad_input, shard_weights, shard_small = leave(
        groups,
        line,
        images,
        grad_query,
        grad_key,
        grad_value,
        weights,
        normed1_t,
        x_all,
        grad_hidden,
        vectors,
        smalls.reshape(line, groups * small_rows, LANES),
    )
    grad_input = grad_input.astype(f32)
    cols = width // line
    shard_wqkv = jnp.stack([shard_weights[:, n * cols : (n + 1) * cols] for n in range(3)])
    shard_wout = shard_wout.T
    shard_fc1, shard_fc2 = (
        jnp.concatenate(
            [
                shard_fc[:, at : at + tile]
                for at in range(first, shard_fc.shape[1], 2 * tile)
            ],
            axis=1,
        )
        for first in (0, tile)
    )
    shard_fc2 = shard_fc2.T
    own = lax.dynamic_slice_in_dim(shard_small[:8], place * own_width, own_width, 1)
    shard_gain, shard_shift, shard_scale, shard_bias = (own[2 * n : 2 * n + 2] for n in range(4))
    shard_bqv = shard_small[8:b_at, :bq_cols].reshape(b_qv.shape)
    shard_bfc1 = shard_small[b_at : b_at + f_rows, :f_cols]
    return (
        block_out,
        grad_input,
        shard_wqkv,
        shard_bqv,
        shard_wout,
        shard_fc1,
        shard_bfc1,
        shard_fc2,
        shard_gain,
        shard_shift,
        shard_scale,
        shard_bias,
    )


def solution(mesh):
    rows = P("dp", "tensor", None)
    vector = P(None, ("dp", "tensor"))
    weights = (
        P(None, "dp", "tensor"),
        P(None, "dp", "tensor"),
        P("tensor", "dp"),
        P("dp", "tensor"),
        P("dp", "tensor"),
        P("tensor", "dp"),
    )
    return jax.shard_map(
        body,
        mesh=mesh,
        in_specs=(rows, rows, P("dp")) + weights + (vector,) * 4,
        out_specs=(rows, rows) + weights + (vector,) * 4,
        check_vma=False,
    )
```
